32 devices in a mesh: seq: 4 (over x, core), expert: 8 (over z, y).
Axes of the slice: x: 2, y: 2, z: 4, core: 2. Of those that a mesh axis runs over, the one named last changes fastest.
Arguments:
- queries: bfloat16 [2, 1024, 2048], P(None, 'seq', 'expert'), may hold values from -6 to 6
- key_rows: bfloat16 [2, 1024, 2048], P(None, 'seq', 'expert'), may hold values from -6 to 6
- value_rows: bfloat16 [2, 1024, 2048], P(None, 'seq', 'expert'), may hold values from -6 to 6
- decay_rate: float32 [16], P('expert'), as said below
- norm_gain: float32 [2048], P('expert'), may hold values from 0.1 to 1.9
- attn_probe: bfloat16 [2, 1024, 2048], P(None, 'seq', 'expert'), may hold values from -6 to 6
- hidden_in: bfloat16 [2, 1024, 6144], P(None, ('seq', 'expert')), may hold values from -6 to 6
- moe_probe: bfloat16 [2, 1024, 6144], P(None, ('seq', 'expert')), may hold values from -6 to 6
- router_weight: bfloat16 [6144, 4], replicated, may hold values from -0.078125 to 0.078125
- routes: int32 [2, 1024, 2], P(None, ('seq', 'expert')), may hold values from 0 to 3, all different within a row; in each aligned block of 32 rows (0 to 31, 32 to 63, ..., all dimensions but the last counted through in order) at most 17 rows name the same one
- gate_weight: bfloat16 [8, 6144, 2304], P('expert', 'seq'), may hold values from -0.078125 to 0.078125
- up_weight: bfloat16 [8, 6144, 2304], P('expert', 'seq'), may hold values from -0.078125 to 0.078125
- down_weight: bfloat16 [8, 6144, 2304], P('expert', 'seq'), may hold values from -0.09375 to 0.09375
- rollout_logprob: float32 [2, 1024], P(None, 'seq'), may hold values from -1 to 0
- trainer_logprob: float32 [2, 1024], P(None, 'seq'), may hold values from -1 to 0
- advantage: float32 [2, 1024], P(None, 'seq'), may hold values from -4 to 4
- clip_low: float32 [1], replicated, may hold values from 0.4 to 0.95
- clip_high: float32 [1], replicated, may hold values from 1.05 to 2.5
Outputs:
- objective: float32 [2, 1024], P(None, 'seq')
- grad_queries: bfloat16 [2, 1024, 2048], P(None, 'seq', 'expert')
- grad_keys: bfloat16 [2, 1024, 2048], P(None, 'seq', 'expert')
- grad_values: bfloat16 [2, 1024, 2048], P(None, 'seq', 'expert')
- grad_hidden: bfloat16 [2, 1024, 6144], P(None, ('seq', 'expert'))
The draws below stay inside these ranges and needn't reach their ends.
Inputs may be any that keep to these rules, and one draw needn't show every extreme that they name: `routes`: in each rollout, the 32 positions that one device holds in the expert block name no expert more than 17 times; the 2 experts of a token differ. `decay_rate`: positive rates.
All inputs are finite; a program needn't handle non-finite values.
Results may differ from the reference program's by a relative error of at most 0.0045.
The reference program's roundings to bfloat16 on the way count: a program that leaves them out, or rounds other values in their place, can miss the bound.
Values may be sent and summed in bfloat16 or wider, within the bound.
No kernel may reach another device: no remote copies, remote signals or barrier semaphores. Data moves between devices by JAX's collectives and lax.ppermute only.
A program may use at most 192 MiB of HBM per device.

```python
import math
import jax
import jax.numpy as jnp
import numpy as np
from jax import lax

D = 6144
HD = 128
TOP = 2
EXP_WIN = 4
FF_WIN = 4608
ROLL = 2
HEADS = 16
LEN = 1024
POS_DEV = 32
MOST = 17
SLICES = 2
FF_DEV = 2304
N_SEQ = 4
N_EXPERT = 8


def draw_decay_rate(key, part):
    pick_key, slow_key, fast_key = jax.random.split(key, 3)
    share = 0.5
    slow = jax.random.uniform(pick_key, (HEADS,), jnp.float32) < share
    slow_rate = jnp.exp(jax.random.uniform(slow_key, (HEADS,), jnp.float32, minval=jnp.log(0.1), maxval=0.0)) * (jnp.log(10.0) / LEN)
    fast_rate = jax.random.uniform(fast_key, (HEADS,), jnp.float32, minval=1.0 / 50.0, maxval=1.0 / 30.0)
    return jnp.where(slow, slow_rate, fast_rate).astype(jnp.float32)


def block_levels(key, dims, shards, least, largest):
    factor_of, own = 1.0, jax.random.fold_in(key, 6)
    for dim, shards_of in shards:
        steps = jnp.exp(jax.random.uniform(jax.random.fold_in(own, dim), (shards_of,), jnp.float32, least / len(shards), largest / len(shards)))
        factor_of = factor_of * jnp.repeat(steps, dims[dim] // shards_of).reshape([-1 if axis == dim else 1 for axis in range(len(dims))])
    return factor_of


def shared_out(own_key, own, number, rows, count, top, bound, skew):
    ranking = jax.random.permutation(own_key, count)
    packed, usual = shares(count, rows * top, bound, skew, True), shares(count, rows * top, bound, skew, False)
    places = jnp.arange(count)

    def named(tallies, offset_by):
        used = int((tallies > 0).sum())
        fixed = max(1, used // 4)
        shifted = fixed + (places - fixed + offset_by * (used - fixed)) % max(1, count - fixed)
        return jnp.zeros((count,), jnp.int32).at[ranking[jnp.where(places < fixed, places, shifted)]].set(jnp.asarray(tallies, jnp.int32))

    tallies = jnp.where(number % 4 == 0, named(packed, number // 4), named(usual, number - number // 4 - 1))
    mixed = jax.random.permutation(jax.random.fold_in(own, 3), count)
    giver, receiver = mixed[0:count // 2 * 2:2], mixed[1:count // 2 * 2:2]
    slack = jnp.minimum(tallies[giver] - 1, bound - tallies[receiver]) // 2
    slack = jnp.where((giver == ranking[0]) | (receiver == ranking[0]) | (tallies[receiver] == 0), 0, jnp.maximum(slack, 0))
    shifted = jax.random.randint(jax.random.fold_in(own, 4), (count // 2,), 0, 1 << 20) % (slack + 1)
    tallies = tallies.at[giver].add(-shifted).at[receiver].add(shifted)
    labels = jnp.searchsorted(jnp.cumsum(tallies), jnp.arange(rows * top), side="right").astype(jnp.int32)
    grid = labels.reshape(top, rows).T
    grid = grid[jax.random.permutation(jax.random.fold_in(own, 1), rows)]
    offset_by = jax.random.randint(jax.random.fold_in(own, 2), (rows, 1), 0, top)
    return jnp.take_along_axis(grid, (jnp.arange(top)[None, :] + offset_by) % top, axis=1)


def shares(count, total, bound, skew, full):
    portions = [(1 << 20) // math.isqrt(rank ** skew) + 1 for rank in range(1, count + 1)]
    largest = bound if full else min(bound, max(-(-total // count), total * portions[0] // sum(portions)))
    least = 1 if total - largest >= count - 1 else 0
    counts, rest = [largest] + [least] * (count - 1), total - largest - least * (count - 1)
    while rest > 0:
        movable = [i for i in range(1, count) if counts[i] < largest] or [i for i in range(1, count) if counts[i] < bound]
        pool, remaining = sum([portions[i] for i in movable]), rest
        for i in movable:
            extra = min(bound - counts[i], max(1, remaining * portions[i] // pool), rest)
            counts[i] = counts[i] + extra
            rest = rest - extra
    return np.array(counts)


def bell_draw(stream_key, dims, spread, reach, cuts=(), kind=jnp.bfloat16):
    drawn = jax.random.normal(stream_key, dims, jnp.float32) * spread
    if len(cuts) > 0:
        drawn = block_levels(stream_key, dims, cuts, -0.22, 0.18) * drawn
    return jnp.clip(drawn, min=-reach, max=reach).astype(kind)


def setup_inputs(seed: int = 0) -> dict:
    arg_keys = jax.random.split(jax.random.key(seed), 19)
    queries = bell_draw(arg_keys[0], (ROLL, LEN, HEADS * HD), 1.0, 6.0, ((1, 4), (2, 8)))
    key_rows = bell_draw(arg_keys[1], (ROLL, LEN, HEADS * HD), 1.0, 6.0, ((1, 4), (2, 8)))
    value_rows = bell_draw(arg_keys[2], (ROLL, LEN, HEADS * HD), 1.0, 6.0, ((1, 4), (2, 8)))
    decay_rate = draw_decay_rate(jax.random.fold_in(arg_keys[18], 71), 0)
    norm_gain = jnp.clip(1.0 + 0.18 * jax.random.normal(arg_keys[4], (HEADS * HD,), jnp.float32), 0.1, 1.9)
    attn_probe = bell_draw(arg_keys[5], (ROLL, LEN, HEADS * HD), 1.0, 6.0, ((1, 4), (2, 8)))
    hidden_in = bell_draw(arg_keys[6], (ROLL, LEN, D), 1.0, 6.0, ((1, 32),))
    moe_probe = bell_draw(arg_keys[7], (ROLL, LEN, D), 1.0, 6.0, ((1, 32),))
    router_weight = bell_draw(arg_keys[8], (D, EXP_WIN), D ** -0.5, 0.078125)
    routes_keys = jax.random.split(jax.random.fold_in(arg_keys[9], 1), ROLL * LEN // POS_DEV)
    routes_turns = jax.random.permutation(jax.random.fold_in(arg_keys[9], 3), ROLL * LEN // POS_DEV)
    routes = jax.vmap(lambda own, number: shared_out(jax.random.fold_in(arg_keys[9], 2), own, number, POS_DEV, EXP_WIN, TOP, MOST, 2))(routes_keys, routes_turns).reshape((ROLL, LEN, TOP))
    gate_weight = bell_draw(arg_keys[10], (EXP_WIN * SLICES, D, FF_DEV), D ** -0.5, 0.078125, ((0, 8), (1, 4)))
    up_weight = bell_draw(arg_keys[11], (EXP_WIN * SLICES, D, FF_DEV), D ** -0.5, 0.078125, ((0, 8), (1, 4)))
    down_weight = bell_draw(arg_keys[12], (EXP_WIN * SLICES, D, FF_DEV), FF_WIN ** -0.5, 0.09375, ((0, 8), (1, 4)))
    rollout_logprob = jnp.clip(-1.0 + 1.0 * jax.random.uniform(arg_keys[13], (ROLL, LEN), jnp.float32) ** block_levels(arg_keys[13], (ROLL, LEN), ((1, 4),), -0.2, 0.2), -1.0, 0.0)
    trainer_logprob = jnp.clip(-1.0 + 1.0 * jax.random.uniform(arg_keys[14], (ROLL, LEN), jnp.float32) ** block_levels(arg_keys[14], (ROLL, LEN), ((1, 4),), -0.2, 0.2), -1.0, 0.0)
    advantage = bell_draw(arg_keys[15], (ROLL, LEN), 1.0, 4.0, ((1, 4),), jnp.float32)
    clip_low = jnp.clip(jax.random.uniform(arg_keys[16], (1,), jnp.float32, 0.4, 0.95), 0.4, 0.95)
    clip_high = jnp.clip(jax.random.uniform(arg_keys[17], (1,), jnp.float32, 1.05, 2.5), 1.05, 2.5)
    return {"queries": queries, "key_rows": key_rows, "value_rows": value_rows, "decay_rate": decay_rate, "norm_gain": norm_gain, "attn_probe": attn_probe, "hidden_in": hidden_in, "moe_probe": moe_probe, "router_weight": router_weight, "routes": routes, "gate_weight": gate_weight, "up_weight": up_weight, "down_weight": down_weight, "rollout_logprob": rollout_logprob, "trainer_logprob": trainer_logprob, "advantage": advantage, "clip_low": clip_low, "clip_high": clip_high}


highest = lax.Precision.HIGHEST
norm_epsilon = 1e-06

def attention_grads(queries, key_rows, value_rows, decay_rate, norm_gain, attn_probe, coeff):

    def split_heads(array):
        return jnp.transpose(array.reshape(ROLL, LEN, HEADS, HD).astype(jnp.float32), (2, 0, 1, 3))

    def one_head(inputs):
        query_head, key_head, value_head, probe_head, rate, gain = inputs
        offsets = jnp.arange(LEN, dtype=jnp.float32)
        distance = offsets[:, None] - offsets[None, :]
        mask_decay = jnp.where(distance >= 0, jnp.exp(-rate * jnp.maximum(distance, 0.0)), 0.0)
        scores = jnp.einsum('ric,rjc->rij', query_head, key_head, precision=highest) * mask_decay
        output = jnp.einsum('rij,rjc->ric', scores, value_head, precision=highest)
        inverse = lax.rsqrt(lax.optimization_barrier(jnp.mean(output * output, axis=-1, keepdims=True)) + norm_epsilon)
        scaled = gain * (coeff[:, :, None] * probe_head)
        grad_out = inverse * scaled - output * inverse ** 3 * lax.optimization_barrier(jnp.mean(scaled * output, axis=-1, keepdims=True))
        product = jnp.einsum('ric,rjc->rij', grad_out, value_head, precision=highest) * mask_decay
        grad_query = jnp.einsum('rij,rjc->ric', product, key_head, precision=highest)
        grad_key = jnp.einsum('rij,ric->rjc', product, query_head, precision=highest)
        grad_value = jnp.einsum('rij,ric->rjc', scores, grad_out, precision=highest)
        return (grad_query.astype(jnp.bfloat16), grad_key.astype(jnp.bfloat16), grad_value.astype(jnp.bfloat16))
    gains = norm_gain.reshape(HEADS, HD)
    results = lax.map(one_head, (split_heads(queries), split_heads(key_rows), split_heads(value_rows), split_heads(attn_probe), decay_rate, gains))

    def merge_heads(array):
        return jnp.transpose(array, (1, 2, 0, 3)).reshape(ROLL, LEN, HEADS * HD)
    return (merge_heads(results[0]), merge_heads(results[1]), merge_heads(results[2]))

def expert_terms(token_flat, grad_flat, member, gate_slices, up_slices, down_slices, capacity):
    order = jnp.argsort(jnp.where(member, 0, 1).astype(jnp.int32), stable=True)[:capacity].astype(jnp.int32)
    valid = member[order].astype(jnp.float32)
    tokens_sel = token_flat[order]
    grads_sel = grad_flat[order]
    model_width = token_flat.shape[1]

    def one_slice(index, totals):
        dx_total, score_total = totals
        gate_mat = gate_slices[index]
        up_mat = up_slices[index]
        down_mat = down_slices[index]
        pre_gate = jnp.dot(tokens_sel, gate_mat, preferred_element_type=jnp.float32)
        pre_up = jnp.dot(tokens_sel, up_mat, preferred_element_type=jnp.float32)
        sigmoid_gate = jax.nn.sigmoid(pre_gate)
        activated = pre_gate * sigmoid_gate
        units = activated * pre_up
        unit_grad = jnp.dot(grads_sel, down_mat, preferred_element_type=jnp.float32)
        up_grad = (unit_grad * activated).astype(jnp.bfloat16)
        gate_grad = (unit_grad * pre_up * sigmoid_gate * (1.0 + pre_gate * (1.0 - sigmoid_gate))).astype(jnp.bfloat16)
        slice_dx = jnp.dot(gate_grad, gate_mat.T, preferred_element_type=jnp.float32) + jnp.dot(up_grad, up_mat.T, preferred_element_type=jnp.float32)
        slice_dx = lax.optimization_barrier(slice_dx.astype(jnp.bfloat16)).astype(jnp.float32)
        slice_score = lax.optimization_barrier(lax.optimization_barrier(jnp.sum(units * unit_grad, axis=-1)).astype(jnp.bfloat16)).astype(jnp.float32)
        return (dx_total + slice_dx, score_total + slice_score)
    start = (jnp.zeros((capacity, model_width), jnp.float32), jnp.zeros((capacity,), jnp.float32))
    dx_total, score_total = lax.fori_loop(0, gate_slices.shape[0], one_slice, start)
    full_dx = jnp.zeros(token_flat.shape, jnp.float32).at[order].add(dx_total * valid[:, None])
    full_score = jnp.zeros((token_flat.shape[0],), jnp.float32).at[order].add(score_total * valid)
    return (full_dx, full_score)

def reference(queries, key_rows, value_rows, decay_rate, norm_gain, attn_probe, hidden_in, moe_probe, router_weight, routes, gate_weight, up_weight, down_weight, rollout_logprob, trainer_logprob, advantage, clip_low, clip_high):
    importance = jnp.exp(trainer_logprob - rollout_logprob)
    clipped = jnp.minimum(jnp.maximum(importance, clip_low[0]), clip_high[0])
    coeff = -(clipped * advantage) / ROLL
    objective = coeff * trainer_logprob
    grad_queries, grad_keys, grad_values = attention_grads(queries, key_rows, value_rows, decay_rate, norm_gain, attn_probe, coeff)
    token_count = ROLL * LEN
    token_flat = hidden_in.reshape(token_count, D)
    grad_flat = (coeff[:, :, None] * moe_probe.astype(jnp.float32)).astype(jnp.bfloat16).reshape(token_count, D)
    routes_flat = routes.reshape(token_count, TOP)
    capacity = min(token_count, ROLL * N_SEQ * N_EXPERT * MOST)
    gate_all = gate_weight.reshape(EXP_WIN, SLICES, D, FF_DEV)
    up_all = up_weight.reshape(EXP_WIN, SLICES, D, FF_DEV)
    down_all = down_weight.reshape(EXP_WIN, SLICES, D, FF_DEV)

    def one_expert(inputs):
        expert_id, gate_slices, up_slices, down_slices = inputs
        member = jnp.any(routes_flat == expert_id, axis=-1)
        return expert_terms(token_flat, grad_flat, member, gate_slices, up_slices, down_slices, capacity)
    expert_ids = jnp.arange(EXP_WIN, dtype=jnp.int32)
    expert_dx, expert_score = lax.map(one_expert, (expert_ids, gate_all, up_all, down_all))
    onehot = (routes_flat[:, :, None] == expert_ids[None, None, :]).astype(jnp.float32)
    logits = jnp.dot(token_flat, router_weight, preferred_element_type=jnp.float32)
    chosen = jnp.einsum('nke,ne->nk', onehot, logits, precision=highest)
    exponent = jnp.exp(chosen)
    gates = exponent / lax.optimization_barrier(jnp.sum(exponent, axis=-1, keepdims=True))
    gate_expert = jnp.einsum('nk,nke->ne', gates, onehot, precision=highest)
    score_pick = jnp.einsum('nke,en->nk', onehot, expert_score, precision=highest)
    score_mean = lax.optimization_barrier(jnp.sum(gates * score_pick, axis=-1, keepdims=True))
    logit_grad = gates * (score_pick - score_mean)
    logit_expert = jnp.einsum('nk,nke->ne', logit_grad, onehot, precision=highest)
    grad_hidden = jnp.einsum('ne,end->nd', gate_expert, expert_dx, precision=highest)
    grad_hidden = grad_hidden + jnp.einsum('ne,de->nd', logit_expert, router_weight.astype(jnp.float32), precision=highest)
    grad_hidden = grad_hidden.astype(jnp.bfloat16).reshape(ROLL, LEN, D)
    return (objective, grad_queries, grad_keys, grad_values, grad_hidden)
```

```python
import jax
import jax.numpy as jnp
from jax import lax
from jax.experimental import pallas as pl
from jax.experimental.pallas import tpu as pltpu
from jax.sharding import PartitionSpec as P

highest = lax.Precision.HIGHEST
norm_epsilon = 1e-06
f32 = jnp.float32
bf16 = jnp.bfloat16
vmem_limit = 48 * 2**20

in_scale = 32.0
out_scale = 4.0


class Layout:
    def __init__(self, window_experts):
        self.seq = lax.axis_size("seq")
        self.chips = self.seq // 2
        self.spread = lax.axis_size("expert")
        self.experts = window_experts
        self.slices = self.spread // window_experts
        here = lax.axis_index("seq")
        self.chip, self.core = here // 2, here % 2
        self.expert = lax.axis_index("expert") // self.slices

    def swap_core(self, v):
        return lax.ppermute(v, "seq", [(i, i ^ 1) for i in range(self.seq)])

    def turn_chip(self, v, p):
        n = self.chips
        return lax.ppermute(
            v, "seq", [(i, ((i // 2 + p) % n) * 2 + i % 2) for i in range(self.seq)]
        )

    def later_chip(self, v, p):
        pairs = [(i, i + 2 * p) for i in range(self.seq) if 0 <= i + 2 * p < self.seq]
        return lax.ppermute(v, "seq", pairs)

    def turn_expert(self, v, d):
        n, m = self.experts, self.slices
        return lax.ppermute(
            v, "expert", [(i, ((i // m + d) % n) * m + i % m) for i in range(self.spread)]
        )

    def turn_slice(self, v, k):
        m = self.slices
        return lax.ppermute(
            v, "expert", [(i, (i // m) * m + (i % m + k) % m) for i in range(self.spread)]
        )


def params(**kw):
    return pltpu.CompilerParams(vmem_limit_bytes=vmem_limit, **kw)


def cost(flops, moved):
    return pl.CostEstimate(flops=int(flops), bytes_accessed=int(moved), transcendentals=0)


def pick_rows(groups, rank, first, count, padded):
    experts = rank.shape[0]
    halves, tokens, width = groups[0].shape
    total = tokens * len(groups)

    def body(rank_ref, *refs):
        group_refs, out_refs = refs[: len(groups)], refs[len(groups) :]
        slot = lax.broadcasted_iota(jnp.int32, (padded, total), 0)
        wanted = jnp.where(slot < count, slot + first, -2)
        for h in range(halves):
            rows = jnp.concatenate([g[h] for g in group_refs], axis=0)
            for d in range(experts):
                pick = (rank_ref[d : d + 1, :] == wanted).astype(bf16)
                out_refs[d][h] = jnp.dot(pick, rows, preferred_element_type=f32).astype(bf16)

    shape = jax.ShapeDtypeStruct((halves, padded, width), bf16)
    return pl.pallas_call(
        body,
        out_shape=[shape] * experts,
        compiler_params=params(),
        cost_estimate=cost(
            2 * experts * halves * padded * total * width,
            2 * halves * width * (total + experts * padded),
        ),
        name="pick_rows",
    )(rank, *groups)


def project(blocks, rows, mats, chip, chips):
    halves, padded, width = blocks[0].shape
    count = len(blocks)
    total = rows * count
    part = total // chips
    per_part = count // chips
    units = mats[0].shape[1]
    tile = 256 if units % 256 == 0 else units

    def body(chip_ref, *refs):
        block_refs = refs[:count]
        own_ref, other_ref, keep_ref, send_ref, held = refs[count:]

        @pl.when(pl.program_id(0) == 0)
        def _():
            column = lax.broadcasted_iota(jnp.int32, (1, count * padded), 1)
            target = jnp.full((1, count * padded), -1, jnp.int32)
            for b in range(count):
                place = (b // per_part - chip_ref[0] + chips) % chips
                start = place * part + (b % per_part) * rows
                inside = (column >= b * padded) & (column < b * padded + rows)
                target = jnp.where(inside, column - b * padded + start, target)
            line = lax.broadcasted_iota(jnp.int32, (total, count * padded), 0)
            pick = (line == target).astype(bf16)
            for h in range(halves):
                every = jnp.concatenate([b[h] for b in block_refs], axis=0)
                held[h] = jnp.dot(pick, every, preferred_element_type=f32).astype(bf16)

        result = jnp.dot(held[0], own_ref[...], preferred_element_type=f32)
        result = result + jnp.dot(held[1], other_ref[...], preferred_element_type=f32)
        keep_ref[...] = result[:part]
        for p in range(1, chips):
            send_ref[p - 1] = result[p * part : (p + 1) * part]

    mat_spec = pl.BlockSpec((width, tile), lambda i: (0, i))
    return pl.pallas_call(
        body,
        grid=(units // tile,),
        in_specs=[pl.BlockSpec(memory_space=pltpu.SMEM)]
        + [pl.BlockSpec((halves, padded, width), lambda i: (0, 0, 0))] * count
        + [mat_spec, mat_spec],
        out_specs=[
            pl.BlockSpec((part, tile), lambda i: (0, i)),
            pl.BlockSpec((chips - 1, part, tile), lambda i: (0, 0, i)),
        ],
        out_shape=[
            jax.ShapeDtypeStruct((part, units), f32),
            jax.ShapeDtypeStruct((chips - 1, part, units), f32),
        ],
        scratch_shapes=[pltpu.VMEM((halves, total, width), bf16)],
        compiler_params=params(),
        cost_estimate=cost(
            2 * halves * total * width * units, 2 * halves * width * units + 4 * total * units
        ),
        name="project",
    )(chip, *blocks, *mats)


def project_back(gate_parts, up_parts, gate_mat, up_mat):
    chips = len(gate_parts)
    part, units = gate_parts[0].shape
    width = gate_mat.shape[0]
    tile = 256 if width % 256 == 0 else width
    total = part * chips

    def body(*refs):
        gate_refs, up_refs = refs[:chips], refs[chips : 2 * chips]
        gate_mat_ref, up_mat_ref, out_ref, gate_all, up_all = refs[2 * chips :]

        @pl.when(pl.program_id(0) == 0)
        def _():
            for r in range(chips):
                gate_all[r * part : (r + 1) * part] = gate_refs[r][...]
                up_all[r * part : (r + 1) * part] = up_refs[r][...]

        contract = (((1,), (1,)), ((), ()))
        result = lax.dot_general(
            gate_all[...], gate_mat_ref[...], contract, preferred_element_type=f32
        )
        result = result + lax.dot_general(
            up_all[...], up_mat_ref[...], contract, preferred_element_type=f32
        )
        for r in range(chips):
            out_ref[r] = result[r * part : (r + 1) * part].astype(bf16)

    part_spec = pl.BlockSpec((part, units), lambda i: (0, 0))
    mat_spec = pl.BlockSpec((tile, units), lambda i: (i, 0))
    return pl.pallas_call(
        body,
        grid=(width // tile,),
        in_specs=[part_spec] * (2 * chips) + [mat_spec, mat_spec],
        out_specs=pl.BlockSpec((chips, part, tile), lambda i: (0, 0, i)),
        out_shape=jax.ShapeDtypeStruct((chips, part, width), bf16),
        scratch_shapes=[pltpu.VMEM((total, units), bf16)] * 2,
        compiler_params=params(),
        cost_estimate=cost(4 * total * width * units, 4 * width * units + 2 * total * width),
        name="project_back",
    )(*gate_parts, *up_parts, gate_mat, up_mat)


def combine(returned, scores, rank, gates, router, firsts, groups):
    chunk_count, experts = len(returned), len(returned[0])
    width = returned[0][0].shape[1]
    total = rank.shape[0]
    tokens = total // groups
    flat = [v for chunk in returned for v in chunk]

    def body(*refs):
        flat_refs = refs[: len(flat)]
        score_ref, rank_ref, gate_ref, router_ref = refs[len(flat) : len(flat) + 4]
        out_refs = refs[len(flat) + 4 :]
        acc = jnp.zeros((total, width), f32)
        picked = []
        slots = lax.broadcasted_iota(jnp.int32, (total, score_ref.shape[1]), 1)
        for d in range(experts):
            hit = rank_ref[:, d : d + 1] == slots
            picked.append(
                jnp.sum(jnp.where(hit, score_ref[d : d + 1, :], 0.0), axis=1, keepdims=True)
            )
        mean = sum(gate_ref[:, d : d + 1] * picked[d] for d in range(experts))
        for d in range(experts):
            grad = gate_ref[:, d : d + 1] * (picked[d] - mean)
            acc = acc + grad * router_ref[d : d + 1, :]
        for c in range(chunk_count):
            for d in range(experts):
                value = flat_refs[c * experts + d][...]
                slot = lax.broadcasted_iota(jnp.int32, (total, value.shape[0]), 1) + firsts[c]
                weight = jnp.where(rank_ref[:, d : d + 1] == slot, gate_ref[:, d : d + 1], 0.0)
                high = weight.astype(bf16)
                low = (weight - high.astype(f32)).astype(bf16)
                acc = acc + jnp.dot(high, value, preferred_element_type=f32)
                acc = acc + jnp.dot(low, value, preferred_element_type=f32)
        for g in range(groups):
            out_refs[g][...] = acc[g * tokens : (g + 1) * tokens].astype(bf16)

    return pl.pallas_call(
        body,
        out_shape=[jax.ShapeDtypeStruct((tokens, width), bf16)] * groups,
        compiler_params=params(),
        cost_estimate=cost(
            4 * total * width * experts * 68, 2 * width * (total + experts * 68)
        ),
        name="combine",
    )(*flat, scores, rank, gates, router)


def attention(
    place, queries, key_rows, value_rows, decay_rate, norm_gain, attn_probe, coeff
):
    rollouts, block_size, feature_width = queries.shape
    head_count = decay_rate.shape[0]
    head_size = feature_width // head_count
    shape_four = (rollouts, block_size, head_count, head_size)
    query_full = queries.reshape(shape_four).astype(f32)
    key_full = key_rows.reshape(shape_four).astype(f32)
    value_full = value_rows.reshape(shape_four).astype(f32)
    probe_full = attn_probe.reshape(shape_four).astype(f32)
    gain_full = norm_gain.reshape(head_count, head_size)
    offsets = jnp.arange(block_size, dtype=f32)
    rate_row = decay_rate[None, :]
    distance = offsets[:, None] - offsets[None, :]
    within = jnp.where(
        (distance >= 0)[None],
        jnp.exp(-decay_rate[:, None, None] * jnp.maximum(distance, 0.0)[None]),
        0.0,
    )
    lead_decay = jnp.exp(-rate_row * (offsets[:, None] + 1.0))[None, :, :, None]
    key_tail = jnp.exp(-rate_row * (block_size - 1.0 - offsets[:, None]))[None, :, :, None]
    query_tail = jnp.exp(-rate_row * offsets[:, None])[None, :, :, None]
    grad_tail = jnp.exp(-rate_row * (block_size - offsets[:, None]))[None, :, :, None]

    def block_decay(blocks):
        return jnp.exp(-decay_rate * (block_size * blocks)).reshape(1, head_count, 1, 1)

    def carried(summary, direction):
        partner = place.swap_core(summary)
        first = (place.core == 0) if direction > 0 else (place.core == 1)
        one = block_decay(1)
        near = jnp.where(first, partner + one * summary, summary + one * partner)
        outside = jnp.zeros_like(summary)
        for p in range(1, place.chips):
            outside = outside + block_decay(2 * (p - 1)) * place.later_chip(near, direction * p)
        return jnp.where(first, outside, partner + one * outside)

    forward_summary = jnp.einsum(
        "rjhk,rjhv->rhkv", key_full * key_tail, value_full, precision=highest
    )
    state_before = carried(forward_summary, 1)
    scores = jnp.einsum("rihc,rjhc->rhij", query_full, key_full, precision=highest) * within[None]
    output = jnp.einsum("rhij,rjhv->rihv", scores, value_full, precision=highest)
    output = output + lead_decay * jnp.einsum(
        "rihk,rhkv->rihv", query_full, state_before, precision=highest
    )
    inverse = lax.rsqrt(jnp.mean(output * output, axis=-1, keepdims=True) + norm_epsilon)
    scaled = gain_full[None, None] * (coeff[:, :, None, None] * probe_full)
    grad_out = inverse * scaled - output * inverse**3 * jnp.mean(
        scaled * output, axis=-1, keepdims=True
    )
    backward_summary = jnp.einsum(
        "rihk,rihv->rhkv", query_full * query_tail, grad_out, precision=highest
    )
    state_after = carried(backward_summary, -1)
    product = jnp.einsum("rihv,rjhv->rhij", grad_out, value_full, precision=highest) * within[None]
    grad_query = jnp.einsum("rhij,rjhk->rihk", product, key_full, precision=highest)
    grad_query = grad_query + lead_decay * jnp.einsum(
        "rihv,rhkv->rihk", grad_out, state_before, precision=highest
    )
    grad_key = jnp.einsum("rhij,rihk->rjhk", product, query_full, precision=highest)
    grad_key = grad_key + grad_tail * jnp.einsum(
        "rjhv,rhkv->rjhk", value_full, state_after, precision=highest
    )
    grad_value = jnp.einsum("rhij,rihv->rjhv", scores, grad_out, precision=highest)
    grad_value = grad_value + grad_tail * jnp.einsum(
        "rjhk,rhkv->rjhv", key_full, state_after, precision=highest
    )
    out_shape = (rollouts, block_size, feature_width)
    return tuple(v.reshape(out_shape).astype(bf16) for v in (grad_query, grad_key, grad_value))


def expert_block(
    place, hidden_in, moe_probe, router_weight, routes, gate_weight, up_weight, down_weight, coeff
):
    rollouts, positions, model_width = hidden_in.shape
    chips, experts, slices = place.chips, place.experts, place.slices
    tokens = rollouts * positions
    width = gate_weight.shape[1]
    own_mats = (gate_weight[0], up_weight[0], down_weight[0])

    hidden = hidden_in.reshape(tokens, model_width)
    local_coeff = lax.dynamic_slice_in_dim(
        coeff, lax.axis_index("expert") * positions, positions, 1
    )
    grads = (local_coeff[:, :, None] * moe_probe.astype(f32)).astype(bf16)
    grads = grads.reshape(tokens, model_width)

    def halves_of(v, p):
        chip = (place.chip + p) % chips
        return jnp.stack(
            [
                lax.dynamic_slice_in_dim(v, (2 * chip + core) * width, width, 1)
                for core in (place.core, 1 - place.core)
            ]
        )

    far = (place.expert + jnp.arange(experts, dtype=jnp.int32)) % experts
    logits = jnp.dot(hidden, router_weight, preferred_element_type=f32)
    flat_routes = routes.reshape(tokens, -1)
    onehot = (flat_routes[:, :, None] == jnp.arange(experts, dtype=jnp.int32)).astype(f32)
    chosen = jnp.sum(onehot * logits[:, None, :], axis=-1)
    exponent = jnp.exp(chosen)
    gate = exponent / jnp.sum(exponent, axis=-1, keepdims=True)
    near_hot = (flat_routes[:, :, None] == far).astype(f32)
    facts = jnp.concatenate(
        [near_hot.sum(axis=1), jnp.sum(near_hot * gate[:, :, None], axis=1)], axis=1
    )
    all_facts = [facts] + [place.turn_chip(facts, p) for p in range(1, chips)]

    def across(v):
        return [halves_of(v, 0)] + [
            place.turn_chip(halves_of(v, p), p) for p in range(1, chips)
        ]

    hidden_groups = across(hidden)
    grad_groups = across(grads)
    pairs = [(m, place.swap_core(m)) for m in own_mats]

    fact_stack = jnp.stack(all_facts)
    member, gates = fact_stack[:, :, :experts], fact_stack[:, :, experts:]
    whose = (place.chip - jnp.arange(chips)) % chips
    earlier = (whose[None, :] < whose[:, None]).astype(f32)
    offset = jnp.sum(earlier[:, :, None] * member.sum(axis=1)[None], axis=1)
    step = jnp.arange(tokens)
    below = (step[:, None] > step[None, :]).astype(f32)
    rank = jnp.einsum("ts,gse->gte", below, member) + offset[:, None, :]
    rank = jnp.where(member > 0, rank, -1.0).astype(jnp.int32)
    rank = rank.reshape(chips * tokens, experts)
    gates = gates.reshape(chips * tokens, experts)
    rank_lanes = rank.T

    most = chips * rollouts * (positions // 2 + 1)
    small = max(16, most // 2 // 16 * 16)
    chunks = [(0, small), (small, most - small)]
    chip_here = place.chip.reshape(1).astype(jnp.int32)

    def dispatch(groups, first, count):
        padded = -(-count // 16) * 16
        picked = pick_rows(groups, rank_lanes, first, count, padded)
        mine = [picked[0]] + [place.turn_expert(picked[d], d) for d in range(1, experts)]
        blocks = list(mine)
        for k in range(1, slices):
            blocks += [place.turn_slice(v, k) for v in mine]
        return blocks

    def partial(blocks, count, pair, scale):
        keep, send = project(blocks, count, pair, chip_here, chips)
        ready = (send * scale).astype(jnp.float16)
        arrived = [place.turn_chip(ready[p - 1], p) for p in range(1, chips)]
        return keep, arrived

    def settle(part, scale):
        keep, arrived = part
        return keep + sum(v.astype(f32) for v in arrived) * (1.0 / scale)

    def ring(v):
        found = [v] + [None] * (chips - 1)
        for p in range(1, chips):
            found[chips - p] = place.turn_chip(v, p)
        return found

    def forward(first, count):
        blocks = dispatch(hidden_groups, first, count)
        gate_part = partial(blocks, count, pairs[0], in_scale)
        up_part = partial(blocks, count, pairs[1], in_scale)
        blocks = dispatch(grad_groups, first, count)
        down_part = partial(blocks, count, pairs[2], out_scale)
        return gate_part, up_part, down_part

    def middle(parts):
        pre_gate = settle(parts[0], in_scale)
        pre_up = settle(parts[1], in_scale)
        unit_grad = settle(parts[2], out_scale)
        sigmoid_gate = jax.nn.sigmoid(pre_gate)
        activated = pre_gate * sigmoid_gate
        units = activated * pre_up
        score = jnp.sum(units * unit_grad, axis=-1).astype(bf16)
        up_grad = (unit_grad * activated).astype(bf16)
        gate_grad = (
            unit_grad * pre_up * sigmoid_gate * (1.0 + pre_gate * (1.0 - sigmoid_gate))
        ).astype(bf16)
        return ring(gate_grad), ring(up_grad), ring(score)

    def rows_for(parts, k, count):
        per_part = slices // chips
        block = experts * count
        which = (k // per_part - place.chip + chips) % chips
        part = lax.dynamic_index_in_dim(parts, which, 0, keepdims=False)
        return lax.slice_in_dim(part, (k % per_part) * block, (k % per_part + 1) * block, axis=0)

    def home(parts, count):
        total = rows_for(parts, 0, count).astype(f32)
        for k in range(1, slices):
            total = total + place.turn_slice(rows_for(parts, k, count), -k).astype(f32)
        return total

    def homeward(v, count):
        blocks = [lax.slice_in_dim(v, d * count, (d + 1) * count, axis=0) for d in range(experts)]
        return [blocks[0]] + [place.turn_expert(blocks[d], -d) for d in range(1, experts)]

    def backward(gate_parts, up_parts, count):
        out = []
        for h in range(2):
            dx = project_back(gate_parts, up_parts, pairs[0][h], pairs[1][h])
            out.append(homeward(home(dx, count).astype(bf16), count))
        return out

    first_parts = forward(*chunks[0])
    second_parts = forward(*chunks[1])
    first_grads = middle(first_parts)
    first_back = backward(first_grads[0], first_grads[1], chunks[0][1])
    second_grads = middle(second_parts)
    second_back = backward(second_grads[0], second_grads[1], chunks[1][1])

    score_rows = [
        home(jnp.stack(g[2]), count).reshape(experts, count)
        for g, (_, count) in zip((first_grads, second_grads), chunks)
    ]
    score_rows = jnp.concatenate(score_rows, axis=1)
    score_home = jnp.concatenate(
        [score_rows[:1]]
        + [place.turn_expert(score_rows[d : d + 1], -d) for d in range(1, experts)],
        axis=0,
    )

    router_rows = halves_of(router_weight.T.astype(f32), 0)
    router_rows = jnp.take(router_rows, far, axis=1)
    firsts = [first for first, _ in chunks]
    result = jnp.zeros((tokens, model_width), bf16)
    for h in range(2):
        groups = combine(
            [first_back[h], second_back[h]],
            score_home,
            rank,
            gates,
            router_rows[h],
            firsts,
            chips,
        )
        core = place.core if h == 0 else 1 - place.core
        for g in range(chips):
            part = groups[g] if g == 0 else place.turn_chip(groups[g], -g)
            chip = (place.chip + g) % chips
            result = lax.dynamic_update_slice_in_dim(result, part, (2 * chip + core) * width, 1)
    return result.reshape(rollouts, positions, model_width)


def on_device(
    queries,
    key_rows,
    value_rows,
    decay_rate,
    norm_gain,
    attn_probe,
    hidden_in,
    moe_probe,
    router_weight,
    routes,
    gate_weight,
    up_weight,
    down_weight,
    rollout_logprob,
    trainer_logprob,
    advantage,
    clip_low,
    clip_high,
):
    place = Layout(router_weight.shape[1])
    importance = jnp.exp(trainer_logprob - rollout_logprob)
    clipped = jnp.minimum(jnp.maximum(importance, clip_low[0]), clip_high[0])
    coeff = -(clipped * advantage) / queries.shape[0]
    objective = coeff * trainer_logprob
    grad_hidden = expert_block(
        place,
        hidden_in,
        moe_probe,
        router_weight,
        routes,
        gate_weight,
        up_weight,
        down_weight,
        coeff,
    )
    attention_grads = attention(
        place, queries, key_rows, value_rows, decay_rate, norm_gain, attn_probe, coeff
    )
    return (objective, *attention_grads, grad_hidden)


def solution(mesh):
    in_specs = (
        P(None, "seq", "expert"),
        P(None, "seq", "expert"),
        P(None, "seq", "expert"),
        P("expert"),
        P("expert"),
        P(None, "seq", "expert"),
        P(None, ("seq", "expert"), None),
        P(None, ("seq", "expert"), None),
        P(),
        P(None, ("seq", "expert"), None),
        P("expert", "seq", None),
        P("expert", "seq", None),
        P("expert", "seq", None),
        P(None, "seq"),
        P(None, "seq"),
        P(None, "seq"),
        P(),
        P(),
    )
    out_specs = (
        P(None, "seq"),
        P(None, "seq", "expert"),
        P(None, "seq", "expert"),
        P(None, "seq", "expert"),
        P(None, ("seq", "expert"), None),
    )
    return jax.shard_map(
        on_device, mesh=mesh, in_specs=in_specs, out_specs=out_specs, check_vma=False
    )
```

```python
import jax
import jax.numpy as jnp
from jax import lax
from jax.experimental import pallas as pl
from jax.experimental.pallas import tpu as pltpu
from jax.sharding import PartitionSpec as P

highest = lax.Precision.HIGHEST
norm_epsilon = 1e-06
f32 = jnp.float32
bf16 = jnp.bfloat16
vmem_limit = 48 * 2**20

in_scale = 32.0
out_scale = 4.0


class Layout:
    def __init__(self, window_experts):
        self.seq = lax.axis_size("seq")
        self.chips = self.seq // 2
        self.spread = lax.axis_size("expert")
        self.experts = window_experts
        self.slices = self.spread // window_experts
        here = lax.axis_index("seq")
        self.chip, self.core = here // 2, here % 2
        self.expert = lax.axis_index("expert") // self.slices

    def swap_core(self, v):
        return lax.ppermute(v, "seq", [(i, i ^ 1) for i in range(self.seq)])

    def turn_chip(self, v, p):
        n = self.chips
        return lax.ppermute(
            v, "seq", [(i, ((i // 2 + p) % n) * 2 + i % 2) for i in range(self.seq)]
        )

    def later_chip(self, v, p):
        pairs = [(i, i + 2 * p) for i in range(self.seq) if 0 <= i + 2 * p < self.seq]
        return lax.ppermute(v, "seq", pairs)

    def between_experts(self, v):
        n, m = self.experts, self.slices
        groups = [[q * m + j for q in range(n)] for j in range(m)]
        return lax.all_to_all(v, "expert", 0, 0, axis_index_groups=groups, tiled=True)

    def turn_expert(self, v, d):
        n, m = self.experts, self.slices
        return lax.ppermute(
            v, "expert", [(i, ((i // m + d) % n) * m + i % m) for i in range(self.spread)]
        )

    def turn_slice(self, v, k):
        m = self.slices
        return lax.ppermute(
            v, "expert", [(i, (i // m) * m + (i % m + k) % m) for i in range(self.spread)]
        )


def params(**kw):
    return pltpu.CompilerParams(vmem_limit_bytes=vmem_limit, **kw)


short = pl.CostEstimate(flops=1000, bytes_accessed=1000, transcendentals=0)


def tile_of(size):
    return 768 if size % 768 == 0 else size


def any_spec():
    return pl.BlockSpec(memory_space=pl.ANY)


def pick_rows(groups, rank, first, count, padded, after):
    experts = rank.shape[0]
    halves, tokens, width = groups[0].shape
    total = tokens * len(groups)

    def body(rank_ref, *refs):
        group_refs, out_ref = refs[: len(groups)], refs[-1]
        slot = lax.broadcasted_iota(jnp.int32, (padded, total), 0)
        wanted = jnp.where(slot < count, slot + first, -2)
        for h in range(halves):
            rows = jnp.concatenate([g[h] for g in group_refs], axis=0)
            for d in range(experts):
                pick = (rank_ref[d : d + 1, :] == wanted).astype(bf16)
                out_ref[d, h] = jnp.dot(pick, rows, preferred_element_type=f32).astype(bf16)

    vmem = pl.BlockSpec(memory_space=pltpu.VMEM)
    return pl.pallas_call(
        body,
        in_specs=[vmem] * (1 + len(groups)) + [any_spec()] * len(after),
        out_specs=vmem,
        out_shape=jax.ShapeDtypeStruct((experts, halves, padded, width), bf16),
        compiler_params=params(),
        cost_estimate=short,
        name="pick_rows",
    )(rank, *groups, *after)


def project(jobs, rows, chip, chips, after):
    experts, halves, padded, width = jobs[0][0][0].shape
    arrays_each = len(jobs[0][0])
    count = arrays_each * experts
    part = rows * count // chips
    per_part = count // chips
    units = jobs[0][1][0][0].shape[1]
    tile = tile_of(units)
    arrays = [v for job in jobs for v in job[0]]
    mats = [half for job in jobs for pair in job[1] for half in pair]
    owner = [j for j, job in enumerate(jobs) for _ in job[1]]
    mat_count = len(owner)

    def body(chip_ref, *refs):
        array_refs = refs[: len(arrays)]
        mat_refs = refs[len(arrays) : len(arrays) + len(mats)]
        keep_ref, send_ref, held = refs[-3:]

        def left(job, h):
            found = [
                r[:, h].reshape(experts * padded, width)
                for r in array_refs[job * arrays_each : (job + 1) * arrays_each]
            ]
            return found[0] if len(found) == 1 else jnp.concatenate(found, axis=0)

        for m in range(mat_count):
            result = jnp.dot(
                left(owner[m], 0), mat_refs[2 * m][...], preferred_element_type=f32
            )
            result = result + jnp.dot(
                left(owner[m], 1), mat_refs[2 * m + 1][...], preferred_element_type=f32
            )
            held[...] = result.reshape(chips, per_part * padded, tile)
            for p in range(chips):
                value = held[(chip_ref[0] + p) % chips]
                for b in range(per_part):
                    piece = value[b * padded : b * padded + rows]
                    if p == 0:
                        keep_ref[m, b * rows : (b + 1) * rows] = piece
                    else:
                        send_ref[p - 1, m, b * rows : (b + 1) * rows] = piece

    mat_spec = pl.BlockSpec((width, tile), lambda i: (0, i))
    return pl.pallas_call(
        body,
        grid=(units // tile,),
        in_specs=[pl.BlockSpec(memory_space=pltpu.SMEM)]
        + [pl.BlockSpec(arrays[0].shape, lambda i: (0, 0, 0, 0))] * len(arrays)
        + [mat_spec] * len(mats)
        + [any_spec()] * len(after),
        out_specs=[
            pl.BlockSpec((mat_count, part, tile), lambda i: (0, 0, i)),
            pl.BlockSpec((chips - 1, mat_count, part, tile), lambda i: (0, 0, 0, i)),
        ],
        out_shape=[
            jax.ShapeDtypeStruct((mat_count, part, units), f32),
            jax.ShapeDtypeStruct((chips - 1, mat_count, part, units), f32),
        ],
        scratch_shapes=[pltpu.VMEM((chips, per_part * padded, tile), f32)],
        compiler_params=params(),
        cost_estimate=short,
        name="project",
    )(chip, *arrays, *mats, *after)


def project_back(groups, mats, chip, rows, after):
    chips = len(groups[0])
    units = groups[0][0].shape[2]
    width = mats[0][0].shape[0]
    halves = len(mats)
    tile = tile_of(width)
    steps = width // tile
    parts = [v for group in groups for v in group]
    sizes = [group[0].shape[1] for group in groups]
    rooms = [-(-size // 16) * 16 for size in sizes]
    bases = [chips * sum(rooms[:g]) for g in range(len(groups))]
    total = chips * sum(rooms)
    counts = [size * chips // rows for size in sizes]

    def body(chip_ref, *refs):
        part_refs = refs[: len(parts)]
        mat_refs = refs[len(parts) : len(parts) + 2 * halves]
        out_refs = refs[-2 - len(groups) : -2]
        gate_all, up_all = refs[-2:]
        step = pl.program_id(0)

        @pl.when(step == 0)
        def _():
            for g, size in enumerate(sizes):
                for r in range(chips):
                    place = (chip_ref[0] + r) % chips
                    start = pl.multiple_of(bases[g] + place * rooms[g], 16)
                    gate_all[pl.ds(start, size)] = part_refs[g * chips + r][0]
                    up_all[pl.ds(start, size)] = part_refs[g * chips + r][1]

        def multiply(gate_mat_ref, up_mat_ref):
            contract = (((1,), (1,)), ((), ()))
            result = lax.dot_general(
                gate_all[...], gate_mat_ref[...], contract, preferred_element_type=f32
            )
            result = result + lax.dot_general(
                up_all[...], up_mat_ref[...], contract, preferred_element_type=f32
            )
            for g, count in enumerate(counts):
                per_part = count // chips
                for b in range(count):
                    start = bases[g] + b // per_part * rooms[g] + b % per_part * rows
                    out_refs[g][b, 0] = result[start : start + rows].astype(bf16)

        if halves == 1:
            multiply(*mat_refs)
        else:
            for h in range(halves):

                @pl.when(step // steps == h)
                def _():
                    multiply(mat_refs[2 * h], mat_refs[2 * h + 1])

    def mat_spec(h):
        return pl.BlockSpec((tile, units), lambda i: (jnp.clip(i - h * steps, 0, steps - 1), 0))

    def row_spec(count):
        return pl.BlockSpec((count, 1, rows, tile), lambda i: (0, i // steps, 0, i % steps))

    return pl.pallas_call(
        body,
        grid=(halves * steps,),
        in_specs=[pl.BlockSpec(memory_space=pltpu.SMEM)]
        + [pl.BlockSpec(v.shape, lambda i: (0, 0, 0)) for v in parts]
        + [mat_spec(h) for h in range(halves) for _ in range(2)]
        + [any_spec()] * len(after),
        out_specs=[row_spec(count) for count in counts],
        out_shape=[
            jax.ShapeDtypeStruct((count, halves, rows, width), bf16) for count in counts
        ],
        scratch_shapes=[pltpu.VMEM((total, units), bf16)] * 2,
        compiler_params=params(),
        cost_estimate=short,
        name="project_back",
    )(chip, *parts, *[m for pair in mats for m in pair], *after)


def combine(returned, scores, rank, gates, router, firsts, groups):
    experts, _, _, width = returned[0][0].shape
    counts = [v.shape[2] for v, _ in returned]
    total = rank.shape[0]
    tokens = total // groups

    def body(*refs):
        returned_refs = refs[: len(returned)]
        score_ref, rank_ref, gate_ref, router_ref = refs[len(returned) : len(returned) + 4]
        out_refs = refs[len(returned) + 4 :]
        acc = jnp.zeros((total, width), f32)
        picked = []
        slots = lax.broadcasted_iota(jnp.int32, (total, score_ref.shape[1]), 1)
        for d in range(experts):
            hit = rank_ref[:, d : d + 1] == slots
            picked.append(
                jnp.sum(jnp.where(hit, score_ref[d : d + 1, :], 0.0), axis=1, keepdims=True)
            )
        mean = sum(gate_ref[:, d : d + 1] * picked[d] for d in range(experts))
        for d in range(experts):
            grad = gate_ref[:, d : d + 1] * (picked[d] - mean)
            acc = acc + grad * router_ref[d : d + 1, :]
        for c, rows_ref in enumerate(returned_refs):
            for d in range(experts):
                value = rows_ref[d, 0]
                slot = lax.broadcasted_iota(jnp.int32, (total, value.shape[0]), 1) + firsts[c]
                weight = jnp.where(rank_ref[:, d : d + 1] == slot, gate_ref[:, d : d + 1], 0.0)
                high = weight.astype(bf16)
                low = (weight - high.astype(f32)).astype(bf16)
                acc = acc + jnp.dot(high, value, preferred_element_type=f32)
                acc = acc + jnp.dot(low, value, preferred_element_type=f32)
        for g in range(groups):
            out_refs[g][...] = acc[g * tokens : (g + 1) * tokens].astype(bf16)

    row_count = experts * sum(counts)

    def half_spec(count, h):
        return pl.BlockSpec((experts, 1, count, width), lambda i: (0, h, 0, 0))

    def whole_spec(v):
        return pl.BlockSpec(v.shape, lambda i: (0, 0))

    return pl.pallas_call(
        body,
        grid=(1,),
        in_specs=[half_spec(v.shape[2], h) for v, h in returned]
        + [whole_spec(v) for v in (scores, rank, gates, router)],
        out_specs=[pl.BlockSpec((tokens, width), lambda i: (0, 0))] * groups,
        out_shape=[jax.ShapeDtypeStruct((tokens, width), bf16)] * groups,
        compiler_params=params(),
        cost_estimate=short,
        name="combine",
    )(*[v for v, _ in returned], scores, rank, gates, router)


def split3(v):
    high = v.astype(bf16)
    rest = v - high.astype(f32)
    middle = rest.astype(bf16)
    return high, middle, (rest - middle.astype(f32)).astype(bf16)


def dot_left(a, b, dims):
    contract = (((dims[0],), (dims[1],)), ((), ()))
    return sum(lax.dot_general(t, b, contract, preferred_element_type=f32) for t in split3(a))


def dot_right(a, b, dims):
    contract = (((dims[0],), (dims[1],)), ((), ()))
    return sum(lax.dot_general(a, t, contract, preferred_element_type=f32) for t in split3(b))


def dot_full(a, b, dims):
    contract = (((dims[0],), (dims[1],)), ((), ()))
    return lax.dot_general(a, b, contract, precision=highest, preferred_element_type=f32)


def head_specs(rollouts, block, head):
    rows = pl.BlockSpec((rollouts, block, head), lambda h: (0, 0, h))
    state = pl.BlockSpec((rollouts, 1, head, head), lambda h: (0, h, 0, 0))
    return pl.BlockSpec(memory_space=pltpu.SMEM), rows, state


def key_value_state(key_rows, value_rows, decay_rate, after):
    rollouts, block, width = key_rows.shape
    heads = decay_rate.shape[0]
    head = width // heads
    smem, rows, state = head_specs(rollouts, block, head)

    def body(rate_ref, key_ref, value_ref, *refs):
        rate = rate_ref[pl.program_id(0)]
        offset = lax.broadcasted_iota(jnp.int32, (block, 1), 0).astype(f32)
        tail = jnp.exp(-rate * (block - 1.0 - offset))
        for r in range(rollouts):
            decayed = key_ref[r].astype(f32) * tail
            refs[-1][r, 0] = dot_left(decayed, value_ref[r], (0, 0))

    return pl.pallas_call(
        body,
        grid=(heads,),
        in_specs=[smem, rows, rows] + [any_spec()] * len(after),
        out_specs=state,
        out_shape=jax.ShapeDtypeStruct((rollouts, heads, head, head), f32),
        compiler_params=params(),
        cost_estimate=short,
        name="key_value_state",
    )(decay_rate, key_rows, value_rows, *after)


def local_grads(
    queries, key_rows, value_rows, attn_probe, gain, coeff, decay_rate, state, after
):
    rollouts, block, width = queries.shape
    heads = decay_rate.shape[0]
    head = width // heads
    smem, rows, state_spec = head_specs(rollouts, block, head)

    def body(rate_ref, q_ref, k_ref, v_ref, probe_ref, gain_ref, coeff_ref, state_ref, *refs):
        grad_q_ref, grad_k_ref, grad_v_ref, summary_ref = refs[-4:]
        rate = rate_ref[pl.program_id(0)]
        offset = lax.broadcasted_iota(jnp.int32, (block, 1), 0).astype(f32)
        lead = jnp.exp(-rate * (offset + 1.0))
        tail = jnp.exp(-rate * offset)
        line = lax.broadcasted_iota(jnp.int32, (block, block), 0)
        column = lax.broadcasted_iota(jnp.int32, (block, block), 1)
        distance = (line - column).astype(f32)
        within = jnp.where(line >= column, jnp.exp(-rate * jnp.maximum(distance, 0.0)), 0.0)
        for r in range(rollouts):
            query, key, value, before = q_ref[r], k_ref[r], v_ref[r], state_ref[r, 0]
            scores = lax.dot_general(
                query, key, (((1,), (1,)), ((), ())), preferred_element_type=f32
            )
            scores = scores * within
            output = dot_left(scores, value, (1, 0))
            output = output + lead * dot_right(query, before, (1, 0))
            inverse = lax.rsqrt(
                jnp.mean(output * output, axis=-1, keepdims=True) + norm_epsilon
            )
            scaled = gain_ref[...] * (coeff_ref[:, r : r + 1] * probe_ref[r].astype(f32))
            grad_out = inverse * scaled - output * inverse**3 * jnp.mean(
                scaled * output, axis=-1, keepdims=True
            )
            summary_ref[r, 0] = dot_right(query, tail * grad_out, (0, 0))
            product = dot_left(grad_out, value, (1, 1)) * within
            grad_q = dot_left(product, key, (1, 0))
            grad_q = grad_q + lead * dot_full(grad_out, before, (1, 1))
            grad_q_ref[r] = grad_q.astype(bf16)
            grad_k_ref[r] = dot_left(product, query, (0, 0))
            grad_v_ref[r] = dot_full(scores, grad_out, (0, 0))

    return pl.pallas_call(
        body,
        grid=(heads,),
        in_specs=[
            smem,
            rows,
            rows,
            rows,
            rows,
            pl.BlockSpec((1, head), lambda h: (0, h)),
            pl.BlockSpec((block, rollouts), lambda h: (0, 0)),
            state_spec,
        ]
        + [any_spec()] * len(after),
        out_specs=[rows, rows, rows, state_spec],
        out_shape=[
            jax.ShapeDtypeStruct(queries.shape, bf16),
            jax.ShapeDtypeStruct(queries.shape, f32),
            jax.ShapeDtypeStruct(queries.shape, f32),
            jax.ShapeDtypeStruct(state.shape, f32),
        ],
        compiler_params=params(),
        cost_estimate=short,
        name="local_grads",
    )(decay_rate, queries, key_rows, value_rows, attn_probe, gain, coeff, state, *after)


def later_grads(key_rows, value_rows, grad_k, grad_v, decay_rate, state, after):
    rollouts, block, width = key_rows.shape
    heads = decay_rate.shape[0]
    head = width // heads
    smem, rows, state_spec = head_specs(rollouts, block, head)

    def body(rate_ref, k_ref, v_ref, grad_k_ref, grad_v_ref, state_ref, *refs):
        out_k_ref, out_v_ref = refs[-2:]
        rate = rate_ref[pl.program_id(0)]
        offset = lax.broadcasted_iota(jnp.int32, (block, 1), 0).astype(f32)
        tail = jnp.exp(-rate * (block - offset))
        for r in range(rollouts):
            after_state = state_ref[r, 0]
            grad_k = grad_k_ref[r] + tail * dot_right(v_ref[r], after_state, (1, 1))
            grad_v = grad_v_ref[r] + tail * dot_right(k_ref[r], after_state, (1, 0))
            out_k_ref[r] = grad_k.astype(bf16)
            out_v_ref[r] = grad_v.astype(bf16)

    return pl.pallas_call(
        body,
        grid=(heads,),
        in_specs=[smem, rows, rows, rows, rows, state_spec] + [any_spec()] * len(after),
        out_specs=[rows, rows],
        out_shape=[jax.ShapeDtypeStruct(key_rows.shape, bf16)] * 2,
        compiler_params=params(),
        cost_estimate=short,
        name="later_grads",
    )(decay_rate, key_rows, value_rows, grad_k, grad_v, state, *after)


def carried(place, summary, decay_rate, block_size, direction):
    def block_decay(blocks):
        return jnp.exp(-decay_rate * (block_size * blocks)).reshape(1, -1, 1, 1)

    partner = place.swap_core(summary)
    first = (place.core == 0) if direction > 0 else (place.core == 1)
    one = block_decay(1)
    near = jnp.where(first, partner + one * summary, summary + one * partner)
    outside = jnp.zeros_like(summary)
    for p in range(1, place.chips):
        outside = outside + block_decay(2 * (p - 1)) * place.later_chip(near, direction * p)
    return jnp.where(first, outside, partner + one * outside)


def cut_features(v, scale, chip_core, chips, after):
    tokens, model_width = v.shape
    width = model_width // (2 * chips)

    def body(where_ref, v_ref, *refs):
        keep_ref, send_ref = refs[-2:]
        for p in range(chips):
            chip = (where_ref[0] + p) % chips
            for h in range(2):
                core = where_ref[1] if h == 0 else 1 - where_ref[1]
                start = pl.multiple_of((2 * chip + core) * width, 128)
                value = v_ref[:, pl.ds(start, width)]
                if scale is not None:
                    value = (refs[0][...] * value.astype(f32)).astype(bf16)
                if p == 0:
                    keep_ref[h] = value
                else:
                    send_ref[p - 1, h] = value

    vmem = pl.BlockSpec(memory_space=pltpu.VMEM)
    extra = [] if scale is None else [scale]
    return pl.pallas_call(
        body,
        in_specs=[pl.BlockSpec(memory_space=pltpu.SMEM), vmem]
        + [vmem] * len(extra)
        + [any_spec()] * len(after),
        out_specs=[vmem, vmem],
        out_shape=[
            jax.ShapeDtypeStruct((2, tokens, width), bf16),
            jax.ShapeDtypeStruct((chips - 1, 2, tokens, width), bf16),
        ],
        compiler_params=params(),
        cost_estimate=short,
        name="cut_features",
    )(chip_core, v, *extra, *after)


def expert_and_attention(
    place,
    hidden_in,
    moe_probe,
    router_weight,
    routes,
    gate_weight,
    up_weight,
    down_weight,
    coeff,
    queries,
    key_rows,
    value_rows,
    decay_rate,
    norm_gain,
    attn_probe,
):
    rollouts, positions, model_width = hidden_in.shape
    chips, experts, slices = place.chips, place.experts, place.slices
    tokens = rollouts * positions
    width = gate_weight.shape[1]
    own_mats = (gate_weight[0], up_weight[0], down_weight[0])

    hidden = hidden_in.reshape(tokens, model_width)
    local_coeff = lax.dynamic_slice_in_dim(
        coeff, lax.axis_index("expert") * positions, positions, 1
    )
    chip_here = place.chip.reshape(1).astype(jnp.int32)
    chip_core = jnp.stack([place.chip, place.core]).astype(jnp.int32)
    last = []

    def ordered(kernel, *args, needs=()):
        result = kernel(*args, (*last, *needs))
        last[:] = [result[0] if isinstance(result, (list, tuple)) else result]
        return result

    def across(v, scale):
        keep, send = ordered(cut_features, v, scale, chip_core, chips)
        return [keep] + [place.turn_chip(send[p - 1], p) for p in range(1, chips)]

    hidden_groups = across(hidden, None)
    grad_groups = across(
        moe_probe.reshape(tokens, model_width), local_coeff.reshape(tokens, 1)
    )

    def halves_of(v, p):
        chip = (place.chip + p) % chips
        return jnp.stack(
            [
                lax.dynamic_slice_in_dim(v, (2 * chip + core) * width, width, 1)
                for core in (place.core, 1 - place.core)
            ]
        )

    logits = jnp.dot(hidden, router_weight, preferred_element_type=f32)
    flat_routes = routes.reshape(tokens, -1)
    onehot = (flat_routes[:, :, None] == jnp.arange(experts, dtype=jnp.int32)).astype(f32)
    chosen = jnp.sum(onehot * logits[:, None, :], axis=-1)
    exponent = jnp.exp(chosen)
    gate = exponent / jnp.sum(exponent, axis=-1, keepdims=True)
    facts = jnp.concatenate(
        [onehot.sum(axis=1), jnp.sum(onehot * gate[:, :, None], axis=1)], axis=1
    )
    all_facts = [facts] + [place.turn_chip(facts, p) for p in range(1, chips)]

    pairs = [(m, place.swap_core(m)) for m in own_mats[:2]]

    fact_stack = jnp.stack(all_facts)
    member, gates = fact_stack[:, :, :experts], fact_stack[:, :, experts:]
    whose = (place.chip - jnp.arange(chips)) % chips
    earlier = (whose[None, :] < whose[:, None]).astype(f32)
    offset = jnp.sum(earlier[:, :, None] * member.sum(axis=1)[None], axis=1)
    step = jnp.arange(tokens)
    below = (step[:, None] > step[None, :]).astype(f32)
    rank = jnp.einsum("ts,gse->gte", below, member) + offset[:, None, :]
    rank = jnp.where(member > 0, rank, -1.0).astype(jnp.int32)
    rank = rank.reshape(chips * tokens, experts)
    gates = gates.reshape(chips * tokens, experts)
    rank_lanes = rank.T

    most = chips * rollouts * (positions // 2 + 1)
    small = max(16, most // 2 // 16 * 16)
    chunks = [(0, small), (small, most - small)]
    def dispatch(groups, first, count, needs=()):
        padded = -(-count // 8) * 8
        return ordered(pick_rows, groups, rank_lanes, first, count, padded, needs=needs)

    def behind(v, *others):
        return lax.optimization_barrier((v, *others))[0] if others else v

    def relay(mine):
        return [place.turn_slice(mine, k) for k in range(1, slices)]

    def partial(arrays, count, mats, scale, needs=()):
        arrays = [behind(v, *needs) for v in arrays]
        keep, send = ordered(project, [(arrays, mats)], count, chip_here, chips)
        ready = (send * scale).astype(jnp.float16)
        arrived = [place.turn_chip(ready[p - 1], p) for p in range(1, chips)]
        return keep, arrived, scale

    def settle(part):
        keep, arrived, scale = part
        return keep + sum(v.astype(f32) for v in arrived) * (1.0 / scale)

    def ring(v):
        found = [v] + [None] * (chips - 1)
        for p in range(1, chips):
            found[chips - p] = place.turn_chip(v, p)
        return found

    def middle(inner, outer):
        pre_gate, pre_up = settle(inner)
        unit_grad = settle(outer)[0]
        sigmoid_gate = jax.nn.sigmoid(pre_gate)
        activated = pre_gate * sigmoid_gate
        units = activated * pre_up
        score = jnp.sum(units * unit_grad, axis=-1).astype(bf16)
        slope = pre_up * sigmoid_gate * (1.0 + pre_gate * (1.0 - sigmoid_gate))
        which = jnp.arange(2).reshape(2, 1, 1)
        both = (unit_grad * jnp.where(which == 0, slope, activated)).astype(bf16)
        return ring(both), score

    def back(groups, halves, count, needs=()):
        mats = [(pairs[0][h], pairs[1][h]) for h in halves]
        return ordered(project_back, groups, mats, chip_here, count, needs=needs)

    def to_slices(dx):
        return [
            place.turn_slice(dx[(k - 1) * experts : k * experts], -k) for k in range(1, slices)
        ]

    (first_a, count_a), (first_b, count_b) = chunks

    block = queries.shape[1]
    def held(part, kernel_result):
        keep, arrived, scale = part
        return keep, [behind(v, kernel_result) for v in arrived], scale

    summary = ordered(key_value_state, key_rows, value_rows, decay_rate)
    state_before = carried(place, summary, decay_rate, block, 1)
    picked_hidden_a = dispatch(hidden_groups, first_a, count_a)
    picked_hidden_b = dispatch(hidden_groups, first_b, count_b)
    picked_grads_a = dispatch(grad_groups, first_a, count_a, [state_before])
    hidden_a = place.between_experts(behind(picked_hidden_a, picked_grads_a))
    picked_grads_b = dispatch(
        grad_groups, first_b, count_b, [pairs[0][1], pairs[1][1]]
    )
    grad_queries, local_k, local_v, summary = ordered(
        local_grads,
        queries,
        key_rows,
        value_rows,
        attn_probe,
        norm_gain.reshape(1, -1),
        coeff.T,
        decay_rate,
        state_before,
    )
    state_after = carried(place, summary, decay_rate, block, -1)
    far_hidden_a = relay(hidden_a)
    pairs.append((own_mats[2], place.swap_core(behind(own_mats[2], picked_grads_b))))
    inner_own_a = partial([hidden_a], count_a, pairs[:2], in_scale, [state_after])
    grads_a = place.between_experts(behind(picked_grads_a, hidden_a))
    far_grads_a = relay(grads_a)
    outer_own_a = partial([grads_a], count_a, pairs[2:], out_scale)
    grad_keys, grad_values = ordered(
        later_grads, key_rows, value_rows, local_k, local_v, decay_rate, state_after
    )
    hidden_b = place.between_experts(behind(picked_hidden_b, grads_a, inner_own_a[0]))
    own_a, score_own_a = middle(inner_own_a, outer_own_a)
    inner_far_a = partial(far_hidden_a, count_a, pairs[:2], in_scale, own_a[:1])
    outer_far_a = partial(far_grads_a, count_a, pairs[2:], out_scale, own_a[1:])
    far_hidden_b = relay(behind(hidden_b, outer_far_a[0]))
    grads_b = place.between_experts(behind(picked_grads_b, hidden_b, outer_far_a[0]))
    inner_own_b = partial([hidden_b], count_b, pairs[:2], in_scale, inner_far_a[1])
    far_grads_b = relay(grads_b)
    far_a, score_far_a = middle(
        held(inner_far_a, inner_own_b[0]), held(outer_far_a, inner_own_b[0])
    )
    inner_far_b = partial(far_hidden_b, count_b, pairs[:2], in_scale, far_a[:1])
    outer_own_b = partial([grads_b], count_b, pairs[2:], out_scale)
    dx_own_a, dx_far_a = back([own_a, far_a], (0, 1), count_a)
    outer_far_b = partial(far_grads_b, count_b, pairs[2:], out_scale, inner_own_b[1])
    far_b, score_far_b = middle(inner_far_b, outer_far_b)
    own_b, score_own_b = middle(held(inner_own_b, far_b[0]), held(outer_own_b, far_b[0]))
    from_far_a = to_slices(dx_far_a)
    total_a = dx_own_a.astype(f32) + sum(
        behind(v, own_b[1]).astype(f32) for v in from_far_a
    )
    home_a = place.between_experts(total_a.astype(bf16))
    from_far_b = [to_slices(back([far_b], (h,), count_b)[0]) for h in range(2)]
    (dx_own_b,) = back([own_b], (0, 1), count_b)
    total_b = dx_own_b.astype(f32) + sum(
        behind(jnp.concatenate(halves, axis=1), home_a).astype(f32) for halves in zip(*from_far_b)
    )
    home_b = place.between_experts(total_b.astype(bf16))

    kinds = [score_own_a, score_far_a, score_own_b, score_far_b]
    sizes = [v.shape[0] for v in kinds]
    every = jnp.stack(ring(behind(jnp.concatenate(kinds), *far_b)))
    every = jnp.take(every, (jnp.arange(chips) - place.chip) % chips, axis=0)
    split, at = [], 0
    for size in sizes:
        split.append(every[:, at : at + size].reshape(chips * size))
        at += size
    near = [
        v.reshape(experts, count) for v, count in ((split[0], count_a), (split[2], count_b))
    ]
    beyond = [
        v.reshape(slices - 1, experts, count)
        for v, count in ((split[1], count_a), (split[3], count_b))
    ]
    score_rows = jnp.concatenate(near, axis=1).astype(f32)
    beyond = jnp.concatenate(beyond, axis=2)
    for k in range(1, slices):
        score_rows = score_rows + place.turn_slice(beyond[k - 1], -k).astype(f32)
    turned = [score_rows] + [place.turn_expert(score_rows, d) for d in range(1, experts)]
    turned = lax.dynamic_index_in_dim(jnp.stack(turned), place.expert, 1, keepdims=False)
    source = (place.expert - jnp.arange(experts)) % experts
    score_home = jnp.take(turned, source, axis=0)

    router_rows = halves_of(router_weight.T.astype(f32), 0)
    result = jnp.zeros((tokens, model_width), bf16)
    for h in range(2):
        groups = combine(
            [(home_a, h), (home_b, h)],
            score_home,
            rank,
            gates,
            router_rows[h],
            [first_a, first_b],
            chips,
        )
        core = place.core if h == 0 else 1 - place.core
        for g in range(chips):
            part = groups[g] if g == 0 else place.turn_chip(groups[g], -g)
            chip = (place.chip + g) % chips
            result = lax.dynamic_update_slice_in_dim(result, part, (2 * chip + core) * width, 1)
    grad_hidden = result.reshape(rollouts, positions, model_width)
    return grad_queries, grad_keys, grad_values, grad_hidden


def on_device(
    queries,
    key_rows,
    value_rows,
    decay_rate,
    norm_gain,
    attn_probe,
    hidden_in,
    moe_probe,
    router_weight,
    routes,
    gate_weight,
    up_weight,
    down_weight,
    rollout_logprob,
    trainer_logprob,
    advantage,
    clip_low,
    clip_high,
):
    place = Layout(router_weight.shape[1])
    importance = jnp.exp(trainer_logprob - rollout_logprob)
    clipped = jnp.minimum(jnp.maximum(importance, clip_low[0]), clip_high[0])
    coeff = -(clipped * advantage) / queries.shape[0]
    objective = coeff * trainer_logprob
    grads = expert_and_attention(
        place,
        hidden_in,
        moe_probe,
        router_weight,
        routes,
        gate_weight,
        up_weight,
        down_weight,
        coeff,
        queries,
        key_rows,
        value_rows,
        decay_rate,
        norm_gain,
        attn_probe,
    )
    return (objective, *grads)


def solution(mesh):
    in_specs = (
        P(None, "seq", "expert"),
        P(None, "seq", "expert"),
        P(None, "seq", "expert"),
        P("expert"),
        P("expert"),
        P(None, "seq", "expert"),
        P(None, ("seq", "expert"), None),
        P(None, ("seq", "expert"), None),
        P(),
        P(None, ("seq", "expert"), None),
        P("expert", "seq", None),
        P("expert", "seq", None),
        P("expert", "seq", None),
        P(None, "seq"),
        P(None, "seq"),
        P(None, "seq"),
        P(),
        P(),
    )
    out_specs = (
        P(None, "seq"),
        P(None, "seq", "expert"),
        P(None, "seq", "expert"),
        P(None, "seq", "expert"),
        P(None, ("seq", "expert"), None),
    )
    return jax.shard_map(
        on_device, mesh=mesh, in_specs=in_specs, out_specs=out_specs, check_vma=False
    )
```

```python
import jax
import jax.numpy as jnp
from jax import lax
from jax.experimental import pallas as pl
from jax.experimental.pallas import tpu as pltpu
from jax.sharding import PartitionSpec as P

highest = lax.Precision.HIGHEST
norm_epsilon = 1e-06
f32 = jnp.float32
bf16 = jnp.bfloat16
vmem_limit = 48 * 2**20

in_scale = 32.0
out_scale = 4.0


class Layout:
    def __init__(self, window_experts):
        self.seq = lax.axis_size("seq")
        self.chips = self.seq // 2
        self.spread = lax.axis_size("expert")
        self.experts = window_experts
        self.slices = self.spread // window_experts
        here = lax.axis_index("seq")
        self.chip, self.core = here // 2, here % 2
        self.expert = lax.axis_index("expert") // self.slices

    def swap_core(self, v):
        return lax.ppermute(v, "seq", [(i, i ^ 1) for i in range(self.seq)])

    def turn_chip(self, v, p):
        n = self.chips
        return lax.ppermute(
            v, "seq", [(i, ((i // 2 + p) % n) * 2 + i % 2) for i in range(self.seq)]
        )

    def later_chip(self, v, p):
        pairs = [(i, i + 2 * p) for i in range(self.seq) if 0 <= i + 2 * p < self.seq]
        return lax.ppermute(v, "seq", pairs)

    def between_experts(self, v):
        n, m = self.experts, self.slices
        groups = [[q * m + j for q in range(n)] for j in range(m)]
        return lax.all_to_all(v, "expert", 0, 0, axis_index_groups=groups, tiled=True)

    def turn_expert(self, v, d):
        n, m = self.experts, self.slices
        return lax.ppermute(
            v, "expert", [(i, ((i // m + d) % n) * m + i % m) for i in range(self.spread)]
        )

    def turn_slice(self, v, k):
        m = self.slices
        return lax.ppermute(
            v, "expert", [(i, (i // m) * m + (i % m + k) % m) for i in range(self.spread)]
        )


def params(**kw):
    return pltpu.CompilerParams(vmem_limit_bytes=vmem_limit, **kw)


short = pl.CostEstimate(flops=1000, bytes_accessed=1000, transcendentals=0)


def tile_of(size):
    return 768 if size % 768 == 0 else size


def any_spec():
    return pl.BlockSpec(memory_space=pl.ANY)


def pick_rows(groups, rank, first, count, padded, after):
    experts = rank.shape[0]
    halves, tokens, width = groups[0].shape
    total = tokens * len(groups)

    def body(rank_ref, *refs):
        group_refs, out_ref = refs[: len(groups)], refs[-1]
        slot = lax.broadcasted_iota(jnp.int32, (padded, total), 0)
        wanted = jnp.where(slot < count, slot + first, -2)
        for h in range(halves):
            rows = jnp.concatenate([g[h] for g in group_refs], axis=0)
            for d in range(experts):
                pick = (rank_ref[d : d + 1, :] == wanted).astype(bf16)
                out_ref[d, h] = jnp.dot(pick, rows, preferred_element_type=f32).astype(bf16)

    vmem = pl.BlockSpec(memory_space=pltpu.VMEM)
    return pl.pallas_call(
        body,
        in_specs=[vmem] * (1 + len(groups)) + [any_spec()] * len(after),
        out_specs=vmem,
        out_shape=jax.ShapeDtypeStruct((experts, halves, padded, width), bf16),
        compiler_params=params(),
        cost_estimate=short,
        name="pick_rows",
    )(rank, *groups, *after)


def project(jobs, rows, chip, chips, after):
    experts, halves, padded, width = jobs[0][0][0].shape
    arrays_each = len(jobs[0][0])
    count = arrays_each * experts
    part = rows * count // chips
    per_part = count // chips
    units = jobs[0][1][0][0].shape[1]
    tile = tile_of(units)
    arrays = [v for job in jobs for v in job[0]]
    mats = [half for job in jobs for pair in job[1] for half in pair]
    owner = [j for j, job in enumerate(jobs) for _ in job[1]]
    mat_count = len(owner)

    def body(chip_ref, *refs):
        array_refs = refs[: len(arrays)]
        mat_refs = refs[len(arrays) : len(arrays) + len(mats)]
        keep_ref, send_ref, held = refs[-3:]

        def left(job, h):
            found = [
                r[:, h].reshape(experts * padded, width)
                for r in array_refs[job * arrays_each : (job + 1) * arrays_each]
            ]
            return found[0] if len(found) == 1 else jnp.concatenate(found, axis=0)

        for m in range(mat_count):
            result = jnp.dot(
                left(owner[m], 0), mat_refs[2 * m][...], preferred_element_type=f32
            )
            result = result + jnp.dot(
                left(owner[m], 1), mat_refs[2 * m + 1][...], preferred_element_type=f32
            )
            held[...] = result.reshape(chips, per_part * padded, tile)
            for p in range(chips):
                value = held[(chip_ref[0] + p) % chips]
                for b in range(per_part):
                    piece = value[b * padded : b * padded + rows]
                    if p == 0:
                        keep_ref[m, b * rows : (b + 1) * rows] = piece
                    else:
                        send_ref[p - 1, m, b * rows : (b + 1) * rows] = piece

    mat_spec = pl.BlockSpec((width, tile), lambda i: (0, i))
    return pl.pallas_call(
        body,
        grid=(units // tile,),
        in_specs=[pl.BlockSpec(memory_space=pltpu.SMEM)]
        + [pl.BlockSpec(arrays[0].shape, lambda i: (0, 0, 0, 0))] * len(arrays)
        + [mat_spec] * len(mats)
        + [any_spec()] * len(after),
        out_specs=[
            pl.BlockSpec((mat_count, part, tile), lambda i: (0, 0, i)),
            pl.BlockSpec((chips - 1, mat_count, part, tile), lambda i: (0, 0, 0, i)),
        ],
        out_shape=[
            jax.ShapeDtypeStruct((mat_count, part, units), f32),
            jax.ShapeDtypeStruct((chips - 1, mat_count, part, units), f32),
        ],
        scratch_shapes=[pltpu.VMEM((chips, per_part * padded, tile), f32)],
        compiler_params=params(),
        cost_estimate=short,
        name="project",
    )(chip, *arrays, *mats, *after)


def project_back(groups, mats, chip, rows, after):
    chips = len(groups[0])
    units = groups[0][0].shape[2]
    width = mats[0][0].shape[0]
    halves = len(mats)
    tile = tile_of(width)
    steps = width // tile
    parts = [v for group in groups for v in group]
    sizes = [group[0].shape[1] for group in groups]
    rooms = [-(-size // 16) * 16 for size in sizes]
    bases = [chips * sum(rooms[:g]) for g in range(len(groups))]
    total = chips * sum(rooms)
    counts = [size * chips // rows for size in sizes]

    def body(chip_ref, *refs):
        part_refs = refs[: len(parts)]
        mat_refs = refs[len(parts) : len(parts) + 2 * halves]
        out_refs = refs[-2 - len(groups) : -2]
        gate_all, up_all = refs[-2:]
        step = pl.program_id(0)

        @pl.when(step == 0)
        def _():
            for g, size in enumerate(sizes):
                for r in range(chips):
                    place = (chip_ref[0] + r) % chips
                    start = pl.multiple_of(bases[g] + place * rooms[g], 16)
                    gate_all[pl.ds(start, size)] = part_refs[g * chips + r][0]
                    up_all[pl.ds(start, size)] = part_refs[g * chips + r][1]

        def multiply(gate_mat_ref, up_mat_ref):
            contract = (((1,), (1,)), ((), ()))
            result = lax.dot_general(
                gate_all[...], gate_mat_ref[...], contract, preferred_element_type=f32
            )
            result = result + lax.dot_general(
                up_all[...], up_mat_ref[...], contract, preferred_element_type=f32
            )
            for g, count in enumerate(counts):
                per_part = count // chips
                for b in range(count):
                    start = bases[g] + b // per_part * rooms[g] + b % per_part * rows
                    out_refs[g][b, 0] = result[start : start + rows].astype(bf16)

        if halves == 1:
            multiply(*mat_refs)
        else:
            for h in range(halves):

                @pl.when(step // steps == h)
                def _():
                    multiply(mat_refs[2 * h], mat_refs[2 * h + 1])

    def mat_spec(h):
        return pl.BlockSpec((tile, units), lambda i: (jnp.clip(i - h * steps, 0, steps - 1), 0))

    def row_spec(count):
        return pl.BlockSpec((count, 1, rows, tile), lambda i: (0, i // steps, 0, i % steps))

    return pl.pallas_call(
        body,
        grid=(halves * steps,),
        in_specs=[pl.BlockSpec(memory_space=pltpu.SMEM)]
        + [pl.BlockSpec(v.shape, lambda i: (0, 0, 0)) for v in parts]
        + [mat_spec(h) for h in range(halves) for _ in range(2)]
        + [any_spec()] * len(after),
        out_specs=[row_spec(count) for count in counts],
        out_shape=[
            jax.ShapeDtypeStruct((count, halves, rows, width), bf16) for count in counts
        ],
        scratch_shapes=[pltpu.VMEM((total, units), bf16)] * 2,
        compiler_params=params(),
        cost_estimate=short,
        name="project_back",
    )(chip, *parts, *[m for pair in mats for m in pair], *after)


def combine(returned, scores, rank, gates, router, firsts, groups):
    experts, _, _, width = returned[0][0].shape
    counts = [v.shape[2] for v, _ in returned]
    total = rank.shape[0]
    tokens = total // groups

    def body(*refs):
        returned_refs = refs[: len(returned)]
        score_ref, rank_ref, gate_ref, router_ref = refs[len(returned) : len(returned) + 4]
        out_refs = refs[len(returned) + 4 :]
        acc = jnp.zeros((total, width), f32)
        picked = []
        slots = lax.broadcasted_iota(jnp.int32, (total, score_ref.shape[1]), 1)
        for d in range(experts):
            hit = rank_ref[:, d : d + 1] == slots
            picked.append(
                jnp.sum(jnp.where(hit, score_ref[d : d + 1, :], 0.0), axis=1, keepdims=True)
            )
        mean = sum(gate_ref[:, d : d + 1] * picked[d] for d in range(experts))
        for d in range(experts):
            grad = gate_ref[:, d : d + 1] * (picked[d] - mean)
            acc = acc + grad * router_ref[d : d + 1, :]
        for c, rows_ref in enumerate(returned_refs):
            for d in range(experts):
                value = rows_ref[d, 0]
                slot = lax.broadcasted_iota(jnp.int32, (total, value.shape[0]), 1) + firsts[c]
                weight = jnp.where(rank_ref[:, d : d + 1] == slot, gate_ref[:, d : d + 1], 0.0)
                high = weight.astype(bf16)
                low = (weight - high.astype(f32)).astype(bf16)
                acc = acc + jnp.dot(high, value, preferred_element_type=f32)
                acc = acc + jnp.dot(low, value, preferred_element_type=f32)
        for g in range(groups):
            out_refs[g][...] = acc[g * tokens : (g + 1) * tokens].astype(bf16)

    row_count = experts * sum(counts)

    def half_spec(count, h):
        return pl.BlockSpec((experts, 1, count, width), lambda i: (0, h, 0, 0))

    def whole_spec(v):
        return pl.BlockSpec(v.shape, lambda i: (0, 0))

    return pl.pallas_call(
        body,
        grid=(1,),
        in_specs=[half_spec(v.shape[2], h) for v, h in returned]
        + [whole_spec(v) for v in (scores, rank, gates, router)],
        out_specs=[pl.BlockSpec((tokens, width), lambda i: (0, 0))] * groups,
        out_shape=[jax.ShapeDtypeStruct((tokens, width), bf16)] * groups,
        compiler_params=params(),
        cost_estimate=short,
        name="combine",
    )(*[v for v, _ in returned], scores, rank, gates, router)


def split3(v):
    high = v.astype(bf16)
    rest = v - high.astype(f32)
    middle = rest.astype(bf16)
    return high, middle, (rest - middle.astype(f32)).astype(bf16)


def dot_left(a, b, dims):
    contract = (((dims[0],), (dims[1],)), ((), ()))
    return sum(lax.dot_general(t, b, contract, preferred_element_type=f32) for t in split3(a))


def dot_right(a, b, dims):
    contract = (((dims[0],), (dims[1],)), ((), ()))
    return sum(lax.dot_general(a, t, contract, preferred_element_type=f32) for t in split3(b))


def dot_full(a, b, dims):
    contract = (((dims[0],), (dims[1],)), ((), ()))
    return lax.dot_general(a, b, contract, precision=highest, preferred_element_type=f32)


def head_specs(rollouts, block, head):
    rows = pl.BlockSpec((rollouts, block, head), lambda h: (0, 0, h))
    state = pl.BlockSpec((rollouts, 1, head, head), lambda h: (0, h, 0, 0))
    return pl.BlockSpec(memory_space=pltpu.SMEM), rows, state


def key_value_state(key_rows, value_rows, decay_rate, after):
    rollouts, block, width = key_rows.shape
    heads = decay_rate.shape[0]
    head = width // heads
    smem, rows, state = head_specs(rollouts, block, head)

    def body(rate_ref, key_ref, value_ref, *refs):
        rate = rate_ref[pl.program_id(0)]
        offset = lax.broadcasted_iota(jnp.int32, (block, 1), 0).astype(f32)
        tail = jnp.exp(-rate * (block - 1.0 - offset))
        for r in range(rollouts):
            decayed = key_ref[r].astype(f32) * tail
            refs[-1][r, 0] = dot_left(decayed, value_ref[r], (0, 0))

    return pl.pallas_call(
        body,
        grid=(heads,),
        in_specs=[smem, rows, rows] + [any_spec()] * len(after),
        out_specs=state,
        out_shape=jax.ShapeDtypeStruct((rollouts, heads, head, head), f32),
        compiler_params=params(),
        cost_estimate=short,
        name="key_value_state",
    )(decay_rate, key_rows, value_rows, *after)


def local_grads(
    queries, key_rows, value_rows, attn_probe, gain, coeff, decay_rate, state, after
):
    rollouts, block, width = queries.shape
    heads = decay_rate.shape[0]
    head = width // heads
    smem, rows, state_spec = head_specs(rollouts, block, head)

    def body(rate_ref, q_ref, k_ref, v_ref, probe_ref, gain_ref, coeff_ref, state_ref, *refs):
        grad_q_ref, grad_k_ref, grad_v_ref, summary_ref = refs[-4:]
        rate = rate_ref[pl.program_id(0)]
        offset = lax.broadcasted_iota(jnp.int32, (block, 1), 0).astype(f32)
        lead = jnp.exp(-rate * (offset + 1.0))
        tail = jnp.exp(-rate * offset)
        line = lax.broadcasted_iota(jnp.int32, (block, block), 0)
        column = lax.broadcasted_iota(jnp.int32, (block, block), 1)
        distance = (line - column).astype(f32)
        within = jnp.where(line >= column, jnp.exp(-rate * jnp.maximum(distance, 0.0)), 0.0)
        for r in range(rollouts):
            query, key, value, before = q_ref[r], k_ref[r], v_ref[r], state_ref[r, 0]
            scores = lax.dot_general(
                query, key, (((1,), (1,)), ((), ())), preferred_element_type=f32
            )
            scores = scores * within
            output = dot_left(scores, value, (1, 0))
            output = output + lead * dot_right(query, before, (1, 0))
            inverse = lax.rsqrt(
                jnp.mean(output * output, axis=-1, keepdims=True) + norm_epsilon
            )
            scaled = gain_ref[...] * (coeff_ref[:, r : r + 1] * probe_ref[r].astype(f32))
            grad_out = inverse * scaled - output * inverse**3 * jnp.mean(
                scaled * output, axis=-1, keepdims=True
            )
            summary_ref[r, 0] = dot_right(query, tail * grad_out, (0, 0))
            product = dot_left(grad_out, value, (1, 1)) * within
            grad_q = dot_left(product, key, (1, 0))
            grad_q = grad_q + lead * dot_full(grad_out, before, (1, 1))
            grad_q_ref[r] = grad_q.astype(bf16)
            grad_k_ref[r] = dot_left(product, query, (0, 0))
            grad_v_ref[r] = dot_full(scores, grad_out, (0, 0))

    return pl.pallas_call(
        body,
        grid=(heads,),
        in_specs=[
            smem,
            rows,
            rows,
            rows,
            rows,
            pl.BlockSpec((1, head), lambda h: (0, h)),
            pl.BlockSpec((block, rollouts), lambda h: (0, 0)),
            state_spec,
        ]
        + [any_spec()] * len(after),
        out_specs=[rows, rows, rows, state_spec],
        out_shape=[
            jax.ShapeDtypeStruct(queries.shape, bf16),
            jax.ShapeDtypeStruct(queries.shape, f32),
            jax.ShapeDtypeStruct(queries.shape, f32),
            jax.ShapeDtypeStruct(state.shape, f32),
        ],
        compiler_params=params(),
        cost_estimate=short,
        name="local_grads",
    )(decay_rate, queries, key_rows, value_rows, attn_probe, gain, coeff, state, *after)


def later_grads(key_rows, value_rows, grad_k, grad_v, decay_rate, state, after):
    rollouts, block, width = key_rows.shape
    heads = decay_rate.shape[0]
    head = width // heads
    smem, rows, state_spec = head_specs(rollouts, block, head)

    def body(rate_ref, k_ref, v_ref, grad_k_ref, grad_v_ref, state_ref, *refs):
        out_k_ref, out_v_ref = refs[-2:]
        rate = rate_ref[pl.program_id(0)]
        offset = lax.broadcasted_iota(jnp.int32, (block, 1), 0).astype(f32)
        tail = jnp.exp(-rate * (block - offset))
        for r in range(rollouts):
            after_state = state_ref[r, 0]
            grad_k = grad_k_ref[r] + tail * dot_right(v_ref[r], after_state, (1, 1))
            grad_v = grad_v_ref[r] + tail * dot_right(k_ref[r], after_state, (1, 0))
            out_k_ref[r] = grad_k.astype(bf16)
            out_v_ref[r] = grad_v.astype(bf16)

    return pl.pallas_call(
        body,
        grid=(heads,),
        in_specs=[smem, rows, rows, rows, rows, state_spec] + [any_spec()] * len(after),
        out_specs=[rows, rows],
        out_shape=[jax.ShapeDtypeStruct(key_rows.shape, bf16)] * 2,
        compiler_params=params(),
        cost_estimate=short,
        name="later_grads",
    )(decay_rate, key_rows, value_rows, grad_k, grad_v, state, *after)


def carried(place, summary, decay_rate, block_size, direction, hold=None):
    def block_decay(blocks):
        return jnp.exp(-decay_rate * (block_size * blocks)).reshape(1, -1, 1, 1)

    found = [place.later_chip(summary, direction * p) for p in range(1, place.chips)]
    if hold is not None:
        hold.extend(found)
    mine = jnp.stack([summary, *found])
    partner = place.swap_core(mine)
    first = (place.core == 0) if direction > 0 else (place.core == 1)
    one = block_decay(1)
    near = jnp.where(first, partner + one * mine, mine + one * partner)
    outside = sum(block_decay(2 * (p - 1)) * near[p] for p in range(1, place.chips))
    return jnp.where(first, outside, partner[0] + one * outside)


def cut_features(v, scale, chip_core, chips, after):
    tokens, model_width = v.shape
    width = model_width // (2 * chips)

    def body(where_ref, v_ref, *refs):
        keep_ref, send_ref = refs[-2:]
        for p in range(chips):
            chip = (where_ref[0] + p) % chips
            for h in range(2):
                core = where_ref[1] if h == 0 else 1 - where_ref[1]
                start = pl.multiple_of((2 * chip + core) * width, 128)
                value = v_ref[:, pl.ds(start, width)]
                if scale is not None:
                    value = (refs[0][...] * value.astype(f32)).astype(bf16)
                if p == 0:
                    keep_ref[h] = value
                else:
                    send_ref[p - 1, h] = value

    vmem = pl.BlockSpec(memory_space=pltpu.VMEM)
    extra = [] if scale is None else [scale]
    return pl.pallas_call(
        body,
        in_specs=[pl.BlockSpec(memory_space=pltpu.SMEM), vmem]
        + [vmem] * len(extra)
        + [any_spec()] * len(after),
        out_specs=[vmem, vmem],
        out_shape=[
            jax.ShapeDtypeStruct((2, tokens, width), bf16),
            jax.ShapeDtypeStruct((chips - 1, 2, tokens, width), bf16),
        ],
        compiler_params=params(),
        cost_estimate=short,
        name="cut_features",
    )(chip_core, v, *extra, *after)


def expert_and_attention(
    place,
    hidden_in,
    moe_probe,
    router_weight,
    routes,
    gate_weight,
    up_weight,
    down_weight,
    coeff,
    queries,
    key_rows,
    value_rows,
    decay_rate,
    norm_gain,
    attn_probe,
):
    rollouts, positions, model_width = hidden_in.shape
    chips, experts, slices = place.chips, place.experts, place.slices
    tokens = rollouts * positions
    width = gate_weight.shape[1]
    own_mats = (gate_weight[0], up_weight[0], down_weight[0])

    hidden = hidden_in.reshape(tokens, model_width)
    local_coeff = lax.dynamic_slice_in_dim(
        coeff, lax.axis_index("expert") * positions, positions, 1
    )
    chip_here = place.chip.reshape(1).astype(jnp.int32)
    chip_core = jnp.stack([place.chip, place.core]).astype(jnp.int32)
    last = []

    def ordered(kernel, *args, needs=()):
        result = kernel(*args, (*last, *needs))
        last[:] = [result[0] if isinstance(result, (list, tuple)) else result]
        return result

    def across(v, scale):
        keep, send = ordered(cut_features, v, scale, chip_core, chips)
        return [keep] + [place.turn_chip(send[p - 1], p) for p in range(1, chips)]

    hidden_groups = across(hidden, None)
    grad_groups = across(
        moe_probe.reshape(tokens, model_width), local_coeff.reshape(tokens, 1)
    )

    def halves_of(v, p):
        chip = (place.chip + p) % chips
        return jnp.stack(
            [
                lax.dynamic_slice_in_dim(v, (2 * chip + core) * width, width, 1)
                for core in (place.core, 1 - place.core)
            ]
        )

    logits = jnp.dot(hidden, router_weight, preferred_element_type=f32)
    flat_routes = routes.reshape(tokens, -1)
    onehot = (flat_routes[:, :, None] == jnp.arange(experts, dtype=jnp.int32)).astype(f32)
    chosen = jnp.sum(onehot * logits[:, None, :], axis=-1)
    exponent = jnp.exp(chosen)
    gate = exponent / jnp.sum(exponent, axis=-1, keepdims=True)
    facts = jnp.concatenate(
        [onehot.sum(axis=1), jnp.sum(onehot * gate[:, :, None], axis=1)], axis=1
    )
    all_facts = [facts] + [place.turn_chip(facts, p) for p in range(1, chips)]

    pairs = [(m, place.swap_core(m)) for m in own_mats[:2]]

    fact_stack = jnp.stack(all_facts)
    member, gates = fact_stack[:, :, :experts], fact_stack[:, :, experts:]
    whose = (place.chip - jnp.arange(chips)) % chips
    earlier = (whose[None, :] < whose[:, None]).astype(f32)
    offset = jnp.sum(earlier[:, :, None] * member.sum(axis=1)[None], axis=1)
    step = jnp.arange(tokens)
    below = (step[:, None] > step[None, :]).astype(f32)
    rank = jnp.einsum("ts,gse->gte", below, member) + offset[:, None, :]
    rank = jnp.where(member > 0, rank, -1.0).astype(jnp.int32)
    rank = rank.reshape(chips * tokens, experts)
    gates = gates.reshape(chips * tokens, experts)
    rank_lanes = rank.T

    most = chips * rollouts * (positions // 2 + 1)
    small = max(16, most // 2 // 16 * 16)
    chunks = [(0, small), (small, most - small)]
    def dispatch(groups, first, count, needs=()):
        padded = -(-count // 8) * 8
        return ordered(pick_rows, groups, rank_lanes, first, count, padded, needs=needs)

    def behind(v, *others):
        return lax.optimization_barrier((v, *others))[0] if others else v

    def relay(mine):
        return [place.turn_slice(mine, k) for k in range(1, slices)]

    def partial(jobs, count, needs=()):
        scales = jnp.asarray([scale for _, mats, scale in jobs for _ in mats], f32)
        scales = scales.reshape(-1, 1, 1)
        ready = [([behind(v, *needs) for v in arrays], mats) for arrays, mats, _ in jobs]
        keep, send = ordered(project, ready, count, chip_here, chips)
        send = (send * scales).astype(jnp.float16)
        arrived = [place.turn_chip(send[p - 1], p) for p in range(1, chips)]
        return keep, arrived, scales

    def settle(part):
        keep, arrived, scale = part
        return keep + sum(v.astype(f32) for v in arrived) / scale

    def ring(v):
        found = [v] + [None] * (chips - 1)
        for p in range(1, chips):
            found[chips - p] = place.turn_chip(v, p)
        return found

    def middle(*some):
        pre_gate, pre_up, unit_grad = jnp.concatenate([settle(v) for v in some])
        sigmoid_gate = jax.nn.sigmoid(pre_gate)
        activated = pre_gate * sigmoid_gate
        units = activated * pre_up
        score = jnp.sum(units * unit_grad, axis=-1).astype(bf16)
        slope = pre_up * sigmoid_gate * (1.0 + pre_gate * (1.0 - sigmoid_gate))
        which = jnp.arange(2).reshape(2, 1, 1)
        both = (unit_grad * jnp.where(which == 0, slope, activated)).astype(bf16)
        return ring(both), score

    def back(groups, halves, count, needs=()):
        mats = [(pairs[0][h], pairs[1][h]) for h in halves]
        return ordered(project_back, groups, mats, chip_here, count, needs=needs)

    def to_slices(dx):
        return [
            place.turn_slice(dx[(k - 1) * experts : k * experts], -k) for k in range(1, slices)
        ]

    (first_a, count_a), (first_b, count_b) = chunks

    block = queries.shape[1]
    def held(part, kernel_result):
        keep, arrived, scale = part
        return keep, [behind(v, kernel_result) for v in arrived], scale

    summary = ordered(key_value_state, key_rows, value_rows, decay_rate)
    early = []
    state_before = carried(place, summary, decay_rate, block, 1, early)
    picked_hidden_a = dispatch(hidden_groups, first_a, count_a)
    picked_hidden_b = dispatch(hidden_groups, first_b, count_b)
    picked_grads_a = dispatch(grad_groups, first_a, count_a, early)
    hidden_a = place.between_experts(behind(picked_hidden_a, picked_grads_a))
    picked_grads_b = dispatch(grad_groups, first_b, count_b, [pairs[0][1], pairs[1][1]])
    far_hidden_a = relay(hidden_a)
    pairs.append((own_mats[2], place.swap_core(behind(own_mats[2], picked_grads_b))))
    inner_own_a = partial([([hidden_a], pairs[:2], in_scale)], count_a)
    grad_queries, local_k, local_v, summary = ordered(
        local_grads,
        queries,
        key_rows,
        value_rows,
        attn_probe,
        norm_gain.reshape(1, -1),
        coeff.T,
        decay_rate,
        behind(state_before, inner_own_a[0]),
    )
    grads_a = place.between_experts(behind(picked_grads_a, hidden_a))
    far_grads_a = relay(behind(grads_a, summary))
    outer_own_a = partial([([grads_a], pairs[2:], out_scale)], count_a)
    hidden_b = place.between_experts(behind(picked_hidden_b, grads_a, summary))
    own_a, score_own_a = middle(inner_own_a, outer_own_a)
    whole_far_a = partial(
        [(far_hidden_a, pairs[:2], in_scale), (far_grads_a, pairs[2:], out_scale)],
        count_a,
        own_a[:1],
    )
    far_hidden_b = relay(behind(hidden_b, whole_far_a[0]))
    grads_b = place.between_experts(behind(picked_grads_b, hidden_b, whole_far_a[0]))
    inner_own_b = partial([([hidden_b], pairs[:2], in_scale)], count_b, own_a[1:])
    far_grads_b = relay(grads_b)
    far_a, score_far_a = middle(whole_far_a)
    state_after = carried(place, behind(summary, whole_far_a[0]), decay_rate, block, -1)
    inner_far_b = partial([(far_hidden_b, pairs[:2], in_scale)], count_b, far_a[:1])
    outer_own_b = partial([([grads_b], pairs[2:], out_scale)], count_b)
    dx_own_a, dx_far_a = back([own_a, far_a], (0, 1), count_a)
    outer_far_b = partial([(far_grads_b, pairs[2:], out_scale)], count_b, inner_own_b[1])
    grad_keys, grad_values = ordered(
        later_grads, key_rows, value_rows, local_k, local_v, decay_rate, state_after
    )
    far_b, score_far_b = middle(inner_far_b, outer_far_b)
    own_b, score_own_b = middle(held(inner_own_b, far_b[0]), held(outer_own_b, far_b[0]))
    from_far_a = to_slices(dx_far_a)
    total_a = dx_own_a.astype(f32) + sum(
        behind(v, grad_keys).astype(f32) for v in from_far_a
    )
    total_a = total_a.astype(bf16)
    home_a = place.between_experts(total_a)
    total_b = []
    for h in range(2):
        dx_own_b, dx_far_b = back([own_b, far_b], (h,), count_b, [total_a])
        found = sum(v.astype(f32) for v in to_slices(dx_far_b))
        total_b.append((dx_own_b.astype(f32) + found).astype(bf16))
    total_b = behind(jnp.concatenate(total_b, axis=1), home_a)
    home_b = place.between_experts(total_b)

    kinds = [score_own_a, score_far_a, score_own_b, score_far_b]
    sizes = [v.shape[0] for v in kinds]
    every = jnp.stack(ring(behind(jnp.concatenate(kinds), *far_b)))
    every = jnp.take(every, (jnp.arange(chips) - place.chip) % chips, axis=0)
    split, at = [], 0
    for size in sizes:
        split.append(every[:, at : at + size].reshape(chips * size))
        at += size
    near = [
        v.reshape(experts, count) for v, count in ((split[0], count_a), (split[2], count_b))
    ]
    beyond = [
        v.reshape(slices - 1, experts, count)
        for v, count in ((split[1], count_a), (split[3], count_b))
    ]
    score_rows = jnp.concatenate(near, axis=1).astype(f32)
    beyond = jnp.concatenate(beyond, axis=2)
    for k in range(1, slices):
        score_rows = score_rows + place.turn_slice(beyond[k - 1], -k).astype(f32)
    turned = [score_rows] + [place.turn_expert(score_rows, d) for d in range(1, experts)]
    turned = lax.dynamic_index_in_dim(jnp.stack(turned), place.expert, 1, keepdims=False)
    source = (place.expert - jnp.arange(experts)) % experts
    score_home = jnp.take(turned, source, axis=0)

    router_rows = halves_of(router_weight.T.astype(f32), 0)
    result = jnp.zeros((tokens, model_width), bf16)
    for h in range(2):
        groups = combine(
            [(home_a, h), (home_b, h)],
            score_home,
            rank,
            gates,
            router_rows[h],
            [first_a, first_b],
            chips,
        )
        core = place.core if h == 0 else 1 - place.core
        for g in range(chips):
            part = groups[g] if g == 0 else place.turn_chip(groups[g], -g)
            chip = (place.chip + g) % chips
            result = lax.dynamic_update_slice_in_dim(result, part, (2 * chip + core) * width, 1)
    grad_hidden = result.reshape(rollouts, positions, model_width)
    return grad_queries, grad_keys, grad_values, grad_hidden


def on_device(
    queries,
    key_rows,
    value_rows,
    decay_rate,
    norm_gain,
    attn_probe,
    hidden_in,
    moe_probe,
    router_weight,
    routes,
    gate_weight,
    up_weight,
    down_weight,
    rollout_logprob,
    trainer_logprob,
    advantage,
    clip_low,
    clip_high,
):
    place = Layout(router_weight.shape[1])
    importance = jnp.exp(trainer_logprob - rollout_logprob)
    clipped = jnp.minimum(jnp.maximum(importance, clip_low[0]), clip_high[0])
    coeff = -(clipped * advantage) / queries.shape[0]
    objective = coeff * trainer_logprob
    grads = expert_and_attention(
        place,
        hidden_in,
        moe_probe,
        router_weight,
        routes,
        gate_weight,
        up_weight,
        down_weight,
        coeff,
        queries,
        key_rows,
        value_rows,
        decay_rate,
        norm_gain,
        attn_probe,
    )
    return (objective, *grads)


def solution(mesh):
    in_specs = (
        P(None, "seq", "expert"),
        P(None, "seq", "expert"),
        P(None, "seq", "expert"),
        P("expert"),
        P("expert"),
        P(None, "seq", "expert"),
        P(None, ("seq", "expert"), None),
        P(None, ("seq", "expert"), None),
        P(),
        P(None, ("seq", "expert"), None),
        P("expert", "seq", None),
        P("expert", "seq", None),
        P("expert", "seq", None),
        P(None, "seq"),
        P(None, "seq"),
        P(None, "seq"),
        P(),
        P(),
    )
    out_specs = (
        P(None, "seq"),
        P(None, "seq", "expert"),
        P(None, "seq", "expert"),
        P(None, "seq", "expert"),
        P(None, ("seq", "expert"), None),
    )
    return jax.shard_map(
        on_device, mesh=mesh, in_specs=in_specs, out_specs=out_specs, check_vma=False
    )
```

```python
import jax
import jax.numpy as jnp
from jax import lax
from jax.experimental import pallas as pl
from jax.experimental.pallas import tpu as pltpu
from jax.sharding import PartitionSpec as P

highest = lax.Precision.HIGHEST
norm_epsilon = 1e-06
f32 = jnp.float32
bf16 = jnp.bfloat16
vmem_limit = 48 * 2**20

in_scale = 32.0
out_scale = 4.0


class Layout:
    def __init__(self, window_experts):
        self.seq = lax.axis_size("seq")
        self.chips = self.seq // 2
        self.spread = lax.axis_size("expert")
        self.experts = window_experts
        self.slices = self.spread // window_experts
        here = lax.axis_index("seq")
        self.chip, self.core = here // 2, here % 2
        self.expert = lax.axis_index("expert") // self.slices

    def swap_core(self, v):
        return lax.ppermute(v, "seq", [(i, i ^ 1) for i in range(self.seq)])

    def turn_chip(self, v, p):
        n = self.chips
        return lax.ppermute(
            v, "seq", [(i, ((i // 2 + p) % n) * 2 + i % 2) for i in range(self.seq)]
        )

    def later_chip(self, v, p):
        pairs = [(i, i + 2 * p) for i in range(self.seq) if 0 <= i + 2 * p < self.seq]
        return lax.ppermute(v, "seq", pairs)

    def between_experts(self, v):
        n, m = self.experts, self.slices
        groups = [[q * m + j for q in range(n)] for j in range(m)]
        return lax.all_to_all(v, "expert", 0, 0, axis_index_groups=groups, tiled=True)

    def turn_expert(self, v, d):
        n, m = self.experts, self.slices
        return lax.ppermute(
            v, "expert", [(i, ((i // m + d) % n) * m + i % m) for i in range(self.spread)]
        )

    def turn_slice(self, v, k):
        m = self.slices
        return lax.ppermute(
            v, "expert", [(i, (i // m) * m + (i % m + k) % m) for i in range(self.spread)]
        )


def params(**kw):
    return pltpu.CompilerParams(vmem_limit_bytes=vmem_limit, **kw)


short = pl.CostEstimate(flops=1000, bytes_accessed=1000, transcendentals=0)


def tile_of(size):
    return 768 if size % 768 == 0 else size


def any_spec():
    return pl.BlockSpec(memory_space=pl.ANY)


def pick_rows(groups, rank, first, count, padded, after):
    experts = rank.shape[0]
    halves, tokens, width = groups[0].shape
    total = tokens * len(groups)

    def body(rank_ref, *refs):
        group_refs, out_ref = refs[: len(groups)], refs[-1]
        slot = lax.broadcasted_iota(jnp.int32, (padded, total), 0)
        wanted = jnp.where(slot < count, slot + first, -2)
        for h in range(halves):
            rows = jnp.concatenate([g[h] for g in group_refs], axis=0)
            for d in range(experts):
                pick = (rank_ref[d : d + 1, :] == wanted).astype(bf16)
                out_ref[d, h] = jnp.dot(pick, rows, preferred_element_type=f32).astype(bf16)

    vmem = pl.BlockSpec(memory_space=pltpu.VMEM)
    return pl.pallas_call(
        body,
        in_specs=[vmem] * (1 + len(groups)) + [any_spec()] * len(after),
        out_specs=vmem,
        out_shape=jax.ShapeDtypeStruct((experts, halves, padded, width), bf16),
        compiler_params=params(),
        cost_estimate=short,
        name="pick_rows",
    )(rank, *groups, *after)


def project(jobs, rows, chip, chips, after):
    experts, halves, padded, width = jobs[0][0][0].shape
    arrays_each = len(jobs[0][0])
    count = arrays_each * experts
    part = rows * count // chips
    per_part = count // chips
    units = jobs[0][1][0][0].shape[1]
    tile = tile_of(units)
    arrays = [v for job in jobs for v in job[0]]
    mats = [half for job in jobs for pair in job[1] for half in pair]
    owner = [j for j, job in enumerate(jobs) for _ in job[1]]
    mat_count = len(owner)

    def body(chip_ref, *refs):
        array_refs = refs[: len(arrays)]
        mat_refs = refs[len(arrays) : len(arrays) + len(mats)]
        keep_ref, send_ref, held = refs[-3:]

        def left(job, h):
            found = [
                r[:, h].reshape(experts * padded, width)
                for r in array_refs[job * arrays_each : (job + 1) * arrays_each]
            ]
            return found[0] if len(found) == 1 else jnp.concatenate(found, axis=0)

        for m in range(mat_count):
            result = jnp.dot(
                left(owner[m], 0), mat_refs[2 * m][...], preferred_element_type=f32
            )
            result = result + jnp.dot(
                left(owner[m], 1), mat_refs[2 * m + 1][...], preferred_element_type=f32
            )
            held[...] = result.reshape(chips, per_part * padded, tile)
            for p in range(chips):
                value = held[(chip_ref[0] + p) % chips]
                for b in range(per_part):
                    piece = value[b * padded : b * padded + rows]
                    if p == 0:
                        keep_ref[m, b * rows : (b + 1) * rows] = piece
                    else:
                        send_ref[p - 1, m, b * rows : (b + 1) * rows] = piece

    mat_spec = pl.BlockSpec((width, tile), lambda i: (0, i))
    return pl.pallas_call(
        body,
        grid=(units // tile,),
        in_specs=[pl.BlockSpec(memory_space=pltpu.SMEM)]
        + [pl.BlockSpec(arrays[0].shape, lambda i: (0, 0, 0, 0))] * len(arrays)
        + [mat_spec] * len(mats)
        + [any_spec()] * len(after),
        out_specs=[
            pl.BlockSpec((mat_count, part, tile), lambda i: (0, 0, i)),
            pl.BlockSpec((chips - 1, mat_count, part, tile), lambda i: (0, 0, 0, i)),
        ],
        out_shape=[
            jax.ShapeDtypeStruct((mat_count, part, units), f32),
            jax.ShapeDtypeStruct((chips - 1, mat_count, part, units), f32),
        ],
        scratch_shapes=[pltpu.VMEM((chips, per_part * padded, tile), f32)],
        compiler_params=params(),
        cost_estimate=short,
        name="project",
    )(chip, *arrays, *mats, *after)


def project_back(groups, mats, chip, rows, after):
    chips = len(groups[0])
    units = groups[0][0].shape[2]
    width = mats[0][0].shape[0]
    halves = len(mats)
    tile = tile_of(width)
    steps = width // tile
    parts = [v for group in groups for v in group]
    sizes = [group[0].shape[1] for group in groups]
    rooms = [-(-size // 16) * 16 for size in sizes]
    bases = [chips * sum(rooms[:g]) for g in range(len(groups))]
    total = chips * sum(rooms)
    counts = [size * chips // rows for size in sizes]

    def body(chip_ref, *refs):
        part_refs = refs[: len(parts)]
        mat_refs = refs[len(parts) : len(parts) + 2 * halves]
        out_refs = refs[-2 - len(groups) : -2]
        gate_all, up_all = refs[-2:]
        step = pl.program_id(0)

        @pl.when(step == 0)
        def _():
            for g, size in enumerate(sizes):
                for r in range(chips):
                    place = (chip_ref[0] + r) % chips
                    start = pl.multiple_of(bases[g] + place * rooms[g], 16)
                    gate_all[pl.ds(start, size)] = part_refs[g * chips + r][0]
                    up_all[pl.ds(start, size)] = part_refs[g * chips + r][1]

        def multiply(gate_mat_ref, up_mat_ref):
            contract = (((1,), (1,)), ((), ()))
            result = lax.dot_general(
                gate_all[...], gate_mat_ref[...], contract, preferred_element_type=f32
            )
            result = result + lax.dot_general(
                up_all[...], up_mat_ref[...], contract, preferred_element_type=f32
            )
            for g, count in enumerate(counts):
                per_part = count // chips
                for b in range(count):
                    start = bases[g] + b // per_part * rooms[g] + b % per_part * rows
                    out_refs[g][b, 0] = result[start : start + rows].astype(bf16)

        if halves == 1:
            multiply(*mat_refs)
        else:
            for h in range(halves):

                @pl.when(step // steps == h)
                def _():
                    multiply(mat_refs[2 * h], mat_refs[2 * h + 1])

    def mat_spec(h):
        return pl.BlockSpec((tile, units), lambda i: (jnp.clip(i - h * steps, 0, steps - 1), 0))

    def row_spec(count):
        return pl.BlockSpec((count, 1, rows, tile), lambda i: (0, i // steps, 0, i % steps))

    return pl.pallas_call(
        body,
        grid=(halves * steps,),
        in_specs=[pl.BlockSpec(memory_space=pltpu.SMEM)]
        + [pl.BlockSpec(v.shape, lambda i: (0, 0, 0)) for v in parts]
        + [mat_spec(h) for h in range(halves) for _ in range(2)]
        + [any_spec()] * len(after),
        out_specs=[row_spec(count) for count in counts],
        out_shape=[
            jax.ShapeDtypeStruct((count, halves, rows, width), bf16) for count in counts
        ],
        scratch_shapes=[pltpu.VMEM((total, units), bf16)] * 2,
        compiler_params=params(),
        cost_estimate=short,
        name="project_back",
    )(chip, *parts, *[m for pair in mats for m in pair], *after)


def combine(returned, scores, rank, gates, router, firsts, groups):
    experts, _, _, width = returned[0][0].shape
    counts = [v.shape[2] for v, _ in returned]
    total = rank.shape[0]
    tokens = total // groups

    def body(*refs):
        returned_refs = refs[: len(returned)]
        score_ref, rank_ref, gate_ref, router_ref = refs[len(returned) : len(returned) + 4]
        out_refs = refs[len(returned) + 4 :]
        acc = jnp.zeros((total, width), f32)
        picked = []
        slots = lax.broadcasted_iota(jnp.int32, (total, score_ref.shape[1]), 1)
        for d in range(experts):
            hit = rank_ref[:, d : d + 1] == slots
            picked.append(
                jnp.sum(jnp.where(hit, score_ref[d : d + 1, :], 0.0), axis=1, keepdims=True)
            )
        mean = sum(gate_ref[:, d : d + 1] * picked[d] for d in range(experts))
        for d in range(experts):
            grad = gate_ref[:, d : d + 1] * (picked[d] - mean)
            acc = acc + grad * router_ref[d : d + 1, :]
        for c, rows_ref in enumerate(returned_refs):
            for d in range(experts):
                value = rows_ref[d, 0]
                slot = lax.broadcasted_iota(jnp.int32, (total, value.shape[0]), 1) + firsts[c]
                weight = jnp.where(rank_ref[:, d : d + 1] == slot, gate_ref[:, d : d + 1], 0.0)
                high = weight.astype(bf16)
                low = (weight - high.astype(f32)).astype(bf16)
                acc = acc + jnp.dot(high, value, preferred_element_type=f32)
                acc = acc + jnp.dot(low, value, preferred_element_type=f32)
        for g in range(groups):
            out_refs[g][...] = acc[g * tokens : (g + 1) * tokens].astype(bf16)

    row_count = experts * sum(counts)

    def half_spec(count, h):
        return pl.BlockSpec((experts, 1, count, width), lambda i: (0, h, 0, 0))

    def whole_spec(v):
        return pl.BlockSpec(v.shape, lambda i: (0, 0))

    return pl.pallas_call(
        body,
        grid=(1,),
        in_specs=[half_spec(v.shape[2], h) for v, h in returned]
        + [whole_spec(v) for v in (scores, rank, gates, router)],
        out_specs=[pl.BlockSpec((tokens, width), lambda i: (0, 0))] * groups,
        out_shape=[jax.ShapeDtypeStruct((tokens, width), bf16)] * groups,
        compiler_params=params(),
        cost_estimate=short,
        name="combine",
    )(*[v for v, _ in returned], scores, rank, gates, router)


def split3(v):
    high = v.astype(bf16)
    rest = v - high.astype(f32)
    middle = rest.astype(bf16)
    return high, middle, (rest - middle.astype(f32)).astype(bf16)


def dot_left(a, b, dims):
    contract = (((dims[0],), (dims[1],)), ((), ()))
    return sum(lax.dot_general(t, b, contract, preferred_element_type=f32) for t in split3(a))


def dot_right(a, b, dims):
    contract = (((dims[0],), (dims[1],)), ((), ()))
    return sum(lax.dot_general(a, t, contract, preferred_element_type=f32) for t in split3(b))


def dot_full(a, b, dims):
    contract = (((dims[0],), (dims[1],)), ((), ()))
    return lax.dot_general(a, b, contract, precision=highest, preferred_element_type=f32)


def head_specs(rollouts, block, head):
    rows = pl.BlockSpec((rollouts, block, head), lambda h: (0, 0, h))
    state = pl.BlockSpec((rollouts, 1, head, head), lambda h: (0, h, 0, 0))
    return pl.BlockSpec(memory_space=pltpu.SMEM), rows, state


def key_value_state(key_rows, value_rows, decay_rate, after):
    rollouts, block, width = key_rows.shape
    heads = decay_rate.shape[0]
    head = width // heads
    smem, rows, state = head_specs(rollouts, block, head)

    def body(rate_ref, key_ref, value_ref, *refs):
        rate = rate_ref[pl.program_id(0)]
        offset = lax.broadcasted_iota(jnp.int32, (block, 1), 0).astype(f32)
        tail = jnp.exp(-rate * (block - 1.0 - offset))
        for r in range(rollouts):
            decayed = key_ref[r].astype(f32) * tail
            refs[-1][r, 0] = dot_left(decayed, value_ref[r], (0, 0))

    return pl.pallas_call(
        body,
        grid=(heads,),
        in_specs=[smem, rows, rows] + [any_spec()] * len(after),
        out_specs=state,
        out_shape=jax.ShapeDtypeStruct((rollouts, heads, head, head), f32),
        compiler_params=params(),
        cost_estimate=short,
        name="key_value_state",
    )(decay_rate, key_rows, value_rows, *after)


def local_grads(
    queries, key_rows, value_rows, attn_probe, gain, coeff, decay_rate, state, after
):
    rollouts, block, width = queries.shape
    heads = decay_rate.shape[0]
    head = width // heads
    smem, rows, state_spec = head_specs(rollouts, block, head)

    def body(rate_ref, q_ref, k_ref, v_ref, probe_ref, gain_ref, coeff_ref, state_ref, *refs):
        grad_q_ref, grad_k_ref, grad_v_ref, summary_ref = refs[-4:]
        rate = rate_ref[pl.program_id(0)]
        offset = lax.broadcasted_iota(jnp.int32, (block, 1), 0).astype(f32)
        lead = jnp.exp(-rate * (offset + 1.0))
        tail = jnp.exp(-rate * offset)
        line = lax.broadcasted_iota(jnp.int32, (block, block), 0)
        column = lax.broadcasted_iota(jnp.int32, (block, block), 1)
        distance = (line - column).astype(f32)
        within = jnp.where(line >= column, jnp.exp(-rate * jnp.maximum(distance, 0.0)), 0.0)
        for r in range(rollouts):
            query, key, value, before = q_ref[r], k_ref[r], v_ref[r], state_ref[r, 0]
            scores = lax.dot_general(
                query, key, (((1,), (1,)), ((), ())), preferred_element_type=f32
            )
            scores = scores * within
            output = dot_left(scores, value, (1, 0))
            output = output + lead * dot_right(query, before, (1, 0))
            inverse = lax.rsqrt(
                jnp.mean(output * output, axis=-1, keepdims=True) + norm_epsilon
            )
            scaled = gain_ref[...] * (coeff_ref[:, r : r + 1] * probe_ref[r].astype(f32))
            grad_out = inverse * scaled - output * inverse**3 * jnp.mean(
                scaled * output, axis=-1, keepdims=True
            )
            summary_ref[r, 0] = dot_right(query, tail * grad_out, (0, 0))
            product = dot_left(grad_out, value, (1, 1)) * within
            grad_q = dot_left(product, key, (1, 0))
            grad_q = grad_q + lead * dot_full(grad_out, before, (1, 1))
            grad_q_ref[r] = grad_q.astype(bf16)
            grad_k_ref[r] = dot_left(product, query, (0, 0))
            grad_v_ref[r] = dot_full(scores, grad_out, (0, 0))

    return pl.pallas_call(
        body,
        grid=(heads,),
        in_specs=[
            smem,
            rows,
            rows,
            rows,
            rows,
            pl.BlockSpec((1, head), lambda h: (0, h)),
            pl.BlockSpec((block, rollouts), lambda h: (0, 0)),
            state_spec,
        ]
        + [any_spec()] * len(after),
        out_specs=[rows, rows, rows, state_spec],
        out_shape=[
            jax.ShapeDtypeStruct(queries.shape, bf16),
            jax.ShapeDtypeStruct(queries.shape, f32),
            jax.ShapeDtypeStruct(queries.shape, f32),
            jax.ShapeDtypeStruct(state.shape, f32),
        ],
        compiler_params=params(),
        cost_estimate=short,
        name="local_grads",
    )(decay_rate, queries, key_rows, value_rows, attn_probe, gain, coeff, state, *after)


def later_grads(key_rows, value_rows, grad_k, grad_v, decay_rate, state, after):
    rollouts, block, width = key_rows.shape
    heads = decay_rate.shape[0]
    head = width // heads
    smem, rows, state_spec = head_specs(rollouts, block, head)

    def body(rate_ref, k_ref, v_ref, grad_k_ref, grad_v_ref, state_ref, *refs):
        out_k_ref, out_v_ref = refs[-2:]
        rate = rate_ref[pl.program_id(0)]
        offset = lax.broadcasted_iota(jnp.int32, (block, 1), 0).astype(f32)
        tail = jnp.exp(-rate * (block - offset))
        for r in range(rollouts):
            after_state = state_ref[r, 0]
            grad_k = grad_k_ref[r] + tail * dot_right(v_ref[r], after_state, (1, 1))
            grad_v = grad_v_ref[r] + tail * dot_right(k_ref[r], after_state, (1, 0))
            out_k_ref[r] = grad_k.astype(bf16)
            out_v_ref[r] = grad_v.astype(bf16)

    return pl.pallas_call(
        body,
        grid=(heads,),
        in_specs=[smem, rows, rows, rows, rows, state_spec] + [any_spec()] * len(after),
        out_specs=[rows, rows],
        out_shape=[jax.ShapeDtypeStruct(key_rows.shape, bf16)] * 2,
        compiler_params=params(),
        cost_estimate=short,
        name="later_grads",
    )(decay_rate, key_rows, value_rows, grad_k, grad_v, state, *after)


def outside_states(place, summary, direction):
    return [place.later_chip(summary, direction * p) for p in range(1, place.chips)]


def carried(place, summary, decay_rate, block_size, direction, found=None):
    def block_decay(blocks):
        return jnp.exp(-decay_rate * (block_size * blocks)).reshape(1, -1, 1, 1)

    if found is None:
        found = outside_states(place, summary, direction)
    mine = jnp.stack([summary, *found])
    partner = place.swap_core(mine)
    first = (place.core == 0) if direction > 0 else (place.core == 1)
    one = block_decay(1)
    near = jnp.where(first, partner + one * mine, mine + one * partner)
    outside = sum(block_decay(2 * (p - 1)) * near[p] for p in range(1, place.chips))
    return jnp.where(first, outside, partner[0] + one * outside)


def cut_features(v, scale, chip_core, chips, after):
    tokens, model_width = v.shape
    width = model_width // (2 * chips)

    def body(where_ref, v_ref, *refs):
        keep_ref, send_ref = refs[-2:]
        for p in range(chips):
            chip = (where_ref[0] + p) % chips
            for h in range(2):
                core = where_ref[1] if h == 0 else 1 - where_ref[1]
                start = pl.multiple_of((2 * chip + core) * width, 128)
                value = v_ref[:, pl.ds(start, width)]
                if scale is not None:
                    value = (refs[0][...] * value.astype(f32)).astype(bf16)
                if p == 0:
                    keep_ref[h] = value
                else:
                    send_ref[p - 1, h] = value

    vmem = pl.BlockSpec(memory_space=pltpu.VMEM)
    extra = [] if scale is None else [scale]
    return pl.pallas_call(
        body,
        in_specs=[pl.BlockSpec(memory_space=pltpu.SMEM), vmem]
        + [vmem] * len(extra)
        + [any_spec()] * len(after),
        out_specs=[vmem, vmem],
        out_shape=[
            jax.ShapeDtypeStruct((2, tokens, width), bf16),
            jax.ShapeDtypeStruct((chips - 1, 2, tokens, width), bf16),
        ],
        compiler_params=params(),
        cost_estimate=short,
        name="cut_features",
    )(chip_core, v, *extra, *after)


def expert_and_attention(
    place,
    hidden_in,
    moe_probe,
    router_weight,
    routes,
    gate_weight,
    up_weight,
    down_weight,
    coeff,
    queries,
    key_rows,
    value_rows,
    decay_rate,
    norm_gain,
    attn_probe,
):
    rollouts, positions, model_width = hidden_in.shape
    chips, experts, slices = place.chips, place.experts, place.slices
    tokens = rollouts * positions
    width = gate_weight.shape[1]
    own_mats = (gate_weight[0], up_weight[0], down_weight[0])

    hidden = hidden_in.reshape(tokens, model_width)
    local_coeff = lax.dynamic_slice_in_dim(
        coeff, lax.axis_index("expert") * positions, positions, 1
    )
    chip_here = place.chip.reshape(1).astype(jnp.int32)
    chip_core = jnp.stack([place.chip, place.core]).astype(jnp.int32)
    last = []

    def ordered(kernel, *args, needs=()):
        result = kernel(*args, (*last, *needs))
        last[:] = [result[0] if isinstance(result, (list, tuple)) else result]
        return result

    def across(v, scale):
        keep, send = ordered(cut_features, v, scale, chip_core, chips)
        return [keep] + [place.turn_chip(send[p - 1], p) for p in range(1, chips)]

    hidden_groups = across(hidden, None)
    grad_groups = across(
        moe_probe.reshape(tokens, model_width), local_coeff.reshape(tokens, 1)
    )

    def halves_of(v, p):
        chip = (place.chip + p) % chips
        return jnp.stack(
            [
                lax.dynamic_slice_in_dim(v, (2 * chip + core) * width, width, 1)
                for core in (place.core, 1 - place.core)
            ]
        )

    logits = jnp.dot(hidden, router_weight, preferred_element_type=f32)
    flat_routes = routes.reshape(tokens, -1)
    onehot = (flat_routes[:, :, None] == jnp.arange(experts, dtype=jnp.int32)).astype(f32)
    chosen = jnp.sum(onehot * logits[:, None, :], axis=-1)
    exponent = jnp.exp(chosen)
    gate = exponent / jnp.sum(exponent, axis=-1, keepdims=True)
    facts = jnp.concatenate(
        [onehot.sum(axis=1), jnp.sum(onehot * gate[:, :, None], axis=1)], axis=1
    )
    all_facts = [facts] + [place.turn_chip(facts, p) for p in range(1, chips)]

    pairs = [(m, place.swap_core(m)) for m in own_mats[:2]]

    fact_stack = jnp.stack(all_facts)
    member, gates = fact_stack[:, :, :experts], fact_stack[:, :, experts:]
    whose = (place.chip - jnp.arange(chips)) % chips
    earlier = (whose[None, :] < whose[:, None]).astype(f32)
    offset = jnp.sum(earlier[:, :, None] * member.sum(axis=1)[None], axis=1)
    step = jnp.arange(tokens)
    below = (step[:, None] > step[None, :]).astype(f32)
    rank = jnp.einsum("ts,gse->gte", below, member) + offset[:, None, :]
    rank = jnp.where(member > 0, rank, -1.0).astype(jnp.int32)
    rank = rank.reshape(chips * tokens, experts)
    gates = gates.reshape(chips * tokens, experts)
    rank_lanes = rank.T

    most = chips * rollouts * (positions // 2 + 1)
    small = max(16, most // 2 // 16 * 16)
    chunks = [(0, small), (small, most - small)]
    def dispatch(groups, first, count, needs=()):
        padded = -(-count // 8) * 8
        return ordered(pick_rows, groups, rank_lanes, first, count, padded, needs=needs)

    def behind(v, *others):
        return lax.optimization_barrier((v, *others))[0] if others else v

    def relay(mine):
        return [place.turn_slice(mine, k) for k in range(1, slices)]

    def partial(jobs, count, needs=()):
        scales = jnp.asarray([scale for _, mats, scale in jobs for _ in mats], f32)
        scales = scales.reshape(-1, 1, 1)
        ready = [([behind(v, *needs) for v in arrays], mats) for arrays, mats, _ in jobs]
        keep, send = ordered(project, ready, count, chip_here, chips)
        send = (send * scales).astype(jnp.float16)
        arrived = [place.turn_chip(send[p - 1], p) for p in range(1, chips)]
        return keep, arrived, scales

    def settle(part):
        keep, arrived, scale = part
        return keep + sum(v.astype(f32) for v in arrived) / scale

    def ring(v):
        found = [v] + [None] * (chips - 1)
        for p in range(1, chips):
            found[chips - p] = place.turn_chip(v, p)
        return found

    def middle(*some):
        pre_gate, pre_up, unit_grad = jnp.concatenate([settle(v) for v in some])
        sigmoid_gate = jax.nn.sigmoid(pre_gate)
        activated = pre_gate * sigmoid_gate
        units = activated * pre_up
        score = jnp.sum(units * unit_grad, axis=-1).astype(bf16)
        slope = pre_up * sigmoid_gate * (1.0 + pre_gate * (1.0 - sigmoid_gate))
        which = jnp.arange(2).reshape(2, 1, 1)
        both = (unit_grad * jnp.where(which == 0, slope, activated)).astype(bf16)
        return ring(both), score

    def back(groups, halves, count, needs=()):
        mats = [(pairs[0][h], pairs[1][h]) for h in halves]
        return ordered(project_back, groups, mats, chip_here, count, needs=needs)

    def to_slices(dx):
        return [
            place.turn_slice(dx[(k - 1) * experts : k * experts], -k) for k in range(1, slices)
        ]

    (first_a, count_a), (first_b, count_b) = chunks

    block = queries.shape[1]
    def held(part, kernel_result):
        keep, arrived, scale = part
        return keep, [behind(v, kernel_result) for v in arrived], scale

    summary = ordered(key_value_state, key_rows, value_rows, decay_rate)
    early = outside_states(place, summary, 1)
    picked_hidden_a = dispatch(hidden_groups, first_a, count_a)
    picked_grads_a = dispatch(grad_groups, first_a, count_a)
    picked_hidden_b = dispatch(hidden_groups, first_b, count_b)
    hidden_a = place.between_experts(behind(picked_hidden_a, picked_grads_a))
    picked_grads_b = dispatch(grad_groups, first_b, count_b, [pairs[0][1], pairs[1][1]])
    far_hidden_a = relay(hidden_a)
    pairs.append((own_mats[2], place.swap_core(behind(own_mats[2], picked_grads_b))))
    inner_own_a = partial([([hidden_a], pairs[:2], in_scale)], count_a, early)
    early = [behind(v, inner_own_a[0]) for v in early]
    state_before = carried(place, summary, decay_rate, block, 1, early)
    grad_queries, local_k, local_v, summary = ordered(
        local_grads,
        queries,
        key_rows,
        value_rows,
        attn_probe,
        norm_gain.reshape(1, -1),
        coeff.T,
        decay_rate,
        state_before,
    )
    grads_a = place.between_experts(behind(picked_grads_a, hidden_a))
    far_grads_a = relay(behind(grads_a, summary))
    outer_own_a = partial([([grads_a], pairs[2:], out_scale)], count_a)
    hidden_b = place.between_experts(behind(picked_hidden_b, grads_a, summary))
    own_a, score_own_a = middle(inner_own_a, outer_own_a)
    whole_far_a = partial(
        [(far_hidden_a, pairs[:2], in_scale), (far_grads_a, pairs[2:], out_scale)],
        count_a,
        own_a[:1],
    )
    far_hidden_b = relay(behind(hidden_b, whole_far_a[0]))
    grads_b = place.between_experts(behind(picked_grads_b, hidden_b, whole_far_a[0]))
    inner_own_b = partial([([hidden_b], pairs[:2], in_scale)], count_b, own_a[1:])
    far_grads_b = relay(grads_b)
    far_a, score_far_a = middle(whole_far_a)
    state_after = carried(place, behind(summary, whole_far_a[0]), decay_rate, block, -1)
    inner_far_b = partial([(far_hidden_b, pairs[:2], in_scale)], count_b, far_a[:1])
    outer_own_b = partial([([grads_b], pairs[2:], out_scale)], count_b)
    dx_own_a, dx_far_a = back([own_a, far_a], (0, 1), count_a)
    outer_far_b = partial([(far_grads_b, pairs[2:], out_scale)], count_b, inner_own_b[1])
    grad_keys, grad_values = ordered(
        later_grads, key_rows, value_rows, local_k, local_v, decay_rate, state_after
    )
    far_b, score_far_b = middle(inner_far_b, outer_far_b)
    own_b, score_own_b = middle(held(inner_own_b, far_b[0]), held(outer_own_b, far_b[0]))
    from_far_a = to_slices(dx_far_a)
    total_a = dx_own_a.astype(f32) + sum(
        behind(v, own_b[0], grad_keys).astype(f32) for v in from_far_a
    )
    total_a = total_a.astype(bf16)
    home_a = place.between_experts(total_a)
    from_far_b = [
        to_slices(back([far_b], (h,), count_b, [total_a])[0]) for h in range(2)
    ]
    (dx_own_b,) = back([own_b], (0, 1), count_b)
    total_b = dx_own_b.astype(f32) + sum(
        jnp.concatenate(halves, axis=1).astype(f32) for halves in zip(*from_far_b)
    )
    total_b = behind(total_b.astype(bf16), home_a)
    home_b = place.between_experts(total_b)

    kinds = [score_own_a, score_far_a, score_own_b, score_far_b]
    sizes = [v.shape[0] for v in kinds]
    every = jnp.stack(ring(behind(jnp.concatenate(kinds), *far_b)))
    every = jnp.take(every, (jnp.arange(chips) - place.chip) % chips, axis=0)
    split, at = [], 0
    for size in sizes:
        split.append(every[:, at : at + size].reshape(chips * size))
        at += size
    near = [
        v.reshape(experts, count) for v, count in ((split[0], count_a), (split[2], count_b))
    ]
    beyond = [
        v.reshape(slices - 1, experts, count)
        for v, count in ((split[1], count_a), (split[3], count_b))
    ]
    score_rows = jnp.concatenate(near, axis=1).astype(f32)
    beyond = jnp.concatenate(beyond, axis=2)
    for k in range(1, slices):
        score_rows = score_rows + place.turn_slice(beyond[k - 1], -k).astype(f32)
    turned = [score_rows] + [place.turn_expert(score_rows, d) for d in range(1, experts)]
    turned = lax.dynamic_index_in_dim(jnp.stack(turned), place.expert, 1, keepdims=False)
    source = (place.expert - jnp.arange(experts)) % experts
    score_home = jnp.take(turned, source, axis=0)

    router_rows = halves_of(router_weight.T.astype(f32), 0)
    result = jnp.zeros((tokens, model_width), bf16)
    for h in range(2):
        groups = combine(
            [(home_a, h), (home_b, h)],
            score_home,
            rank,
            gates,
            router_rows[h],
            [first_a, first_b],
            chips,
        )
        core = place.core if h == 0 else 1 - place.core
        for g in range(chips):
            part = groups[g] if g == 0 else place.turn_chip(groups[g], -g)
            chip = (place.chip + g) % chips
            result = lax.dynamic_update_slice_in_dim(result, part, (2 * chip + core) * width, 1)
    grad_hidden = result.reshape(rollouts, positions, model_width)
    return grad_queries, grad_keys, grad_values, grad_hidden


def on_device(
    queries,
    key_rows,
    value_rows,
    decay_rate,
    norm_gain,
    attn_probe,
    hidden_in,
    moe_probe,
    router_weight,
    routes,
    gate_weight,
    up_weight,
    down_weight,
    rollout_logprob,
    trainer_logprob,
    advantage,
    clip_low,
    clip_high,
):
    place = Layout(router_weight.shape[1])
    importance = jnp.exp(trainer_logprob - rollout_logprob)
    clipped = jnp.minimum(jnp.maximum(importance, clip_low[0]), clip_high[0])
    coeff = -(clipped * advantage) / queries.shape[0]
    objective = coeff * trainer_logprob
    grads = expert_and_attention(
        place,
        hidden_in,
        moe_probe,
        router_weight,
        routes,
        gate_weight,
        up_weight,
        down_weight,
        coeff,
        queries,
        key_rows,
        value_rows,
        decay_rate,
        norm_gain,
        attn_probe,
    )
    return (objective, *grads)


def solution(mesh):
    in_specs = (
        P(None, "seq", "expert"),
        P(None, "seq", "expert"),
        P(None, "seq", "expert"),
        P("expert"),
        P("expert"),
        P(None, "seq", "expert"),
        P(None, ("seq", "expert"), None),
        P(None, ("seq", "expert"), None),
        P(),
        P(None, ("seq", "expert"), None),
        P("expert", "seq", None),
        P("expert", "seq", None),
        P("expert", "seq", None),
        P(None, "seq"),
        P(None, "seq"),
        P(None, "seq"),
        P(),
        P(),
    )
    out_specs = (
        P(None, "seq"),
        P(None, "seq", "expert"),
        P(None, "seq", "expert"),
        P(None, "seq", "expert"),
        P(None, ("seq", "expert"), None),
    )
    return jax.shard_map(
        on_device, mesh=mesh, in_specs=in_specs, out_specs=out_specs, check_vma=False
    )
```

```python
import jax
import jax.numpy as jnp
from jax import lax
from jax.experimental import pallas as pl
from jax.experimental.pallas import tpu as pltpu
from jax.sharding import PartitionSpec as P

highest = lax.Precision.HIGHEST
norm_epsilon = 1e-06
f32 = jnp.float32
bf16 = jnp.bfloat16
vmem_limit = 48 * 2**20

in_scale = 32.0
out_scale = 4.0


class Layout:
    def __init__(self, window_experts):
        self.seq = lax.axis_size("seq")
        self.chips = self.seq // 2
        self.spread = lax.axis_size("expert")
        self.experts = window_experts
        self.slices = self.spread // window_experts
        here = lax.axis_index("seq")
        self.chip, self.core = here // 2, here % 2
        self.expert = lax.axis_index("expert") // self.slices

    def swap_core(self, v):
        return lax.ppermute(v, "seq", [(i, i ^ 1) for i in range(self.seq)])

    def turn_chip(self, v, p):
        n = self.chips
        return lax.ppermute(
            v, "seq", [(i, ((i // 2 + p) % n) * 2 + i % 2) for i in range(self.seq)]
        )

    def later_chip(self, v, p):
        pairs = [(i, i + 2 * p) for i in range(self.seq) if 0 <= i + 2 * p < self.seq]
        return lax.ppermute(v, "seq", pairs)

    def between_experts(self, v):
        n, m = self.experts, self.slices
        groups = [[q * m + j for q in range(n)] for j in range(m)]
        return lax.all_to_all(v, "expert", 0, 0, axis_index_groups=groups, tiled=True)

    def turn_expert(self, v, d):
        n, m = self.experts, self.slices
        return lax.ppermute(
            v, "expert", [(i, ((i // m + d) % n) * m + i % m) for i in range(self.spread)]
        )

    def turn_slice(self, v, k):
        m = self.slices
        return lax.ppermute(
            v, "expert", [(i, (i // m) * m + (i % m + k) % m) for i in range(self.spread)]
        )


def params(**kw):
    return pltpu.CompilerParams(vmem_limit_bytes=vmem_limit, **kw)


short = pl.CostEstimate(flops=1000, bytes_accessed=1000, transcendentals=0)


def tile_of(size):
    return 768 if size % 768 == 0 else size


def any_spec():
    return pl.BlockSpec(memory_space=pl.ANY)


def pick_rows(groups, rank, first, count, padded, after):
    experts = rank.shape[0]
    halves, tokens, width = groups[0].shape
    total = tokens * len(groups)

    def body(rank_ref, *refs):
        group_refs, out_ref = refs[: len(groups)], refs[-1]
        slot = lax.broadcasted_iota(jnp.int32, (padded, total), 0)
        wanted = jnp.where(slot < count, slot + first, -2)
        for h in range(halves):
            rows = jnp.concatenate([g[h] for g in group_refs], axis=0)
            for d in range(experts):
                pick = (rank_ref[d : d + 1, :] == wanted).astype(bf16)
                out_ref[d, h] = jnp.dot(pick, rows, preferred_element_type=f32).astype(bf16)

    vmem = pl.BlockSpec(memory_space=pltpu.VMEM)
    return pl.pallas_call(
        body,
        in_specs=[vmem] * (1 + len(groups)) + [any_spec()] * len(after),
        out_specs=vmem,
        out_shape=jax.ShapeDtypeStruct((experts, halves, padded, width), bf16),
        compiler_params=params(),
        cost_estimate=short,
        name="pick_rows",
    )(rank, *groups, *after)


def project(jobs, rows, chip, chips, after):
    experts, halves, padded, width = jobs[0][0][0].shape
    arrays_each = len(jobs[0][0])
    count = arrays_each * experts
    part = rows * count // chips
    per_part = count // chips
    units = jobs[0][1][0][0].shape[1]
    tile = tile_of(units)
    arrays = [v for job in jobs for v in job[0]]
    mats = [half for job in jobs for pair in job[1] for half in pair]
    owner = [j for j, job in enumerate(jobs) for _ in job[1]]
    mat_count = len(owner)

    def body(chip_ref, *refs):
        array_refs = refs[: len(arrays)]
        mat_refs = refs[len(arrays) : len(arrays) + len(mats)]
        keep_ref, send_ref, held = refs[-3:]

        def left(job, h):
            found = [
                r[:, h].reshape(experts * padded, width)
                for r in array_refs[job * arrays_each : (job + 1) * arrays_each]
            ]
            return found[0] if len(found) == 1 else jnp.concatenate(found, axis=0)

        for m in range(mat_count):
            result = jnp.dot(
                left(owner[m], 0), mat_refs[2 * m][...], preferred_element_type=f32
            )
            result = result + jnp.dot(
                left(owner[m], 1), mat_refs[2 * m + 1][...], preferred_element_type=f32
            )
            held[...] = result.reshape(chips, per_part * padded, tile)
            for p in range(chips):
                value = held[(chip_ref[0] + p) % chips]
                for b in range(per_part):
                    piece = value[b * padded : b * padded + rows]
                    if p == 0:
                        keep_ref[m, b * rows : (b + 1) * rows] = piece
                    else:
                        send_ref[p - 1, m, b * rows : (b + 1) * rows] = piece

    mat_spec = pl.BlockSpec((width, tile), lambda i: (0, i))
    return pl.pallas_call(
        body,
        grid=(units // tile,),
        in_specs=[pl.BlockSpec(memory_space=pltpu.SMEM)]
        + [pl.BlockSpec(arrays[0].shape, lambda i: (0, 0, 0, 0))] * len(arrays)
        + [mat_spec] * len(mats)
        + [any_spec()] * len(after),
        out_specs=[
            pl.BlockSpec((mat_count, part, tile), lambda i: (0, 0, i)),
            pl.BlockSpec((chips - 1, mat_count, part, tile), lambda i: (0, 0, 0, i)),
        ],
        out_shape=[
            jax.ShapeDtypeStruct((mat_count, part, units), f32),
            jax.ShapeDtypeStruct((chips - 1, mat_count, part, units), f32),
        ],
        scratch_shapes=[pltpu.VMEM((chips, per_part * padded, tile), f32)],
        compiler_params=params(),
        cost_estimate=short,
        name="project",
    )(chip, *arrays, *mats, *after)


def project_back(groups, mats, chip, rows, after):
    chips = len(groups[0])
    units = groups[0][0].shape[2]
    width = mats[0][0].shape[0]
    halves = len(mats)
    tile = tile_of(width)
    steps = width // tile
    parts = [v for group in groups for v in group]
    sizes = [group[0].shape[1] for group in groups]
    rooms = [-(-size // 16) * 16 for size in sizes]
    bases = [chips * sum(rooms[:g]) for g in range(len(groups))]
    total = chips * sum(rooms)
    counts = [size * chips // rows for size in sizes]

    def body(chip_ref, *refs):
        part_refs = refs[: len(parts)]
        mat_refs = refs[len(parts) : len(parts) + 2 * halves]
        out_refs = refs[-2 - len(groups) : -2]
        gate_all, up_all = refs[-2:]
        step = pl.program_id(0)

        @pl.when(step == 0)
        def _():
            for g, size in enumerate(sizes):
                for r in range(chips):
                    place = (chip_ref[0] + r) % chips
                    start = pl.multiple_of(bases[g] + place * rooms[g], 16)
                    gate_all[pl.ds(start, size)] = part_refs[g * chips + r][0]
                    up_all[pl.ds(start, size)] = part_refs[g * chips + r][1]

        def multiply(gate_mat_ref, up_mat_ref):
            contract = (((1,), (1,)), ((), ()))
            result = lax.dot_general(
                gate_all[...], gate_mat_ref[...], contract, preferred_element_type=f32
            )
            result = result + lax.dot_general(
                up_all[...], up_mat_ref[...], contract, preferred_element_type=f32
            )
            for g, count in enumerate(counts):
                per_part = count // chips
                for b in range(count):
                    start = bases[g] + b // per_part * rooms[g] + b % per_part * rows
                    out_refs[g][b, 0] = result[start : start + rows].astype(bf16)

        if halves == 1:
            multiply(*mat_refs)
        else:
            for h in range(halves):

                @pl.when(step // steps == h)
                def _():
                    multiply(mat_refs[2 * h], mat_refs[2 * h + 1])

    def mat_spec(h):
        return pl.BlockSpec((tile, units), lambda i: (jnp.clip(i - h * steps, 0, steps - 1), 0))

    def row_spec(count):
        return pl.BlockSpec((count, 1, rows, tile), lambda i: (0, i // steps, 0, i % steps))

    return pl.pallas_call(
        body,
        grid=(halves * steps,),
        in_specs=[pl.BlockSpec(memory_space=pltpu.SMEM)]
        + [pl.BlockSpec(v.shape, lambda i: (0, 0, 0)) for v in parts]
        + [mat_spec(h) for h in range(halves) for _ in range(2)]
        + [any_spec()] * len(after),
        out_specs=[row_spec(count) for count in counts],
        out_shape=[
            jax.ShapeDtypeStruct((count, halves, rows, width), bf16) for count in counts
        ],
        scratch_shapes=[pltpu.VMEM((total, units), bf16)] * 2,
        compiler_params=params(),
        cost_estimate=short,
        name="project_back",
    )(chip, *parts, *[m for pair in mats for m in pair], *after)


def combine(returned, scores, rank, gates, router, firsts, groups):
    experts, _, _, width = returned[0][0].shape
    counts = [v.shape[2] for v, _ in returned]
    total = rank.shape[0]
    tokens = total // groups

    def body(*refs):
        returned_refs = refs[: len(returned)]
        score_ref, rank_ref, gate_ref, router_ref = refs[len(returned) : len(returned) + 4]
        out_refs = refs[len(returned) + 4 :]
        acc = jnp.zeros((total, width), f32)
        picked = []
        slots = lax.broadcasted_iota(jnp.int32, (total, score_ref.shape[1]), 1)
        for d in range(experts):
            hit = rank_ref[:, d : d + 1] == slots
            picked.append(
                jnp.sum(jnp.where(hit, score_ref[d : d + 1, :], 0.0), axis=1, keepdims=True)
            )
        mean = sum(gate_ref[:, d : d + 1] * picked[d] for d in range(experts))
        for d in range(experts):
            grad = gate_ref[:, d : d + 1] * (picked[d] - mean)
            acc = acc + grad * router_ref[d : d + 1, :]
        for c, rows_ref in enumerate(returned_refs):
            for d in range(experts):
                value = rows_ref[d, 0]
                slot = lax.broadcasted_iota(jnp.int32, (total, value.shape[0]), 1) + firsts[c]
                weight = jnp.where(rank_ref[:, d : d + 1] == slot, gate_ref[:, d : d + 1], 0.0)
                high = weight.astype(bf16)
                low = (weight - high.astype(f32)).astype(bf16)
                acc = acc + jnp.dot(high, value, preferred_element_type=f32)
                acc = acc + jnp.dot(low, value, preferred_element_type=f32)
        for g in range(groups):
            out_refs[g][...] = acc[g * tokens : (g + 1) * tokens].astype(bf16)

    row_count = experts * sum(counts)

    def half_spec(count, h):
        return pl.BlockSpec((experts, 1, count, width), lambda i: (0, h, 0, 0))

    def whole_spec(v):
        return pl.BlockSpec(v.shape, lambda i: (0, 0))

    return pl.pallas_call(
        body,
        grid=(1,),
        in_specs=[half_spec(v.shape[2], h) for v, h in returned]
        + [whole_spec(v) for v in (scores, rank, gates, router)],
        out_specs=[pl.BlockSpec((tokens, width), lambda i: (0, 0))] * groups,
        out_shape=[jax.ShapeDtypeStruct((tokens, width), bf16)] * groups,
        compiler_params=params(),
        cost_estimate=short,
        name="combine",
    )(*[v for v, _ in returned], scores, rank, gates, router)


def split3(v):
    high = v.astype(bf16)
    rest = v - high.astype(f32)
    middle = rest.astype(bf16)
    return high, middle, (rest - middle.astype(f32)).astype(bf16)


def dot_left(a, b, dims):
    contract = (((dims[0],), (dims[1],)), ((), ()))
    return sum(lax.dot_general(t, b, contract, preferred_element_type=f32) for t in split3(a))


def dot_right(a, b, dims):
    contract = (((dims[0],), (dims[1],)), ((), ()))
    return sum(lax.dot_general(a, t, contract, preferred_element_type=f32) for t in split3(b))


def dot_full(a, b, dims):
    contract = (((dims[0],), (dims[1],)), ((), ()))
    return lax.dot_general(a, b, contract, precision=highest, preferred_element_type=f32)


def head_specs(rollouts, block, head):
    rows = pl.BlockSpec((rollouts, block, head), lambda h: (0, 0, h))
    state = pl.BlockSpec((rollouts, 1, head, head), lambda h: (0, h, 0, 0))
    return pl.BlockSpec(memory_space=pltpu.SMEM), rows, state


def key_value_state(key_rows, value_rows, decay_rate, after):
    rollouts, block, width = key_rows.shape
    heads = decay_rate.shape[0]
    head = width // heads
    smem, rows, state = head_specs(rollouts, block, head)

    def body(rate_ref, key_ref, value_ref, *refs):
        rate = rate_ref[pl.program_id(0)]
        offset = lax.broadcasted_iota(jnp.int32, (block, 1), 0).astype(f32)
        tail = jnp.exp(-rate * (block - 1.0 - offset))
        for r in range(rollouts):
            decayed = key_ref[r].astype(f32) * tail
            refs[-1][r, 0] = dot_left(decayed, value_ref[r], (0, 0))

    return pl.pallas_call(
        body,
        grid=(heads,),
        in_specs=[smem, rows, rows] + [any_spec()] * len(after),
        out_specs=state,
        out_shape=jax.ShapeDtypeStruct((rollouts, heads, head, head), f32),
        compiler_params=params(),
        cost_estimate=short,
        name="key_value_state",
    )(decay_rate, key_rows, value_rows, *after)


def local_grads(
    queries, key_rows, value_rows, attn_probe, gain, coeff, decay_rate, state, after
):
    rollouts, block, width = queries.shape
    heads = decay_rate.shape[0]
    head = width // heads
    smem, rows, state_spec = head_specs(rollouts, block, head)

    def body(rate_ref, q_ref, k_ref, v_ref, probe_ref, gain_ref, coeff_ref, state_ref, *refs):
        grad_q_ref, grad_k_ref, grad_v_ref, summary_ref = refs[-4:]
        rate = rate_ref[pl.program_id(0)]
        offset = lax.broadcasted_iota(jnp.int32, (block, 1), 0).astype(f32)
        lead = jnp.exp(-rate * (offset + 1.0))
        tail = jnp.exp(-rate * offset)
        line = lax.broadcasted_iota(jnp.int32, (block, block), 0)
        column = lax.broadcasted_iota(jnp.int32, (block, block), 1)
        distance = (line - column).astype(f32)
        within = jnp.where(line >= column, jnp.exp(-rate * jnp.maximum(distance, 0.0)), 0.0)
        for r in range(rollouts):
            query, key, value, before = q_ref[r], k_ref[r], v_ref[r], state_ref[r, 0]
            scores = lax.dot_general(
                query, key, (((1,), (1,)), ((), ())), preferred_element_type=f32
            )
            scores = scores * within
            output = dot_left(scores, value, (1, 0))
            output = output + lead * dot_right(query, before, (1, 0))
            inverse = lax.rsqrt(
                jnp.mean(output * output, axis=-1, keepdims=True) + norm_epsilon
            )
            scaled = gain_ref[...] * (coeff_ref[:, r : r + 1] * probe_ref[r].astype(f32))
            grad_out = inverse * scaled - output * inverse**3 * jnp.mean(
                scaled * output, axis=-1, keepdims=True
            )
            summary_ref[r, 0] = dot_right(query, tail * grad_out, (0, 0))
            product = dot_left(grad_out, value, (1, 1)) * within
            grad_q = dot_left(product, key, (1, 0))
            grad_q = grad_q + lead * dot_full(grad_out, before, (1, 1))
            grad_q_ref[r] = grad_q.astype(bf16)
            grad_k_ref[r] = dot_left(product, query, (0, 0))
            grad_v_ref[r] = dot_full(scores, grad_out, (0, 0))

    return pl.pallas_call(
        body,
        grid=(heads,),
        in_specs=[
            smem,
            rows,
            rows,
            rows,
            rows,
            pl.BlockSpec((1, head), lambda h: (0, h)),
            pl.BlockSpec((block, rollouts), lambda h: (0, 0)),
            state_spec,
        ]
        + [any_spec()] * len(after),
        out_specs=[rows, rows, rows, state_spec],
        out_shape=[
            jax.ShapeDtypeStruct(queries.shape, bf16),
            jax.ShapeDtypeStruct(queries.shape, f32),
            jax.ShapeDtypeStruct(queries.shape, f32),
            jax.ShapeDtypeStruct(state.shape, f32),
        ],
        compiler_params=params(),
        cost_estimate=short,
        name="local_grads",
    )(decay_rate, queries, key_rows, value_rows, attn_probe, gain, coeff, state, *after)


def later_grads(key_rows, value_rows, grad_k, grad_v, decay_rate, state, after):
    rollouts, block, width = key_rows.shape
    heads = decay_rate.shape[0]
    head = width // heads
    smem, rows, state_spec = head_specs(rollouts, block, head)

    def body(rate_ref, k_ref, v_ref, grad_k_ref, grad_v_ref, state_ref, *refs):
        out_k_ref, out_v_ref = refs[-2:]
        rate = rate_ref[pl.program_id(0)]
        offset = lax.broadcasted_iota(jnp.int32, (block, 1), 0).astype(f32)
        tail = jnp.exp(-rate * (block - offset))
        for r in range(rollouts):
            after_state = state_ref[r, 0]
            grad_k = grad_k_ref[r] + tail * dot_right(v_ref[r], after_state, (1, 1))
            grad_v = grad_v_ref[r] + tail * dot_right(k_ref[r], after_state, (1, 0))
            out_k_ref[r] = grad_k.astype(bf16)
            out_v_ref[r] = grad_v.astype(bf16)

    return pl.pallas_call(
        body,
        grid=(heads,),
        in_specs=[smem, rows, rows, rows, rows, state_spec] + [any_spec()] * len(after),
        out_specs=[rows, rows],
        out_shape=[jax.ShapeDtypeStruct(key_rows.shape, bf16)] * 2,
        compiler_params=params(),
        cost_estimate=short,
        name="later_grads",
    )(decay_rate, key_rows, value_rows, grad_k, grad_v, state, *after)


def outside_states(place, summary, direction):
    return [place.later_chip(summary, direction * p) for p in range(1, place.chips)]


def carried(place, summary, decay_rate, block_size, direction, found=None):
    def block_decay(blocks):
        return jnp.exp(-decay_rate * (block_size * blocks)).reshape(1, -1, 1, 1)

    if found is None:
        found = outside_states(place, summary, direction)
    mine = jnp.stack([summary, *found])
    partner = place.swap_core(mine)
    first = (place.core == 0) if direction > 0 else (place.core == 1)
    one = block_decay(1)
    near = jnp.where(first, partner + one * mine, mine + one * partner)
    outside = sum(block_decay(2 * (p - 1)) * near[p] for p in range(1, place.chips))
    return jnp.where(first, outside, partner[0] + one * outside)


def cut_features(v, scale, chip_core, chips, after):
    tokens, model_width = v.shape
    width = model_width // (2 * chips)

    def body(where_ref, v_ref, *refs):
        keep_ref, send_ref = refs[-2:]
        for p in range(chips):
            chip = (where_ref[0] + p) % chips
            for h in range(2):
                core = where_ref[1] if h == 0 else 1 - where_ref[1]
                start = pl.multiple_of((2 * chip + core) * width, 128)
                value = v_ref[:, pl.ds(start, width)]
                if scale is not None:
                    value = (refs[0][...] * value.astype(f32)).astype(bf16)
                if p == 0:
                    keep_ref[h] = value
                else:
                    send_ref[p - 1, h] = value

    vmem = pl.BlockSpec(memory_space=pltpu.VMEM)
    extra = [] if scale is None else [scale]
    return pl.pallas_call(
        body,
        in_specs=[pl.BlockSpec(memory_space=pltpu.SMEM), vmem]
        + [vmem] * len(extra)
        + [any_spec()] * len(after),
        out_specs=[vmem, vmem],
        out_shape=[
            jax.ShapeDtypeStruct((2, tokens, width), bf16),
            jax.ShapeDtypeStruct((chips - 1, 2, tokens, width), bf16),
        ],
        compiler_params=params(),
        cost_estimate=short,
        name="cut_features",
    )(chip_core, v, *extra, *after)


def expert_and_attention(
    place,
    hidden_in,
    moe_probe,
    router_weight,
    routes,
    gate_weight,
    up_weight,
    down_weight,
    coeff,
    queries,
    key_rows,
    value_rows,
    decay_rate,
    norm_gain,
    attn_probe,
):
    rollouts, positions, model_width = hidden_in.shape
    chips, experts, slices = place.chips, place.experts, place.slices
    tokens = rollouts * positions
    width = gate_weight.shape[1]
    own_mats = (gate_weight[0], up_weight[0], down_weight[0])

    hidden = hidden_in.reshape(tokens, model_width)
    local_coeff = lax.dynamic_slice_in_dim(
        coeff, lax.axis_index("expert") * positions, positions, 1
    )
    chip_here = place.chip.reshape(1).astype(jnp.int32)
    chip_core = jnp.stack([place.chip, place.core]).astype(jnp.int32)
    last = []

    def ordered(kernel, *args, needs=()):
        result = kernel(*args, (*last, *needs))
        last[:] = [result[0] if isinstance(result, (list, tuple)) else result]
        return result

    def across(v, scale):
        keep, send = ordered(cut_features, v, scale, chip_core, chips)
        return [keep] + [place.turn_chip(send[p - 1], p) for p in range(1, chips)]

    hidden_groups = across(hidden, None)
    grad_groups = across(
        moe_probe.reshape(tokens, model_width), local_coeff.reshape(tokens, 1)
    )

    def halves_of(v, p):
        chip = (place.chip + p) % chips
        return jnp.stack(
            [
                lax.dynamic_slice_in_dim(v, (2 * chip + core) * width, width, 1)
                for core in (place.core, 1 - place.core)
            ]
        )

    logits = jnp.dot(hidden, router_weight, preferred_element_type=f32)
    flat_routes = routes.reshape(tokens, -1)
    onehot = (flat_routes[:, :, None] == jnp.arange(experts, dtype=jnp.int32)).astype(f32)
    chosen = jnp.sum(onehot * logits[:, None, :], axis=-1)
    exponent = jnp.exp(chosen)
    gate = exponent / jnp.sum(exponent, axis=-1, keepdims=True)
    facts = jnp.concatenate(
        [onehot.sum(axis=1), jnp.sum(onehot * gate[:, :, None], axis=1)], axis=1
    )
    all_facts = [facts] + [place.turn_chip(facts, p) for p in range(1, chips)]

    pairs = [(m, place.swap_core(m)) for m in own_mats[:2]]

    fact_stack = jnp.stack(all_facts)
    member, gates = fact_stack[:, :, :experts], fact_stack[:, :, experts:]
    whose = (place.chip - jnp.arange(chips)) % chips
    earlier = (whose[None, :] < whose[:, None]).astype(f32)
    offset = jnp.sum(earlier[:, :, None] * member.sum(axis=1)[None], axis=1)
    step = jnp.arange(tokens)
    below = (step[:, None] > step[None, :]).astype(f32)
    rank = jnp.einsum("ts,gse->gte", below, member) + offset[:, None, :]
    rank = jnp.where(member > 0, rank, -1.0).astype(jnp.int32)
    rank = rank.reshape(chips * tokens, experts)
    gates = gates.reshape(chips * tokens, experts)
    rank_lanes = rank.T

    most = chips * rollouts * (positions // 2 + 1)
    small = max(16, most // 2 // 16 * 16)
    chunks = [(0, small), (small, most - small)]
    def dispatch(groups, first, count, needs=()):
        padded = -(-count // 8) * 8
        return ordered(pick_rows, groups, rank_lanes, first, count, padded, needs=needs)

    def behind(v, *others):
        return lax.optimization_barrier((v, *others))[0] if others else v

    def relay(mine):
        return [place.turn_slice(mine, k) for k in range(1, slices)]

    def partial(jobs, count, needs=()):
        scales = jnp.asarray([scale for _, mats, scale in jobs for _ in mats], f32)
        scales = scales.reshape(-1, 1, 1)
        ready = [([behind(v, *needs) for v in arrays], mats) for arrays, mats, _ in jobs]
        keep, send = ordered(project, ready, count, chip_here, chips)
        send = (send * scales).astype(jnp.float16)
        arrived = [place.turn_chip(send[p - 1], p) for p in range(1, chips)]
        return keep, arrived, scales

    def settle(part):
        keep, arrived, scale = part
        return keep + sum(v.astype(f32) for v in arrived) / scale

    def ring(v):
        found = [v] + [None] * (chips - 1)
        for p in range(1, chips):
            found[chips - p] = place.turn_chip(v, p)
        return found

    def middle(*some):
        pre_gate, pre_up, unit_grad = jnp.concatenate([settle(v) for v in some])
        sigmoid_gate = jax.nn.sigmoid(pre_gate)
        activated = pre_gate * sigmoid_gate
        units = activated * pre_up
        score = jnp.sum(units * unit_grad, axis=-1).astype(bf16)
        slope = pre_up * sigmoid_gate * (1.0 + pre_gate * (1.0 - sigmoid_gate))
        which = jnp.arange(2).reshape(2, 1, 1)
        both = (unit_grad * jnp.where(which == 0, slope, activated)).astype(bf16)
        return ring(both), score

    def back(groups, halves, count, needs=()):
        mats = [(pairs[0][h], pairs[1][h]) for h in halves]
        return ordered(project_back, groups, mats, chip_here, count, needs=needs)

    def to_slices(dx):
        return [
            place.turn_slice(dx[(k - 1) * experts : k * experts], -k) for k in range(1, slices)
        ]

    (first_a, count_a), (first_b, count_b) = chunks

    block = queries.shape[1]
    def held(part, kernel_result):
        keep, arrived, scale = part
        return keep, [behind(v, kernel_result) for v in arrived], scale

    summary = ordered(key_value_state, key_rows, value_rows, decay_rate)
    early = outside_states(place, summary, 1)
    picked_hidden_a = dispatch(hidden_groups, first_a, count_a)
    picked_grads_a = dispatch(grad_groups, first_a, count_a)
    picked_hidden_b = dispatch(hidden_groups, first_b, count_b)
    hidden_a = place.between_experts(behind(picked_hidden_a, picked_grads_a))
    picked_grads_b = dispatch(grad_groups, first_b, count_b, [pairs[0][1], pairs[1][1]])
    far_hidden_a = relay(hidden_a)
    pairs.append((own_mats[2], place.swap_core(behind(own_mats[2], picked_grads_b))))
    inner_own_a = partial([([hidden_a], pairs[:2], in_scale)], count_a, early)
    early = [behind(v, inner_own_a[0]) for v in early]
    state_before = carried(place, summary, decay_rate, block, 1, early)
    grad_queries, local_k, local_v, summary = ordered(
        local_grads,
        queries,
        key_rows,
        value_rows,
        attn_probe,
        norm_gain.reshape(1, -1),
        coeff.T,
        decay_rate,
        state_before,
    )
    grads_a = place.between_experts(behind(picked_grads_a, hidden_a))
    far_grads_a = relay(behind(grads_a, summary))
    outer_own_a = partial([([grads_a], pairs[2:], out_scale)], count_a)
    hidden_b = place.between_experts(behind(picked_hidden_b, grads_a, summary))
    own_a, score_own_a = middle(inner_own_a, outer_own_a)
    whole_far_a = partial(
        [(far_hidden_a, pairs[:2], in_scale), (far_grads_a, pairs[2:], out_scale)],
        count_a,
        own_a[:1],
    )
    far_hidden_b = relay(behind(hidden_b, own_a[0]))
    grads_b = place.between_experts(behind(picked_grads_b, hidden_b, own_a[0]))
    inner_own_b = partial([([hidden_b], pairs[:2], in_scale)], count_b, own_a[1:])
    far_grads_b = relay(grads_b)
    far_a, score_far_a = middle(whole_far_a)
    state_after = carried(place, behind(summary, whole_far_a[0]), decay_rate, block, -1)
    inner_far_b = partial([(far_hidden_b, pairs[:2], in_scale)], count_b, far_a[:1])
    outer_own_b = partial([([grads_b], pairs[2:], out_scale)], count_b)
    dx_own_a, dx_far_a = back([own_a, far_a], (0, 1), count_a)
    outer_far_b = partial([(far_grads_b, pairs[2:], out_scale)], count_b, inner_own_b[1])
    grad_keys, grad_values = ordered(
        later_grads, key_rows, value_rows, local_k, local_v, decay_rate, state_after
    )
    far_b, score_far_b = middle(inner_far_b, outer_far_b)
    own_b, score_own_b = middle(held(inner_own_b, far_b[0]), held(outer_own_b, far_b[0]))
    from_far_a = to_slices(dx_far_a)
    total_a = dx_own_a.astype(f32) + sum(
        behind(v, own_b[0], grad_keys).astype(f32) for v in from_far_a
    )
    total_a = total_a.astype(bf16)
    home_a = place.between_experts(total_a)
    from_far_b = [
        to_slices(back([far_b], (h,), count_b, [total_a])[0]) for h in range(2)
    ]
    (dx_own_b,) = back([own_b], (0, 1), count_b)
    total_b = dx_own_b.astype(f32) + sum(
        jnp.concatenate(halves, axis=1).astype(f32) for halves in zip(*from_far_b)
    )
    total_b = behind(total_b.astype(bf16), home_a)
    home_b = place.between_experts(total_b)

    kinds = [score_own_a, score_far_a, score_own_b, score_far_b]
    sizes = [v.shape[0] for v in kinds]
    every = jnp.stack(ring(behind(jnp.concatenate(kinds), *far_b)))
    every = jnp.take(every, (jnp.arange(chips) - place.chip) % chips, axis=0)
    split, at = [], 0
    for size in sizes:
        split.append(every[:, at : at + size].reshape(chips * size))
        at += size
    near = [
        v.reshape(experts, count) for v, count in ((split[0], count_a), (split[2], count_b))
    ]
    beyond = [
        v.reshape(slices - 1, experts, count)
        for v, count in ((split[1], count_a), (split[3], count_b))
    ]
    score_rows = jnp.concatenate(near, axis=1).astype(f32)
    beyond = jnp.concatenate(beyond, axis=2)
    for k in range(1, slices):
        score_rows = score_rows + place.turn_slice(beyond[k - 1], -k).astype(f32)
    turned = [score_rows] + [place.turn_expert(score_rows, d) for d in range(1, experts)]
    turned = lax.dynamic_index_in_dim(jnp.stack(turned), place.expert, 1, keepdims=False)
    source = (place.expert - jnp.arange(experts)) % experts
    score_home = jnp.take(turned, source, axis=0)

    router_rows = halves_of(router_weight.T.astype(f32), 0)
    result = jnp.zeros((tokens, model_width), bf16)
    for h in range(2):
        groups = combine(
            [(home_a, h), (home_b, h)],
            score_home,
            rank,
            gates,
            router_rows[h],
            [first_a, first_b],
            chips,
        )
        core = place.core if h == 0 else 1 - place.core
        for g in range(chips):
            part = groups[g] if g == 0 else place.turn_chip(groups[g], -g)
            chip = (place.chip + g) % chips
            result = lax.dynamic_update_slice_in_dim(result, part, (2 * chip + core) * width, 1)
    grad_hidden = result.reshape(rollouts, positions, model_width)
    return grad_queries, grad_keys, grad_values, grad_hidden


def on_device(
    queries,
    key_rows,
    value_rows,
    decay_rate,
    norm_gain,
    attn_probe,
    hidden_in,
    moe_probe,
    router_weight,
    routes,
    gate_weight,
    up_weight,
    down_weight,
    rollout_logprob,
    trainer_logprob,
    advantage,
    clip_low,
    clip_high,
):
    place = Layout(router_weight.shape[1])
    importance = jnp.exp(trainer_logprob - rollout_logprob)
    clipped = jnp.minimum(jnp.maximum(importance, clip_low[0]), clip_high[0])
    coeff = -(clipped * advantage) / queries.shape[0]
    objective = coeff * trainer_logprob
    grads = expert_and_attention(
        place,
        hidden_in,
        moe_probe,
        router_weight,
        routes,
        gate_weight,
        up_weight,
        down_weight,
        coeff,
        queries,
        key_rows,
        value_rows,
        decay_rate,
        norm_gain,
        attn_probe,
    )
    return (objective, *grads)


def solution(mesh):
    in_specs = (
        P(None, "seq", "expert"),
        P(None, "seq", "expert"),
        P(None, "seq", "expert"),
        P("expert"),
        P("expert"),
        P(None, "seq", "expert"),
        P(None, ("seq", "expert"), None),
        P(None, ("seq", "expert"), None),
        P(),
        P(None, ("seq", "expert"), None),
        P("expert", "seq", None),
        P("expert", "seq", None),
        P("expert", "seq", None),
        P(None, "seq"),
        P(None, "seq"),
        P(None, "seq"),
        P(),
        P(),
    )
    out_specs = (
        P(None, "seq"),
        P(None, "seq", "expert"),
        P(None, "seq", "expert"),
        P(None, "seq", "expert"),
        P(None, ("seq", "expert"), None),
    )
    return jax.shard_map(
        on_device, mesh=mesh, in_specs=in_specs, out_specs=out_specs, check_vma=False
    )
```

```python
import jax
import jax.numpy as jnp
from jax import lax
from jax.experimental import pallas as pl
from jax.experimental.pallas import tpu as pltpu
from jax.sharding import PartitionSpec as P

highest = lax.Precision.HIGHEST
norm_epsilon = 1e-06
f32 = jnp.float32
bf16 = jnp.bfloat16
vmem_limit = 48 * 2**20

in_scale = 32.0
out_scale = 4.0


class Layout:
    def __init__(self, window_experts):
        self.seq = lax.axis_size("seq")
        self.chips = self.seq // 2
        self.spread = lax.axis_size("expert")
        self.experts = window_experts
        self.slices = self.spread // window_experts
        here = lax.axis_index("seq")
        self.chip, self.core = here // 2, here % 2
        self.expert = lax.axis_index("expert") // self.slices

    def swap_core(self, v):
        return lax.ppermute(v, "seq", [(i, i ^ 1) for i in range(self.seq)])

    def turn_chip(self, v, p):
        n = self.chips
        return lax.ppermute(
            v, "seq", [(i, ((i // 2 + p) % n) * 2 + i % 2) for i in range(self.seq)]
        )

    def later_chip(self, v, p):
        pairs = [(i, i + 2 * p) for i in range(self.seq) if 0 <= i + 2 * p < self.seq]
        return lax.ppermute(v, "seq", pairs)

    def between_experts(self, v):
        n, m = self.experts, self.slices
        groups = [[q * m + j for q in range(n)] for j in range(m)]
        return lax.all_to_all(v, "expert", 0, 0, axis_index_groups=groups, tiled=True)

    def turn_expert(self, v, d):
        n, m = self.experts, self.slices
        return lax.ppermute(
            v, "expert", [(i, ((i // m + d) % n) * m + i % m) for i in range(self.spread)]
        )

    def turn_slice(self, v, k):
        m = self.slices
        return lax.ppermute(
            v, "expert", [(i, (i // m) * m + (i % m + k) % m) for i in range(self.spread)]
        )


def params(**kw):
    return pltpu.CompilerParams(vmem_limit_bytes=vmem_limit, **kw)


short = pl.CostEstimate(flops=1000, bytes_accessed=1000, transcendentals=0)


def tile_of(size):
    return 768 if size % 768 == 0 else size


def any_spec():
    return pl.BlockSpec(memory_space=pl.ANY)


def pick_rows(groups, rank, first, count, padded, after):
    experts = rank.shape[0]
    halves, tokens, width = groups[0].shape
    total = tokens * len(groups)

    def body(rank_ref, *refs):
        group_refs, out_ref = refs[: len(groups)], refs[-1]
        slot = lax.broadcasted_iota(jnp.int32, (padded, total), 0)
        wanted = jnp.where(slot < count, slot + first, -2)
        for h in range(halves):
            rows = jnp.concatenate([g[h] for g in group_refs], axis=0)
            for d in range(experts):
                pick = (rank_ref[d : d + 1, :] == wanted).astype(bf16)
                out_ref[d, h] = jnp.dot(pick, rows, preferred_element_type=f32).astype(bf16)

    vmem = pl.BlockSpec(memory_space=pltpu.VMEM)
    return pl.pallas_call(
        body,
        in_specs=[vmem] * (1 + len(groups)) + [any_spec()] * len(after),
        out_specs=vmem,
        out_shape=jax.ShapeDtypeStruct((experts, halves, padded, width), bf16),
        compiler_params=params(),
        cost_estimate=short,
        name="pick_rows",
    )(rank, *groups, *after)


def project(jobs, rows, chip, chips, after):
    experts, halves, padded, width = jobs[0][0][0].shape
    arrays_each = len(jobs[0][0])
    count = arrays_each * experts
    part = rows * count // chips
    per_part = count // chips
    units = jobs[0][1][0][0].shape[1]
    tile = tile_of(units)
    arrays = [v for job in jobs for v in job[0]]
    mats = [half for job in jobs for pair in job[1] for half in pair]
    owner = [j for j, job in enumerate(jobs) for _ in job[1]]
    mat_count = len(owner)

    def body(chip_ref, *refs):
        array_refs = refs[: len(arrays)]
        mat_refs = refs[len(arrays) : len(arrays) + len(mats)]
        keep_ref, send_ref, held = refs[-3:]

        def left(job, h):
            found = [
                r[:, h].reshape(experts * padded, width)
                for r in array_refs[job * arrays_each : (job + 1) * arrays_each]
            ]
            return found[0] if len(found) == 1 else jnp.concatenate(found, axis=0)

        for m in range(mat_count):
            result = jnp.dot(
                left(owner[m], 0), mat_refs[2 * m][...], preferred_element_type=f32
            )
            result = result + jnp.dot(
                left(owner[m], 1), mat_refs[2 * m + 1][...], preferred_element_type=f32
            )
            held[...] = result.reshape(chips, per_part * padded, tile)
            for p in range(chips):
                value = held[(chip_ref[0] + p) % chips]
                for b in range(per_part):
                    piece = value[b * padded : b * padded + rows]
                    if p == 0:
                        keep_ref[m, b * rows : (b + 1) * rows] = piece
                    else:
                        send_ref[p - 1, m, b * rows : (b + 1) * rows] = piece

    mat_spec = pl.BlockSpec((width, tile), lambda i: (0, i))
    return pl.pallas_call(
        body,
        grid=(units // tile,),
        in_specs=[pl.BlockSpec(memory_space=pltpu.SMEM)]
        + [pl.BlockSpec(arrays[0].shape, lambda i: (0, 0, 0, 0))] * len(arrays)
        + [mat_spec] * len(mats)
        + [any_spec()] * len(after),
        out_specs=[
            pl.BlockSpec((mat_count, part, tile), lambda i: (0, 0, i)),
            pl.BlockSpec((chips - 1, mat_count, part, tile), lambda i: (0, 0, 0, i)),
        ],
        out_shape=[
            jax.ShapeDtypeStruct((mat_count, part, units), f32),
            jax.ShapeDtypeStruct((chips - 1, mat_count, part, units), f32),
        ],
        scratch_shapes=[pltpu.VMEM((chips, per_part * padded, tile), f32)],
        compiler_params=params(),
        cost_estimate=short,
        name="project",
    )(chip, *arrays, *mats, *after)


def project_back(groups, mats, chip, rows, after):
    chips = len(groups[0])
    units = groups[0][0].shape[2]
    width = mats[0][0].shape[0]
    halves = len(mats)
    tile = 512 if width % 512 == 0 else tile_of(width)
    steps = width // tile
    parts = [v for group in groups for v in group]
    sizes = [group[0].shape[1] for group in groups]
    rooms = [-(-size // 16) * 16 for size in sizes]
    bases = [chips * sum(rooms[:g]) for g in range(len(groups))]
    total = chips * sum(rooms)
    counts = [size * chips // rows for size in sizes]

    def body(chip_ref, *refs):
        part_refs = refs[: len(parts)]
        mat_refs = refs[len(parts) : len(parts) + 2 * halves]
        out_refs = refs[-2 - len(groups) : -2]
        gate_all, up_all = refs[-2:]
        step = pl.program_id(0)

        @pl.when(step == 0)
        def _():
            for g, size in enumerate(sizes):
                for r in range(chips):
                    place = (chip_ref[0] + r) % chips
                    start = pl.multiple_of(bases[g] + place * rooms[g], 16)
                    gate_all[pl.ds(start, size)] = part_refs[g * chips + r][0]
                    up_all[pl.ds(start, size)] = part_refs[g * chips + r][1]

        def multiply(gate_mat_ref, up_mat_ref):
            contract = (((1,), (1,)), ((), ()))
            result = lax.dot_general(
                gate_all[...], gate_mat_ref[...], contract, preferred_element_type=f32
            )
            result = result + lax.dot_general(
                up_all[...], up_mat_ref[...], contract, preferred_element_type=f32
            )
            for g, count in enumerate(counts):
                per_part = count // chips
                for b in range(count):
                    start = bases[g] + b // per_part * rooms[g] + b % per_part * rows
                    out_refs[g][b, 0] = result[start : start + rows].astype(bf16)

        if halves == 1:
            multiply(*mat_refs)
        else:
            for h in range(halves):

                @pl.when(step // steps == h)
                def _():
                    multiply(mat_refs[2 * h], mat_refs[2 * h + 1])

    def mat_spec(h):
        return pl.BlockSpec((tile, units), lambda i: (jnp.clip(i - h * steps, 0, steps - 1), 0))

    def row_spec(count):
        return pl.BlockSpec((count, 1, rows, tile), lambda i: (0, i // steps, 0, i % steps))

    return pl.pallas_call(
        body,
        grid=(halves * steps,),
        in_specs=[pl.BlockSpec(memory_space=pltpu.SMEM)]
        + [pl.BlockSpec(v.shape, lambda i: (0, 0, 0)) for v in parts]
        + [mat_spec(h) for h in range(halves) for _ in range(2)]
        + [any_spec()] * len(after),
        out_specs=[row_spec(count) for count in counts],
        out_shape=[
            jax.ShapeDtypeStruct((count, halves, rows, width), bf16) for count in counts
        ],
        scratch_shapes=[pltpu.VMEM((total, units), bf16)] * 2,
        compiler_params=params(),
        cost_estimate=short,
        name="project_back",
    )(chip, *parts, *[m for pair in mats for m in pair], *after)


def combine(returned, scores, rank, gates, router, firsts, groups):
    experts, _, _, width = returned[0][0].shape
    counts = [v.shape[2] for v, _ in returned]
    total = rank.shape[0]
    tokens = total // groups

    def body(*refs):
        returned_refs = refs[: len(returned)]
        score_ref, rank_ref, gate_ref, router_ref = refs[len(returned) : len(returned) + 4]
        out_refs = refs[len(returned) + 4 :]
        acc = jnp.zeros((total, width), f32)
        picked = []
        slots = lax.broadcasted_iota(jnp.int32, (total, score_ref.shape[1]), 1)
        for d in range(experts):
            hit = rank_ref[:, d : d + 1] == slots
            picked.append(
                jnp.sum(jnp.where(hit, score_ref[d : d + 1, :], 0.0), axis=1, keepdims=True)
            )
        mean = sum(gate_ref[:, d : d + 1] * picked[d] for d in range(experts))
        for d in range(experts):
            grad = gate_ref[:, d : d + 1] * (picked[d] - mean)
            acc = acc + grad * router_ref[d : d + 1, :]
        for c, rows_ref in enumerate(returned_refs):
            for d in range(experts):
                value = rows_ref[d, 0]
                slot = lax.broadcasted_iota(jnp.int32, (total, value.shape[0]), 1) + firsts[c]
                weight = jnp.where(rank_ref[:, d : d + 1] == slot, gate_ref[:, d : d + 1], 0.0)
                high = weight.astype(bf16)
                low = (weight - high.astype(f32)).astype(bf16)
                acc = acc + jnp.dot(high, value, preferred_element_type=f32)
                acc = acc + jnp.dot(low, value, preferred_element_type=f32)
        for g in range(groups):
            out_refs[g][...] = acc[g * tokens : (g + 1) * tokens].astype(bf16)

    row_count = experts * sum(counts)

    def half_spec(count, h):
        return pl.BlockSpec((experts, 1, count, width), lambda i: (0, h, 0, 0))

    def whole_spec(v):
        return pl.BlockSpec(v.shape, lambda i: (0, 0))

    return pl.pallas_call(
        body,
        grid=(1,),
        in_specs=[half_spec(v.shape[2], h) for v, h in returned]
        + [whole_spec(v) for v in (scores, rank, gates, router)],
        out_specs=[pl.BlockSpec((tokens, width), lambda i: (0, 0))] * groups,
        out_shape=[jax.ShapeDtypeStruct((tokens, width), bf16)] * groups,
        compiler_params=params(),
        cost_estimate=short,
        name="combine",
    )(*[v for v, _ in returned], scores, rank, gates, router)


def split3(v):
    high = v.astype(bf16)
    rest = v - high.astype(f32)
    middle = rest.astype(bf16)
    return high, middle, (rest - middle.astype(f32)).astype(bf16)


def dot_left(a, b, dims):
    contract = (((dims[0],), (dims[1],)), ((), ()))
    return sum(lax.dot_general(t, b, contract, preferred_element_type=f32) for t in split3(a))


def dot_right(a, b, dims):
    contract = (((dims[0],), (dims[1],)), ((), ()))
    return sum(lax.dot_general(a, t, contract, preferred_element_type=f32) for t in split3(b))


def dot_full(a, b, dims):
    contract = (((dims[0],), (dims[1],)), ((), ()))
    return lax.dot_general(a, b, contract, precision=highest, preferred_element_type=f32)


def head_specs(rollouts, block, head):
    rows = pl.BlockSpec((rollouts, block, head), lambda h: (0, 0, h))
    state = pl.BlockSpec((rollouts, 1, head, head), lambda h: (0, h, 0, 0))
    return pl.BlockSpec(memory_space=pltpu.SMEM), rows, state


def key_value_state(key_rows, value_rows, decay_rate, after):
    rollouts, block, width = key_rows.shape
    heads = decay_rate.shape[0]
    head = width // heads
    smem, rows, state = head_specs(rollouts, block, head)

    def body(rate_ref, key_ref, value_ref, *refs):
        rate = rate_ref[pl.program_id(0)]
        offset = lax.broadcasted_iota(jnp.int32, (block, 1), 0).astype(f32)
        tail = jnp.exp(-rate * (block - 1.0 - offset))
        for r in range(rollouts):
            decayed = key_ref[r].astype(f32) * tail
            refs[-1][r, 0] = dot_left(decayed, value_ref[r], (0, 0))

    return pl.pallas_call(
        body,
        grid=(heads,),
        in_specs=[smem, rows, rows] + [any_spec()] * len(after),
        out_specs=state,
        out_shape=jax.ShapeDtypeStruct((rollouts, heads, head, head), f32),
        compiler_params=params(),
        cost_estimate=short,
        name="key_value_state",
    )(decay_rate, key_rows, value_rows, *after)


def local_grads(
    queries, key_rows, value_rows, attn_probe, gain, coeff, decay_rate, state, after
):
    rollouts, block, width = queries.shape
    heads = decay_rate.shape[0]
    head = width // heads
    smem, rows, state_spec = head_specs(rollouts, block, head)

    def body(rate_ref, q_ref, k_ref, v_ref, probe_ref, gain_ref, coeff_ref, state_ref, *refs):
        grad_q_ref, grad_k_ref, grad_v_ref, summary_ref = refs[-4:]
        rate = rate_ref[pl.program_id(0)]
        offset = lax.broadcasted_iota(jnp.int32, (block, 1), 0).astype(f32)
        lead = jnp.exp(-rate * (offset + 1.0))
        tail = jnp.exp(-rate * offset)
        line = lax.broadcasted_iota(jnp.int32, (block, block), 0)
        column = lax.broadcasted_iota(jnp.int32, (block, block), 1)
        distance = (line - column).astype(f32)
        within = jnp.where(line >= column, jnp.exp(-rate * jnp.maximum(distance, 0.0)), 0.0)
        for r in range(rollouts):
            query, key, value, before = q_ref[r], k_ref[r], v_ref[r], state_ref[r, 0]
            scores = lax.dot_general(
                query, key, (((1,), (1,)), ((), ())), preferred_element_type=f32
            )
            scores = scores * within
            output = dot_left(scores, value, (1, 0))
            output = output + lead * dot_right(query, before, (1, 0))
            inverse = lax.rsqrt(
                jnp.mean(output * output, axis=-1, keepdims=True) + norm_epsilon
            )
            scaled = gain_ref[...] * (coeff_ref[:, r : r + 1] * probe_ref[r].astype(f32))
            grad_out = inverse * scaled - output * inverse**3 * jnp.mean(
                scaled * output, axis=-1, keepdims=True
            )
            summary_ref[r, 0] = dot_right(query, tail * grad_out, (0, 0))
            product = dot_left(grad_out, value, (1, 1)) * within
            grad_q = dot_left(product, key, (1, 0))
            grad_q = grad_q + lead * dot_full(grad_out, before, (1, 1))
            grad_q_ref[r] = grad_q.astype(bf16)
            grad_k_ref[r] = dot_left(product, query, (0, 0))
            grad_v_ref[r] = dot_full(scores, grad_out, (0, 0))

    return pl.pallas_call(
        body,
        grid=(heads,),
        in_specs=[
            smem,
            rows,
            rows,
            rows,
            rows,
            pl.BlockSpec((1, head), lambda h: (0, h)),
            pl.BlockSpec((block, rollouts), lambda h: (0, 0)),
            state_spec,
        ]
        + [any_spec()] * len(after),
        out_specs=[rows, rows, rows, state_spec],
        out_shape=[
            jax.ShapeDtypeStruct(queries.shape, bf16),
            jax.ShapeDtypeStruct(queries.shape, f32),
            jax.ShapeDtypeStruct(queries.shape, f32),
            jax.ShapeDtypeStruct(state.shape, f32),
        ],
        compiler_params=params(),
        cost_estimate=short,
        name="local_grads",
    )(decay_rate, queries, key_rows, value_rows, attn_probe, gain, coeff, state, *after)


def later_grads(key_rows, value_rows, grad_k, grad_v, decay_rate, state, after):
    rollouts, block, width = key_rows.shape
    heads = decay_rate.shape[0]
    head = width // heads
    smem, rows, state_spec = head_specs(rollouts, block, head)

    def body(rate_ref, k_ref, v_ref, grad_k_ref, grad_v_ref, state_ref, *refs):
        out_k_ref, out_v_ref = refs[-2:]
        rate = rate_ref[pl.program_id(0)]
        offset = lax.broadcasted_iota(jnp.int32, (block, 1), 0).astype(f32)
        tail = jnp.exp(-rate * (block - offset))
        for r in range(rollouts):
            after_state = state_ref[r, 0]
            grad_k = grad_k_ref[r] + tail * dot_right(v_ref[r], after_state, (1, 1))
            grad_v = grad_v_ref[r] + tail * dot_right(k_ref[r], after_state, (1, 0))
            out_k_ref[r] = grad_k.astype(bf16)
            out_v_ref[r] = grad_v.astype(bf16)

    return pl.pallas_call(
        body,
        grid=(heads,),
        in_specs=[smem, rows, rows, rows, rows, state_spec] + [any_spec()] * len(after),
        out_specs=[rows, rows],
        out_shape=[jax.ShapeDtypeStruct(key_rows.shape, bf16)] * 2,
        compiler_params=params(),
        cost_estimate=short,
        name="later_grads",
    )(decay_rate, key_rows, value_rows, grad_k, grad_v, state, *after)


def outside_states(place, summary, direction):
    return [place.later_chip(summary, direction * p) for p in range(1, place.chips)]


def carried(place, summary, decay_rate, block_size, direction, found=None):
    def block_decay(blocks):
        return jnp.exp(-decay_rate * (block_size * blocks)).reshape(1, -1, 1, 1)

    if found is None:
        found = outside_states(place, summary, direction)
    mine = jnp.stack([summary, *found])
    partner = place.swap_core(mine)
    first = (place.core == 0) if direction > 0 else (place.core == 1)
    one = block_decay(1)
    near = jnp.where(first, partner + one * mine, mine + one * partner)
    outside = sum(block_decay(2 * (p - 1)) * near[p] for p in range(1, place.chips))
    return jnp.where(first, outside, partner[0] + one * outside)


def cut_features(v, scale, chip_core, chips, after):
    tokens, model_width = v.shape
    width = model_width // (2 * chips)

    def body(where_ref, v_ref, *refs):
        keep_ref, send_ref = refs[-2:]
        for p in range(chips):
            chip = (where_ref[0] + p) % chips
            for h in range(2):
                core = where_ref[1] if h == 0 else 1 - where_ref[1]
                start = pl.multiple_of((2 * chip + core) * width, 128)
                value = v_ref[:, pl.ds(start, width)]
                if scale is not None:
                    value = (refs[0][...] * value.astype(f32)).astype(bf16)
                if p == 0:
                    keep_ref[h] = value
                else:
                    send_ref[p - 1, h] = value

    vmem = pl.BlockSpec(memory_space=pltpu.VMEM)
    extra = [] if scale is None else [scale]
    return pl.pallas_call(
        body,
        in_specs=[pl.BlockSpec(memory_space=pltpu.SMEM), vmem]
        + [vmem] * len(extra)
        + [any_spec()] * len(after),
        out_specs=[vmem, vmem],
        out_shape=[
            jax.ShapeDtypeStruct((2, tokens, width), bf16),
            jax.ShapeDtypeStruct((chips - 1, 2, tokens, width), bf16),
        ],
        compiler_params=params(),
        cost_estimate=short,
        name="cut_features",
    )(chip_core, v, *extra, *after)


def expert_and_attention(
    place,
    hidden_in,
    moe_probe,
    router_weight,
    routes,
    gate_weight,
    up_weight,
    down_weight,
    coeff,
    queries,
    key_rows,
    value_rows,
    decay_rate,
    norm_gain,
    attn_probe,
):
    rollouts, positions, model_width = hidden_in.shape
    chips, experts, slices = place.chips, place.experts, place.slices
    tokens = rollouts * positions
    width = gate_weight.shape[1]
    own_mats = (gate_weight[0], up_weight[0], down_weight[0])

    hidden = hidden_in.reshape(tokens, model_width)
    local_coeff = lax.dynamic_slice_in_dim(
        coeff, lax.axis_index("expert") * positions, positions, 1
    )
    chip_here = place.chip.reshape(1).astype(jnp.int32)
    chip_core = jnp.stack([place.chip, place.core]).astype(jnp.int32)
    last = []

    def ordered(kernel, *args, needs=()):
        result = kernel(*args, (*last, *needs))
        last[:] = [result[0] if isinstance(result, (list, tuple)) else result]
        return result

    def across(v, scale):
        keep, send = ordered(cut_features, v, scale, chip_core, chips)
        return [keep] + [place.turn_chip(send[p - 1], p) for p in range(1, chips)]

    hidden_groups = across(hidden, None)
    grad_groups = across(
        moe_probe.reshape(tokens, model_width), local_coeff.reshape(tokens, 1)
    )

    def halves_of(v, p):
        chip = (place.chip + p) % chips
        return jnp.stack(
            [
                lax.dynamic_slice_in_dim(v, (2 * chip + core) * width, width, 1)
                for core in (place.core, 1 - place.core)
            ]
        )

    logits = jnp.dot(hidden, router_weight, preferred_element_type=f32)
    flat_routes = routes.reshape(tokens, -1)
    onehot = (flat_routes[:, :, None] == jnp.arange(experts, dtype=jnp.int32)).astype(f32)
    chosen = jnp.sum(onehot * logits[:, None, :], axis=-1)
    exponent = jnp.exp(chosen)
    gate = exponent / jnp.sum(exponent, axis=-1, keepdims=True)
    facts = jnp.concatenate(
        [onehot.sum(axis=1), jnp.sum(onehot * gate[:, :, None], axis=1)], axis=1
    )
    all_facts = [facts] + [place.turn_chip(facts, p) for p in range(1, chips)]

    pairs = [(m, place.swap_core(m)) for m in own_mats[:2]]

    fact_stack = jnp.stack(all_facts)
    member, gates = fact_stack[:, :, :experts], fact_stack[:, :, experts:]
    whose = (place.chip - jnp.arange(chips)) % chips
    earlier = (whose[None, :] < whose[:, None]).astype(f32)
    offset = jnp.sum(earlier[:, :, None] * member.sum(axis=1)[None], axis=1)
    step = jnp.arange(tokens)
    below = (step[:, None] > step[None, :]).astype(f32)
    rank = jnp.einsum("ts,gse->gte", below, member) + offset[:, None, :]
    rank = jnp.where(member > 0, rank, -1.0).astype(jnp.int32)
    rank = rank.reshape(chips * tokens, experts)
    gates = gates.reshape(chips * tokens, experts)
    rank_lanes = rank.T

    most = chips * rollouts * (positions // 2 + 1)
    small = max(16, most // 2 // 16 * 16)
    chunks = [(0, small), (small, most - small)]
    def dispatch(groups, first, count, needs=()):
        padded = -(-count // 8) * 8
        return ordered(pick_rows, groups, rank_lanes, first, count, padded, needs=needs)

    def behind(v, *others):
        return lax.optimization_barrier((v, *others))[0] if others else v

    def relay(mine):
        return [place.turn_slice(mine, k) for k in range(1, slices)]

    def partial(jobs, count, needs=()):
        scales = jnp.asarray([scale for _, mats, scale in jobs for _ in mats], f32)
        scales = scales.reshape(-1, 1, 1)
        ready = [([behind(v, *needs) for v in arrays], mats) for arrays, mats, _ in jobs]
        keep, send = ordered(project, ready, count, chip_here, chips)
        send = (send * scales).astype(jnp.float16)
        arrived = [place.turn_chip(send[p - 1], p) for p in range(1, chips)]
        return keep, arrived, scales

    def settle(part):
        keep, arrived, scale = part
        return keep + sum(v.astype(f32) for v in arrived) / scale

    def ring(v):
        found = [v] + [None] * (chips - 1)
        for p in range(1, chips):
            found[chips - p] = place.turn_chip(v, p)
        return found

    def middle(*some):
        pre_gate, pre_up, unit_grad = jnp.concatenate([settle(v) for v in some])
        sigmoid_gate = jax.nn.sigmoid(pre_gate)
        activated = pre_gate * sigmoid_gate
        units = activated * pre_up
        score = jnp.sum(units * unit_grad, axis=-1).astype(bf16)
        slope = pre_up * sigmoid_gate * (1.0 + pre_gate * (1.0 - sigmoid_gate))
        which = jnp.arange(2).reshape(2, 1, 1)
        both = (unit_grad * jnp.where(which == 0, slope, activated)).astype(bf16)
        return ring(both), score

    def back(groups, halves, count, needs=()):
        mats = [(pairs[0][h], pairs[1][h]) for h in halves]
        return ordered(project_back, groups, mats, chip_here, count, needs=needs)

    def to_slices(dx):
        return [
            place.turn_slice(dx[(k - 1) * experts : k * experts], -k) for k in range(1, slices)
        ]

    (first_a, count_a), (first_b, count_b) = chunks

    block = queries.shape[1]
    def held(part, kernel_result):
        keep, arrived, scale = part
        return keep, [behind(v, kernel_result) for v in arrived], scale

    summary = ordered(key_value_state, key_rows, value_rows, decay_rate)
    early = outside_states(place, summary, 1)
    picked_hidden_a = dispatch(hidden_groups, first_a, count_a)
    picked_grads_a = dispatch(grad_groups, first_a, count_a)
    picked_hidden_b = dispatch(hidden_groups, first_b, count_b)
    hidden_a = place.between_experts(behind(picked_hidden_a, picked_grads_a))
    picked_grads_b = dispatch(grad_groups, first_b, count_b, [pairs[0][1], pairs[1][1]])
    far_hidden_a = relay(hidden_a)
    pairs.append((own_mats[2], place.swap_core(behind(own_mats[2], picked_grads_b))))
    inner_own_a = partial([([hidden_a], pairs[:2], in_scale)], count_a, early)
    early = [behind(v, inner_own_a[0]) for v in early]
    state_before = carried(place, summary, decay_rate, block, 1, early)
    grad_queries, local_k, local_v, summary = ordered(
        local_grads,
        queries,
        key_rows,
        value_rows,
        attn_probe,
        norm_gain.reshape(1, -1),
        coeff.T,
        decay_rate,
        state_before,
    )
    grads_a = place.between_experts(behind(picked_grads_a, hidden_a))
    far_grads_a = relay(behind(grads_a, summary))
    outer_own_a = partial([([grads_a], pairs[2:], out_scale)], count_a)
    hidden_b = place.between_experts(behind(picked_hidden_b, grads_a, summary))
    own_a, score_own_a = middle(inner_own_a, outer_own_a)
    whole_far_a = partial(
        [(far_hidden_a, pairs[:2], in_scale), (far_grads_a, pairs[2:], out_scale)],
        count_a,
        own_a[:1],
    )
    far_hidden_b = relay(behind(hidden_b, own_a[0]))
    grads_b = place.between_experts(behind(picked_grads_b, hidden_b, own_a[0]))
    inner_own_b = partial([([hidden_b], pairs[:2], in_scale)], count_b, own_a[1:])
    far_grads_b = relay(grads_b)
    far_a, score_far_a = middle(whole_far_a)
    state_after = carried(place, behind(summary, whole_far_a[0]), decay_rate, block, -1)
    inner_far_b = partial([(far_hidden_b, pairs[:2], in_scale)], count_b, far_a[:1])
    outer_own_b = partial([([grads_b], pairs[2:], out_scale)], count_b)
    dx_own_a, dx_far_a = back([own_a, far_a], (0, 1), count_a)
    outer_far_b = partial([(far_grads_b, pairs[2:], out_scale)], count_b, inner_own_b[1])
    grad_keys, grad_values = ordered(
        later_grads, key_rows, value_rows, local_k, local_v, decay_rate, state_after
    )
    far_b, score_far_b = middle(inner_far_b, outer_far_b)
    own_b, score_own_b = middle(held(inner_own_b, far_b[0]), held(outer_own_b, far_b[0]))
    from_far_a = to_slices(dx_far_a)
    total_a = dx_own_a.astype(f32) + sum(
        behind(v, own_b[0], grad_keys).astype(f32) for v in from_far_a
    )
    total_a = total_a.astype(bf16)
    home_a = place.between_experts(total_a)
    from_far_b = [
        to_slices(back([far_b], (h,), count_b, [total_a])[0]) for h in range(2)
    ]
    (dx_own_b,) = back([own_b], (0, 1), count_b)
    total_b = dx_own_b.astype(f32) + sum(
        jnp.concatenate(halves, axis=1).astype(f32) for halves in zip(*from_far_b)
    )
    total_b = behind(total_b.astype(bf16), home_a)
    home_b = place.between_experts(total_b)

    kinds = [score_own_a, score_far_a, score_own_b, score_far_b]
    sizes = [v.shape[0] for v in kinds]
    every = jnp.stack(ring(behind(jnp.concatenate(kinds), *far_b)))
    every = jnp.take(every, (jnp.arange(chips) - place.chip) % chips, axis=0)
    split, at = [], 0
    for size in sizes:
        split.append(every[:, at : at + size].reshape(chips * size))
        at += size
    near = [
        v.reshape(experts, count) for v, count in ((split[0], count_a), (split[2], count_b))
    ]
    beyond = [
        v.reshape(slices - 1, experts, count)
        for v, count in ((split[1], count_a), (split[3], count_b))
    ]
    score_rows = jnp.concatenate(near, axis=1).astype(f32)
    beyond = jnp.concatenate(beyond, axis=2)
    for k in range(1, slices):
        score_rows = score_rows + place.turn_slice(beyond[k - 1], -k).astype(f32)
    turned = [score_rows] + [place.turn_expert(score_rows, d) for d in range(1, experts)]
    turned = lax.dynamic_index_in_dim(jnp.stack(turned), place.expert, 1, keepdims=False)
    source = (place.expert - jnp.arange(experts)) % experts
    score_home = jnp.take(turned, source, axis=0)

    router_rows = halves_of(router_weight.T.astype(f32), 0)
    result = jnp.zeros((tokens, model_width), bf16)
    for h in range(2):
        groups = combine(
            [(home_a, h), (home_b, h)],
            score_home,
            rank,
            gates,
            router_rows[h],
            [first_a, first_b],
            chips,
        )
        core = place.core if h == 0 else 1 - place.core
        for g in range(chips):
            part = groups[g] if g == 0 else place.turn_chip(groups[g], -g)
            chip = (place.chip + g) % chips
            result = lax.dynamic_update_slice_in_dim(result, part, (2 * chip + core) * width, 1)
    grad_hidden = result.reshape(rollouts, positions, model_width)
    return grad_queries, grad_keys, grad_values, grad_hidden


def on_device(
    queries,
    key_rows,
    value_rows,
    decay_rate,
    norm_gain,
    attn_probe,
    hidden_in,
    moe_probe,
    router_weight,
    routes,
    gate_weight,
    up_weight,
    down_weight,
    rollout_logprob,
    trainer_logprob,
    advantage,
    clip_low,
    clip_high,
):
    place = Layout(router_weight.shape[1])
    importance = jnp.exp(trainer_logprob - rollout_logprob)
    clipped = jnp.minimum(jnp.maximum(importance, clip_low[0]), clip_high[0])
    coeff = -(clipped * advantage) / queries.shape[0]
    objective = coeff * trainer_logprob
    grads = expert_and_attention(
        place,
        hidden_in,
        moe_probe,
        router_weight,
        routes,
        gate_weight,
        up_weight,
        down_weight,
        coeff,
        queries,
        key_rows,
        value_rows,
        decay_rate,
        norm_gain,
        attn_probe,
    )
    return (objective, *grads)


def solution(mesh):
    in_specs = (
        P(None, "seq", "expert"),
        P(None, "seq", "expert"),
        P(None, "seq", "expert"),
        P("expert"),
        P("expert"),
        P(None, "seq", "expert"),
        P(None, ("seq", "expert"), None),
        P(None, ("seq", "expert"), None),
        P(),
        P(None, ("seq", "expert"), None),
        P("expert", "seq", None),
        P("expert", "seq", None),
        P("expert", "seq", None),
        P(None, "seq"),
        P(None, "seq"),
        P(None, "seq"),
        P(),
        P(),
    )
    out_specs = (
        P(None, "seq"),
        P(None, "seq", "expert"),
        P(None, "seq", "expert"),
        P(None, "seq", "expert"),
        P(None, ("seq", "expert"), None),
    )
    return jax.shard_map(
        on_device, mesh=mesh, in_specs=in_specs, out_specs=out_specs, check_vma=False
    )
```
